32 devices in a mesh: gx: 4 (over y, x), gy: 4 (over z), gz: 2 (over core).
Axes of the slice: x: 2, y: 2, z: 4, core: 2. Of those that a mesh axis runs over, the one named last changes fastest.
Arguments:
- initial: float32 [32, 32, 256], P('gx', 'gy', 'gz'), may hold values from -6 to 6
- source: float32 [32, 32, 256], P('gx', 'gy', 'gz'), may hold values from -6 to 6
- metric: float32 [3, 32, 32, 256], P(None, 'gx', 'gy', 'gz'), may hold values from 0.005 to 0.05
- eigenvectors: float32 [3, 10, 10, 4, 4, 32], P(None, None, None, 'gx', 'gy', 'gz'), may hold values from -2 to 2
- eigenvalues: float32 [3, 10, 4, 4, 32], P(None, None, 'gx', 'gy', 'gz'), may hold values from 1 to 8
Outputs:
- solution: float32 [32, 32, 256], P('gx', 'gy', 'gz')
The draws below stay inside these ranges and needn't reach their ends.
All inputs are finite; a program needn't handle non-finite values.
Results may differ from the reference program's by a relative error of at most 0.0001.
Values sent between devices are 32-bit elements; how exact they have to be, the bound alone decides.
No kernel may reach another device: no remote copies, remote signals or barrier semaphores. Data moves between devices by JAX's collectives and lax.ppermute only.
A program may use at most 64 MiB of HBM per device.

```python
import math
import jax
import jax.numpy as jnp
import numpy as np
from jax import lax

STEPS = 1
MX = 4
MY = 4
MZ = 32
NX = 32
NY = 32
NZ = 256


def levels(stream_key, dims, pieces, smallest, high):
    loudness, own = 1.0, jax.random.fold_in(stream_key, 6)
    for axis_at, parts in pieces:
        steps = jnp.exp(jax.random.uniform(jax.random.fold_in(own, axis_at), (parts,), jnp.float32, smallest / len(pieces), high / len(pieces)))
        loudness = loudness * jnp.repeat(steps, dims[axis_at] // parts).reshape([-1 if axis == axis_at else 1 for axis in range(len(dims))])
    return loudness


def scatter_about(rng, shape, width, bound, shards=(), held_as=jnp.bfloat16):
    values = jax.random.normal(rng, shape, jnp.float32) * width
    if len(shards) > 0:
        values = levels(rng, shape, shards, -0.22, 0.18) * values
    return jnp.clip(values, min=-bound, max=bound).astype(held_as)


def setup_inputs(seed: int = 0) -> dict:
    seeds = jax.random.split(jax.random.key(seed), 6)
    return {
        "initial": scatter_about(seeds[0], (NX, NY, NZ), 1.0, 6.0, ((0, 4), (1, 4), (2, 2)), jnp.float32),
        "source": scatter_about(seeds[1], (NX, NY, NZ), 1.0, 6.0, ((0, 4), (1, 4), (2, 2)), jnp.float32),
        "metric": jnp.clip(jnp.exp(math.log(0.05) - 2.3025851 * jax.random.uniform(seeds[2], (3, NX, NY, NZ), jnp.float32) ** levels(seeds[2], (3, NX, NY, NZ), ((1, 4), (2, 4), (3, 2)), -0.2, 0.2)), 0.005, 0.05),
        "eigenvectors": scatter_about(seeds[3], (3, 10, 10, MX, MY, MZ), 10 ** -0.5, 2.0, ((3, 4), (4, 4), (5, 2)), jnp.float32),
        "eigenvalues": jnp.clip(jnp.exp(math.log(8.0) - 2.0794415 * jax.random.uniform(seeds[4], (3, 10, MX, MY, MZ), jnp.float32) ** levels(seeds[4], (3, 10, MX, MY, MZ), ((2, 4), (3, 4), (4, 2)), -0.2, 0.2)), 1.0, 8.0),
    }


gll_points = np.array([-1.0, -0.8717401485096066, -0.5917001814331423, -0.2092992179024789, 0.2092992179024789, 0.5917001814331423, 0.8717401485096066, 1.0])


def derivative_table():
    number = gll_points.shape[0]
    products = np.array([np.prod([gll_points[row_index] - gll_points[other] for other in range(number) if other != row_index]) for row_index in range(number)])
    matrix_out = np.zeros((number, number))
    for row_index in range(number):
        for col_index in range(number):
            if row_index != col_index:
                matrix_out[row_index, col_index] = products[row_index] / products[col_index] / (gll_points[row_index] - gll_points[col_index])
        matrix_out[row_index, row_index] = -np.sum(matrix_out[row_index])
    return matrix_out


def apply_along(values, matrix, direction):
    block_size = matrix.shape[1]
    old_shape = values.shape
    pieces_shape = old_shape[:direction] + (old_shape[direction] // block_size, block_size) + old_shape[direction + 1:]
    result = jnp.tensordot(values.reshape(pieces_shape), matrix, axes=((direction + 1,), (1,)), precision=lax.Precision.HIGHEST)
    result = jnp.moveaxis(result, -1, direction + 1)
    return result.reshape(old_shape[:direction] + (old_shape[direction] // block_size * matrix.shape[0],) + old_shape[direction + 1:])


def apply_operator(values, metric):
    deriv_table = jnp.asarray(derivative_table(), jnp.float32)
    summed = jnp.zeros_like(values)
    for direction in range(3):
        gradient = apply_along(values, deriv_table, direction)
        summed = summed + apply_along(metric[direction] * gradient, deriv_table.T, direction)
    return summed


def assemble(padded, offset):
    result = padded
    for direction in range(3):
        length = result.shape[direction]
        view_shape = [1, 1, 1]
        view_shape[direction] = length
        node_index = ((jnp.arange(length) - offset) % 8).reshape(view_shape)
        edge_zero = jnp.zeros_like(lax.slice_in_dim(result, 0, 1, axis=direction))
        upward = jnp.concatenate([lax.slice_in_dim(result, 1, length, axis=direction), edge_zero], axis=direction)
        downward = jnp.concatenate([edge_zero, lax.slice_in_dim(result, 0, length - 1, axis=direction)], axis=direction)
        result = result + jnp.where(node_index == 7, upward, 0.0) + jnp.where(node_index == 0, downward, 0.0)
    return result


def extend_axis(padded, direction):
    shifted = jnp.moveaxis(padded, direction, 0)
    blocks = (shifted.shape[0] - 4) // 8
    trailing = shifted.shape[1:]
    middle = shifted[2:-2].reshape((blocks, 8) + trailing)
    lowest = shifted[0:8 * blocks:8][:, None]
    beyond = shifted[11::8][:, None]
    joined = jnp.concatenate([lowest, middle, beyond], axis=1).reshape((blocks * 10,) + trailing)
    return jnp.moveaxis(joined, 0, direction)


def widen(padded):
    return extend_axis(extend_axis(extend_axis(padded, 0), 1), 2)


def fast_solve(extended, eigenvectors, eigenvalues):
    count_x, count_y, count_z = eigenvectors.shape[3:]
    precise = lax.Precision.HIGHEST
    spectral = extended.reshape(count_x, 10, count_y, 10, count_z, 10)
    spectral = jnp.einsum('apxyz,xaybzc->xpybzc', eigenvectors[0], spectral, precision=precise)
    spectral = jnp.einsum('bqxyz,xpybzc->xpyqzc', eigenvectors[1], spectral, precision=precise)
    spectral = jnp.einsum('csxyz,xpyqzc->xpyqzs', eigenvectors[2], spectral, precision=precise)
    rate_x = jnp.transpose(eigenvalues[0], (1, 0, 2, 3))[:, :, :, None, :, None]
    rate_y = jnp.transpose(eigenvalues[1], (1, 2, 0, 3))[:, None, :, :, :, None]
    rate_z = jnp.transpose(eigenvalues[2], (1, 2, 3, 0))[:, None, :, None, :, :]
    spectral = spectral / (rate_x + rate_y + rate_z)
    spectral = jnp.einsum('csxyz,xpyqzs->xpyqzc', eigenvectors[2], spectral, precision=precise)
    spectral = jnp.einsum('bqxyz,xpyqzc->xpybzc', eigenvectors[1], spectral, precision=precise)
    spectral = jnp.einsum('apxyz,xpybzc->xaybzc', eigenvectors[0], spectral, precision=precise)
    return spectral.reshape(count_x * 10, count_y * 10, count_z * 10)


def return_axis(padded, direction):
    shifted = jnp.moveaxis(padded, direction, 0)
    blocks = (shifted.shape[0] - 4) // 10
    trailing = shifted.shape[1:]
    owned = shifted[2:-2].reshape((blocks, 10) + trailing)[:, 1:9]
    before = shifted[0:10 * blocks].reshape((blocks, 10) + trailing)[:, 0:2]
    following = shifted[4:].reshape((blocks, 10) + trailing)[:, 8:10]
    middle = jnp.zeros((blocks, 4) + trailing, shifted.dtype)
    summed = owned + jnp.concatenate([before, middle, following], axis=1)
    return jnp.moveaxis(summed.reshape((blocks * 8,) + trailing), 0, direction)


def reference(initial, source, metric, eigenvectors, eigenvalues):
    solution = initial
    for smooth_step in range(STEPS):
        local_res = source - apply_operator(solution, metric)
        widened = assemble(jnp.pad(local_res, 2), 2)
        extended = widen(widened)
        corrected = fast_solve(extended, eigenvectors, eigenvalues)
        padded = jnp.pad(corrected, 2)
        correction = return_axis(return_axis(return_axis(padded, 0), 1), 2)
        solution = solution + correction
    return solution
```

```python
import functools

import jax
import jax.numpy as jnp
import ml_dtypes
import numpy as np
from jax import lax
from jax.experimental import pallas as pl
from jax.experimental.pallas import tpu as pltpu
from jax.sharding import PartitionSpec as P

gll_points = np.array(
    [
        -1.0,
        -0.8717401485096066,
        -0.5917001814331423,
        -0.2092992179024789,
        0.2092992179024789,
        0.5917001814331423,
        0.8717401485096066,
        1.0,
    ]
)


def extended_2(value, sides, width):
    for axis, dim in sides:
        size, length = (lax.axis_size(axis), value.shape[dim])
        up = [(i, (i + 1) % size) for i in range(size - 1)]
        down = [(j, i) for i, j in up]
        last = lax.slice_in_dim(value, length - width, length, axis=dim)
        first = lax.slice_in_dim(value, 0, width, axis=dim)
        before = lax.ppermute(last, axis, up)
        after = lax.ppermute(first, axis, down)
        value = jnp.concatenate([before, value, after], axis=dim)
    return value


def derivative_table():
    number = gll_points.shape[0]
    products = np.array(
        [
            np.prod(
                [
                    gll_points[row_index] - gll_points[other]
                    for other in range(number)
                    if other != row_index
                ]
            )
            for row_index in range(number)
        ]
    )
    matrix_out = np.zeros((number, number))
    for row_index in range(number):
        for col_index in range(number):
            if row_index != col_index:
                matrix_out[row_index, col_index] = (
                    products[row_index]
                    / products[col_index]
                    / (gll_points[row_index] - gll_points[col_index])
                )
        matrix_out[row_index, row_index] = -np.sum(matrix_out[row_index])
    return matrix_out


def apply_along(values, matrix, direction):
    block_size = matrix.shape[1]
    old_shape = values.shape
    pieces_shape = (
        old_shape[:direction]
        + (old_shape[direction] // block_size, block_size)
        + old_shape[direction + 1 :]
    )
    result = jnp.tensordot(
        values.reshape(pieces_shape),
        matrix,
        axes=((direction + 1,), (1,)),
        precision=lax.Precision.HIGHEST,
    )
    result = jnp.moveaxis(result, -1, direction + 1)
    return result.reshape(
        old_shape[:direction]
        + (old_shape[direction] // block_size * matrix.shape[0],)
        + old_shape[direction + 1 :]
    )


def apply_operator(values, metric):
    deriv_table = jnp.asarray(derivative_table(), jnp.float32)
    summed = jnp.zeros_like(values)
    for direction in range(3):
        gradient = apply_along(values, deriv_table, direction)
        summed = summed + apply_along(metric[direction] * gradient, deriv_table.T, direction)
    return summed


def assemble(padded, offset):
    result = padded
    for direction in range(3):
        length = result.shape[direction]
        view_shape = [1, 1, 1]
        view_shape[direction] = length
        node_index = ((jnp.arange(length) - offset) % 8).reshape(view_shape)
        edge_zero = jnp.zeros_like(lax.slice_in_dim(result, 0, 1, axis=direction))
        upward = jnp.concatenate(
            [lax.slice_in_dim(result, 1, length, axis=direction), edge_zero], axis=direction
        )
        downward = jnp.concatenate(
            [edge_zero, lax.slice_in_dim(result, 0, length - 1, axis=direction)], axis=direction
        )
        result = (
            result
            + jnp.where(node_index == 7, upward, 0.0)
            + jnp.where(node_index == 0, downward, 0.0)
        )
    return result


def extend_axis(padded, direction):
    shifted = jnp.moveaxis(padded, direction, 0)
    blocks = (shifted.shape[0] - 4) // 8
    trailing = shifted.shape[1:]
    middle = shifted[2:-2].reshape((blocks, 8) + trailing)
    lowest = shifted[0 : 8 * blocks : 8][:, None]
    beyond = shifted[11::8][:, None]
    joined = jnp.concatenate([lowest, middle, beyond], axis=1).reshape((blocks * 10,) + trailing)
    return jnp.moveaxis(joined, 0, direction)


def widen(padded):
    return extend_axis(extend_axis(extend_axis(padded, 0), 1), 2)


def fast_solve(extended, eigenvectors, eigenvalues):
    count_x, count_y, count_z = eigenvectors.shape[3:]
    precise = lax.Precision.HIGHEST
    spectral = extended.reshape(count_x, 10, count_y, 10, count_z, 10)
    spectral = jnp.einsum("apxyz,xaybzc->xpybzc", eigenvectors[0], spectral, precision=precise)
    spectral = jnp.einsum("bqxyz,xpybzc->xpyqzc", eigenvectors[1], spectral, precision=precise)
    spectral = jnp.einsum("csxyz,xpyqzc->xpyqzs", eigenvectors[2], spectral, precision=precise)
    rate_x = jnp.transpose(eigenvalues[0], (1, 0, 2, 3))[:, :, :, None, :, None]
    rate_y = jnp.transpose(eigenvalues[1], (1, 2, 0, 3))[:, None, :, :, :, None]
    rate_z = jnp.transpose(eigenvalues[2], (1, 2, 3, 0))[:, None, :, None, :, :]
    spectral = spectral / (rate_x + rate_y + rate_z)
    spectral = jnp.einsum("csxyz,xpyqzs->xpyqzc", eigenvectors[2], spectral, precision=precise)
    spectral = jnp.einsum("bqxyz,xpyqzc->xpybzc", eigenvectors[1], spectral, precision=precise)
    spectral = jnp.einsum("apxyz,xpybzc->xaybzc", eigenvectors[0], spectral, precision=precise)
    return spectral.reshape(count_x * 10, count_y * 10, count_z * 10)


def return_axis(padded, direction):
    shifted = jnp.moveaxis(padded, direction, 0)
    blocks = (shifted.shape[0] - 4) // 10
    trailing = shifted.shape[1:]
    owned = shifted[2:-2].reshape((blocks, 10) + trailing)[:, 1:9]
    before = shifted[0 : 10 * blocks].reshape((blocks, 10) + trailing)[:, 0:2]
    following = shifted[4:].reshape((blocks, 10) + trailing)[:, 8:10]
    middle = jnp.zeros((blocks, 4) + trailing, shifted.dtype)
    summed = owned + jnp.concatenate([before, middle, following], axis=1)
    return jnp.moveaxis(summed.reshape((blocks * 8,) + trailing), 0, direction)


def general_body(initial, source, metric, eigenvectors, eigenvalues):
    solution = initial
    local_res = source - apply_operator(solution, metric)
    deeper = extended_2(local_res, (("gx", 0), ("gy", 1), ("gz", 2)), 2)
    widened = assemble(deeper, 2)
    extended = widen(widened)
    corrected = fast_solve(extended, eigenvectors, eigenvalues)
    padded = extended_2(corrected, (("gx", 0), ("gy", 1), ("gz", 2)), 2)
    correction = return_axis(return_axis(return_axis(padded, 0), 1), 2)
    solution = solution + correction
    return solution


AXES = ("gx", "gy", "gz")
VMEM = pl.BlockSpec(memory_space=pltpu.VMEM)
VMEM_LIMIT = 16 * 2**20
f32 = jnp.float32
bf16 = jnp.bfloat16


def call(kernel, outs, args, flops=0, scratch=()):
    moved = sum(int(np.prod(a.shape)) * a.dtype.itemsize for a in (*args, *outs))
    return pl.pallas_call(
        kernel,
        out_shape=outs,
        in_specs=[VMEM] * len(args),
        out_specs=[VMEM] * len(outs),
        scratch_shapes=scratch,
        compiler_params=pltpu.CompilerParams(vmem_limit_bytes=VMEM_LIMIT),
        cost_estimate=pl.CostEstimate(flops=flops, bytes_accessed=moved, transcendentals=0),
    )(*args)


def shaped(shape, dtype=f32):
    return jax.ShapeDtypeStruct(shape, dtype)


def split2(value):
    high = value.astype(bf16)
    return high, (value - high.astype(f32)).astype(bf16)


def split3(value):
    high = value.astype(bf16)
    rest = value - high.astype(f32)
    middle = rest.astype(bf16)
    return high, middle, (rest - middle.astype(f32)).astype(bf16)


def table_split2(table):
    table = np.asarray(table, np.float32)
    high = table.astype(ml_dtypes.bfloat16)
    return high, (table - high.astype(np.float32)).astype(ml_dtypes.bfloat16)


def dot(left, right, transposed=False):
    dims = (((1,), (1 if transposed else 0,)), ((), ()))
    return lax.dot_general(left, right, dims, preferred_element_type=f32)


def operator_tables(count_y, length_z):
    table = np.asarray(derivative_table(), np.float32)
    nodes = table.shape[0]
    along_y = np.kron(np.eye(nodes), table)
    along_z = np.kron(np.eye(length_z // nodes), table.T)
    tables = []
    for matrix in (along_y, along_y.T):
        high, low = table_split2(matrix)
        tables.append(np.concatenate([high, high, low], axis=1))
    for matrix in (along_z, along_z.T):
        high, low = table_split2(matrix)
        tables.append(np.concatenate([high, high, low], axis=0))
    return [jnp.asarray(t) for t in tables]


def residual_kernel(u_ref, source_ref, metric_ref, ay, ayt, bz, bzt, out_ref):
    nodes, rows, width = u_ref.shape
    table = np.asarray(derivative_table(), np.float32)

    def stacked(value, axis):
        high, low = split2(value)
        return jnp.concatenate([high, low, high], axis=axis)

    flat = u_ref[...].reshape(nodes * rows, width)
    along_y = dot(ay[...], stacked(flat, 0)) * metric_ref[1].reshape(flat.shape)
    along_z = dot(stacked(flat, 1), bz[...]) * metric_ref[2].reshape(flat.shape)
    total = dot(ayt[...], stacked(along_y, 0)) + dot(stacked(along_z, 1), bzt[...])
    total = total.reshape(nodes, rows, width)
    layers = [u_ref[j] for j in range(nodes)]
    fluxes = []
    for i in range(nodes):
        gradient = sum(float(table[i, j]) * layers[j] for j in range(nodes))
        fluxes.append(metric_ref[0, i] * gradient)
    for j in range(nodes):
        applied = sum(float(table[i, j]) * fluxes[i] for i in range(nodes))
        out_ref[j] = source_ref[j] - (applied + total[j])


def spread_tables(blocks, ext):
    lanes = np.arange(blocks * ext)
    repeat = (lanes[None, :] // ext == np.arange(blocks)[:, None]).astype(np.float32)
    repeat = np.concatenate([repeat] * 3, axis=0)
    rows = np.arange(ext * ext)
    mask = (rows[:, None] % ext == lanes[None, :] % ext).astype(np.float32)
    gather = (rows[None, :] // ext == np.arange(ext)[:, None]).astype(np.float32)
    gather = np.concatenate([gather] * 3, axis=1)
    padded = 2 * (ext - 2)
    order = list(range(1, ext - 1)) + [0, ext - 1]
    forward = np.zeros((ext, padded, ext * ext), np.float32)
    backward = np.zeros((ext, padded, ext * ext), np.float32)
    for first in range(ext):
        for second in range(ext):
            forward[first, second, first * ext + second] = 1
            backward[first, second, order[second] * ext + first] = 1
    both = np.concatenate([forward.reshape(-1, ext * ext), backward.reshape(-1, ext * ext)])
    both = np.concatenate([both] * 3, axis=1)
    return [
        jnp.asarray(repeat, bf16),
        jnp.asarray(mask),
        jnp.asarray(gather, bf16),
        jnp.asarray(both, bf16),
    ]


def coefficients_kernel(
    vec_ref, val_ref, repeat, mask, gather, both, after_ref, cx_ref, cy_ref, rate_ref, mz_ref
):
    ext = rate_ref.shape[0]
    square = ext * ext
    padded, lanes = rate_ref.shape[1:]
    blocks = lanes // ext
    nodes = ext - 2
    core = lax.axis_index("gz")

    def spread(ref, first, count):
        value = ref[first : first + count].reshape(count, blocks)
        return dot(jnp.concatenate(split3(value), axis=1), repeat[...])

    cx_ref[...] = spread(vec_ref, 0, square)
    along_y = spread(vec_ref, square, square)
    cy_ref[...] = dot(both[...], jnp.concatenate(split3(along_y), axis=0)).reshape(cy_ref.shape)
    along_z = spread(vec_ref, 2 * square, square) * mask[...]
    along_z = dot(gather[...], jnp.concatenate(split3(along_z), axis=0))

    rate_x = spread(val_ref, 0, ext)
    rate_y = spread(val_ref, ext, ext)
    rate_z = jnp.sum(spread(val_ref, 2 * ext, ext) * mask[0:ext, :], axis=0, keepdims=True)
    rate_y = jnp.concatenate([rate_y, jnp.ones((padded - ext, lanes), f32)], axis=0)
    for p in range(ext):
        rate_ref[p] = 1.0 / (rate_x[p : p + 1] + rate_y + rate_z)

    zeros = jnp.zeros((nodes - 2, lanes), f32)
    own = along_z[1 : nodes + 1]
    below = jnp.concatenate([zeros, along_z[0:2]], axis=0)
    above = jnp.concatenate([along_z[nodes : nodes + 2], zeros], axis=0)
    element = lax.broadcasted_iota(jnp.int32, (nodes, lanes), 1) // ext
    zero = jnp.zeros_like(own)
    for half in range(2):
        shift = 0 if half == 0 else jnp.where(core == 0, blocks, -blocks)
        for first in range(0, blocks, 2):
            pair = []
            for block in (first + shift, first + 1 + shift):
                value = jnp.where(element == block, own, zero)
                value = value + jnp.where(element == block + 1, below, zero)
                pair.append(value + jnp.where(element == block - 1, above, zero))
            high, low = split2(jnp.concatenate(pair, axis=0))
            start = (half * blocks + first) * nodes
            mz_ref[0, start : start + 2 * nodes, :] = high
            mz_ref[1, start : start + 2 * nodes, :] = low


def both_sides(core, direct, passed):
    low = [jnp.where(core == 0, direct[h], passed[1 - h]) for h in range(2)]
    high = [jnp.where(core == 0, passed[1 - h], direct[h]) for h in range(2)]
    return low, high


def edges(axis):
    place, size = lax.axis_index(axis), lax.axis_size(axis)
    return place > 0, place < size - 1


def layers_kernel(own_ref, partner_ref, out_ref):
    start = lax.axis_index("gz") * (own_ref.shape[0] - 2)
    for half, ref in enumerate((partner_ref, own_ref)):
        for layer in range(2):
            out_ref[half, layer] = ref[start + layer]


def x_layers(core, own_ref, partner_ref, direct_ref, passed_ref):
    has_low, has_high = edges("gx")
    length = own_ref.shape[0]

    def at(layer):
        if 2 <= layer < length + 2:
            return own_ref[layer - 2], partner_ref[layer - 2]
        slot = layer if layer < 2 else layer - length - 2
        direct = [direct_ref[h, slot] for h in range(2)]
        passed = [passed_ref[h, slot] for h in range(2)]
        low, high = both_sides(core, direct, passed)
        side, valid = (low, has_low) if layer < 2 else (high, has_high)
        return [jnp.where(valid, v, jnp.zeros_like(v)) for v in side]

    return at


def rows_kernel(own_ref, partner_ref, direct_ref, passed_ref, out_ref):
    core = lax.axis_index("gz")
    length, rows, _ = own_ref.shape
    at = x_layers(core, own_ref, partner_ref, direct_ref, passed_ref)
    for layer in range(length + 4):
        own, partner = at(layer)
        for half, value in enumerate((partner, own)):
            row = layer * 4 + half * 2
            out_ref[row // 8, row % 8 : row % 8 + 2, :] = jnp.where(
                core == 0, value[0:2], value[rows - 2 : rows]
            )


def solve_kernel(
    own_ref, partner_ref, xd_ref, xp_ref, yd_ref, yp_ref, cx, cy, rate, mz, out_ref, grid, spectral
):
    core = lax.axis_index("gz")
    length, rows, width = own_ref.shape
    ext, padded, lanes = rate.shape
    has_low, has_high = edges("gy")
    at = x_layers(core, own_ref, partner_ref, xd_ref, xp_ref)
    nothing = jnp.zeros((padded - rows - 4, width), f32)
    for layer in range(length + 4):
        place, row = divmod(layer * 4, 8)
        direct = [yd_ref[place, row + 2 * h : row + 2 * h + 2, :] for h in range(2)]
        passed = [yp_ref[place, row + 2 * h : row + 2 * h + 2, :] for h in range(2)]
        low, high = both_sides(core, direct, passed)
        for half, value in enumerate(at(layer)):
            before = jnp.where(has_low, low[half], jnp.zeros_like(low[half]))
            after = jnp.where(has_high, high[half], jnp.zeros_like(high[half]))
            at_lanes = slice(half * width, (half + 1) * width)
            grid[layer, 0:rows, at_lanes] = value
            grid[layer, rows:padded, at_lanes] = jnp.concatenate([before, after, nothing], axis=0)

    high, low = split2(grid[...].reshape((length + 4) * padded, 2 * width))
    along_z = dot(high, mz[0]) + (dot(low, mz[0]) + dot(high, mz[1]))
    along_z = along_z.reshape(length + 4, padded, lanes)
    block = [along_z[0], along_z[1] + along_z[2]]
    block += [along_z[k] for k in range(3, length + 1)]
    block += [along_z[length + 1] + along_z[length + 2], along_z[length + 3]]

    places = [(rows,), (rows + 1, 0)] + [(k,) for k in range(1, rows - 1)]
    places += [(rows - 1, rows + 2), (rows + 3,)]
    for p in range(ext):
        value = sum(cx[a * ext + p : a * ext + p + 1, :] * block[a] for a in range(ext))
        total = None
        for b in range(ext):
            row = sum(value[k : k + 1] for k in places[b])
            term = cy[0, b] * row
            total = term if total is None else total + term
        total = total * rate[p]
        spectral[p] = sum(cy[1, q] * total[q : q + 1] for q in range(ext))
    back = []
    for a in range(ext):
        back.append(sum(cx[a * ext + p : a * ext + p + 1, :] * spectral[p] for p in range(ext)))
    high, low = split2(jnp.concatenate(back, axis=0))
    result = dot(high, mz[0], True) + (dot(low, mz[0], True) + dot(high, mz[1], True))
    out_ref[...] = result.reshape(out_ref.shape)


def totals(layer, mine_ref, other_ref, width, rows=slice(None)):
    own = mine_ref[layer, rows, 0:width] + other_ref[layer, rows, width:]
    partner = mine_ref[layer, rows, width:] + other_ref[layer, rows, 0:width]
    return own, partner


def return_layers_kernel(mine_ref, other_ref, out_ref):
    ext, padded, width = mine_ref.shape
    nodes, width = ext - 2, width // 2
    start = lax.axis_index("gz") * nodes
    for layer in range(2):
        own, partner = totals(start + layer, mine_ref, other_ref, width)
        for half, value in enumerate((partner, own)):
            place = half * 2 + layer
            out_ref[place] = value[0:nodes]
            out_ref[4, 2 * place : 2 * place + 2, :] = value[nodes : nodes + 2]


def interior_kernel(mine_ref, other_ref, after_ref, out_ref):
    ext, padded, width = mine_ref.shape
    for layer in range(1, ext - 1):
        own, partner = totals(layer, mine_ref, other_ref, width // 2)
        out_ref[0, layer - 1] = own
        out_ref[1, layer - 1] = partner


def return_rows_kernel(initial_ref, inner_ref, direct_ref, passed_ref, out_ref, base_ref):
    core = lax.axis_index("gz")
    has_low, has_high = edges("gx")
    nodes, rows, _ = initial_ref.shape
    for layer in range(nodes):
        values = [inner_ref[h, layer] for h in range(2)]
        outer = [values[h][rows : rows + 2] for h in range(2)]
        values = [values[h][0:rows] for h in range(2)]
        if layer < 2 or layer >= nodes - 2:
            slot = layer if layer < 2 else layer - (nodes - 2)

            def parts(ref, h, slot=slot):
                place = 2 * h + slot
                return ref[place], ref[4, 2 * place : 2 * place + 2, :]

            direct = [parts(direct_ref, h) for h in range(2)]
            passed = [parts(passed_ref, h) for h in range(2)]
            side = 0 if layer < 2 else 1
            valid = (has_low, has_high)[side]
            for k, target in enumerate((values, outer)):
                both = both_sides(core, [d[k] for d in direct], [d[k] for d in passed])[side]
                for h in range(2):
                    target[h] = target[h] + jnp.where(valid, both[h], jnp.zeros_like(both[h]))
        base_ref[layer] = initial_ref[layer] + values[0]
        for place, h in enumerate((1, 0)):
            row = layer * 4 + place * 2
            first = jnp.where(core == 0, outer[h][0:1], values[h][rows - 1 : rows])
            second = jnp.where(core == 0, values[h][0:1], outer[h][1:2])
            out_ref[row // 8, row % 8 : row % 8 + 1, :] = first
            out_ref[row // 8, row % 8 + 1 : row % 8 + 2, :] = second


def result_kernel(base_ref, direct_ref, passed_ref, out_ref):
    core = lax.axis_index("gz")
    has_low, has_high = edges("gy")
    nodes, rows, _ = base_ref.shape
    for layer in range(nodes):
        place, row = divmod(layer * 4, 8)
        direct = direct_ref[place, row : row + 2, :]
        passed = passed_ref[place, row + 2 : row + 4, :]
        low = jnp.where(core == 0, direct, passed)
        high = jnp.where(core == 0, passed, direct)
        low = jnp.where(has_low, low, jnp.zeros_like(low))
        high = jnp.where(has_high, high, jnp.zeros_like(high))
        between = jnp.zeros((rows - 4, low.shape[1]), f32)
        out_ref[layer] = base_ref[layer] + jnp.concatenate([low, between, high], axis=0)


def swap_pairs(axis):
    sizes = [lax.axis_size(name) for name in AXES]
    along, across = (0, 1) if axis == "gx" else (1, 0)

    def number(place, other, core):
        spot = (place, other) if along == 0 else (other, place)
        return (spot[0] * sizes[1] + spot[1]) * 2 + core

    pairs = []
    for other in range(sizes[across]):
        for place in range(sizes[along] - 1):
            here, there = number(place, other, 1), number(place + 1, other, 0)
            pairs += [(here, there), (there, here)]
        if other ^ 1 < sizes[across]:
            for place, core in ((0, 0), (sizes[along] - 1, 1)):
                pairs.append((number(place, other, core), number(place, other ^ 1, core)))
    return pairs


def swap(value, axis):
    if axis == "gz":
        return lax.ppermute(value, "gz", [(0, 1), (1, 0)])
    return lax.ppermute(value, AXES, swap_pairs(axis))


def paired_body(initial, source, metric, eigenvectors, eigenvalues):
    nodes, rows, width = initial.shape
    ext = eigenvectors.shape[1]
    blocks = width // nodes
    lanes = blocks * ext
    padded = 2 * rows

    own = call(
        residual_kernel,
        [shaped(initial.shape)],
        [initial, source, metric, *operator_tables(rows, width)],
    )[0]
    vectors = eigenvectors.reshape(3 * ext * ext, 1, blocks)
    values = eigenvalues.reshape(3 * ext, 1, blocks)
    cx, cy, rate, mz = call(
        coefficients_kernel,
        [
            shaped((ext * ext, lanes)),
            shaped((2, ext, padded, lanes)),
            shaped((ext, padded, lanes)),
            shaped((2, 2 * width, lanes), bf16),
        ],
        [vectors, values, *spread_tables(blocks, ext), own],
    )
    partner = swap(own, "gz")
    sent = call(layers_kernel, [shaped((2, 2, rows, width))], [own, partner])[0]
    x_direct = swap(sent, "gx")
    x_passed = swap(x_direct, "gz")
    sent = call(
        rows_kernel,
        [shaped(((nodes + 4) * 4 // 8, 8, width))],
        [own, partner, x_direct, x_passed],
    )[0]
    y_direct = swap(sent, "gy")
    y_passed = swap(y_direct, "gz")
    mine = call(
        solve_kernel,
        [shaped((ext, padded, 2 * width))],
        [own, partner, x_direct, x_passed, y_direct, y_passed, cx, cy, rate, mz],
        scratch=[
            pltpu.VMEM((nodes + 4, padded, 2 * width), f32),
            pltpu.VMEM((ext, padded, lanes), f32),
        ],
    )[0]

    other = swap(mine, "gz")
    sent = call(return_layers_kernel, [shaped((5, rows, width))], [mine, other])[0]
    inner = call(interior_kernel, [shaped((2, nodes, padded, width))], [mine, other, sent])[0]
    x_direct = swap(sent, "gx")
    x_passed = swap(x_direct, "gz")
    sent, base = call(
        return_rows_kernel,
        [shaped((nodes * 4 // 8, 8, width)), shaped(initial.shape)],
        [initial, inner, x_direct, x_passed],
    )
    y_direct = swap(sent, "gy")
    y_passed = swap(y_direct, "gz")
    return call(result_kernel, [shaped(initial.shape)], [base, y_direct, y_passed])[0]


def body(initial, source, metric, eigenvectors, eigenvalues):
    nodes = gll_points.shape[0]
    one_element = initial.shape[0] == nodes and initial.shape[1] == nodes
    if lax.axis_size("gz") == 2 and one_element and initial.shape[2] % 128 == 0:
        return paired_body(initial, source, metric, eigenvectors, eigenvalues)
    return general_body(initial, source, metric, eigenvectors, eigenvalues)


def solution(mesh):
    placed = (
        P("gx", "gy", "gz"),
        P("gx", "gy", "gz"),
        P(None, "gx", "gy", "gz"),
        P(None, None, None, "gx", "gy", "gz"),
        P(None, None, "gx", "gy", "gz"),
    )
    return jax.shard_map(
        body, mesh=mesh, in_specs=placed, out_specs=P("gx", "gy", "gz"), check_vma=False
    )
```

```python
import functools

import jax
import jax.numpy as jnp
import ml_dtypes
import numpy as np
from jax import lax
from jax.experimental import pallas as pl
from jax.experimental.pallas import tpu as pltpu
from jax.sharding import PartitionSpec as P

gll_points = np.array(
    [
        -1.0,
        -0.8717401485096066,
        -0.5917001814331423,
        -0.2092992179024789,
        0.2092992179024789,
        0.5917001814331423,
        0.8717401485096066,
        1.0,
    ]
)


def extended_2(value, sides, width):
    for axis, dim in sides:
        size, length = (lax.axis_size(axis), value.shape[dim])
        up = [(i, (i + 1) % size) for i in range(size - 1)]
        down = [(j, i) for i, j in up]
        last = lax.slice_in_dim(value, length - width, length, axis=dim)
        first = lax.slice_in_dim(value, 0, width, axis=dim)
        before = lax.ppermute(last, axis, up)
        after = lax.ppermute(first, axis, down)
        value = jnp.concatenate([before, value, after], axis=dim)
    return value


def derivative_table():
    number = gll_points.shape[0]
    products = np.array(
        [
            np.prod(
                [
                    gll_points[row_index] - gll_points[other]
                    for other in range(number)
                    if other != row_index
                ]
            )
            for row_index in range(number)
        ]
    )
    matrix_out = np.zeros((number, number))
    for row_index in range(number):
        for col_index in range(number):
            if row_index != col_index:
                matrix_out[row_index, col_index] = (
                    products[row_index]
                    / products[col_index]
                    / (gll_points[row_index] - gll_points[col_index])
                )
        matrix_out[row_index, row_index] = -np.sum(matrix_out[row_index])
    return matrix_out


def apply_along(values, matrix, direction):
    block_size = matrix.shape[1]
    old_shape = values.shape
    pieces_shape = (
        old_shape[:direction]
        + (old_shape[direction] // block_size, block_size)
        + old_shape[direction + 1 :]
    )
    result = jnp.tensordot(
        values.reshape(pieces_shape),
        matrix,
        axes=((direction + 1,), (1,)),
        precision=lax.Precision.HIGHEST,
    )
    result = jnp.moveaxis(result, -1, direction + 1)
    return result.reshape(
        old_shape[:direction]
        + (old_shape[direction] // block_size * matrix.shape[0],)
        + old_shape[direction + 1 :]
    )


def apply_operator(values, metric):
    deriv_table = jnp.asarray(derivative_table(), jnp.float32)
    summed = jnp.zeros_like(values)
    for direction in range(3):
        gradient = apply_along(values, deriv_table, direction)
        summed = summed + apply_along(metric[direction] * gradient, deriv_table.T, direction)
    return summed


def assemble(padded, offset):
    result = padded
    for direction in range(3):
        length = result.shape[direction]
        view_shape = [1, 1, 1]
        view_shape[direction] = length
        node_index = ((jnp.arange(length) - offset) % 8).reshape(view_shape)
        edge_zero = jnp.zeros_like(lax.slice_in_dim(result, 0, 1, axis=direction))
        upward = jnp.concatenate(
            [lax.slice_in_dim(result, 1, length, axis=direction), edge_zero], axis=direction
        )
        downward = jnp.concatenate(
            [edge_zero, lax.slice_in_dim(result, 0, length - 1, axis=direction)], axis=direction
        )
        result = (
            result
            + jnp.where(node_index == 7, upward, 0.0)
            + jnp.where(node_index == 0, downward, 0.0)
        )
    return result


def extend_axis(padded, direction):
    shifted = jnp.moveaxis(padded, direction, 0)
    blocks = (shifted.shape[0] - 4) // 8
    trailing = shifted.shape[1:]
    middle = shifted[2:-2].reshape((blocks, 8) + trailing)
    lowest = shifted[0 : 8 * blocks : 8][:, None]
    beyond = shifted[11::8][:, None]
    joined = jnp.concatenate([lowest, middle, beyond], axis=1).reshape((blocks * 10,) + trailing)
    return jnp.moveaxis(joined, 0, direction)


def widen(padded):
    return extend_axis(extend_axis(extend_axis(padded, 0), 1), 2)


def fast_solve(extended, eigenvectors, eigenvalues):
    count_x, count_y, count_z = eigenvectors.shape[3:]
    precise = lax.Precision.HIGHEST
    spectral = extended.reshape(count_x, 10, count_y, 10, count_z, 10)
    spectral = jnp.einsum("apxyz,xaybzc->xpybzc", eigenvectors[0], spectral, precision=precise)
    spectral = jnp.einsum("bqxyz,xpybzc->xpyqzc", eigenvectors[1], spectral, precision=precise)
    spectral = jnp.einsum("csxyz,xpyqzc->xpyqzs", eigenvectors[2], spectral, precision=precise)
    rate_x = jnp.transpose(eigenvalues[0], (1, 0, 2, 3))[:, :, :, None, :, None]
    rate_y = jnp.transpose(eigenvalues[1], (1, 2, 0, 3))[:, None, :, :, :, None]
    rate_z = jnp.transpose(eigenvalues[2], (1, 2, 3, 0))[:, None, :, None, :, :]
    spectral = spectral / (rate_x + rate_y + rate_z)
    spectral = jnp.einsum("csxyz,xpyqzs->xpyqzc", eigenvectors[2], spectral, precision=precise)
    spectral = jnp.einsum("bqxyz,xpyqzc->xpybzc", eigenvectors[1], spectral, precision=precise)
    spectral = jnp.einsum("apxyz,xpybzc->xaybzc", eigenvectors[0], spectral, precision=precise)
    return spectral.reshape(count_x * 10, count_y * 10, count_z * 10)


def return_axis(padded, direction):
    shifted = jnp.moveaxis(padded, direction, 0)
    blocks = (shifted.shape[0] - 4) // 10
    trailing = shifted.shape[1:]
    owned = shifted[2:-2].reshape((blocks, 10) + trailing)[:, 1:9]
    before = shifted[0 : 10 * blocks].reshape((blocks, 10) + trailing)[:, 0:2]
    following = shifted[4:].reshape((blocks, 10) + trailing)[:, 8:10]
    middle = jnp.zeros((blocks, 4) + trailing, shifted.dtype)
    summed = owned + jnp.concatenate([before, middle, following], axis=1)
    return jnp.moveaxis(summed.reshape((blocks * 8,) + trailing), 0, direction)


def general_body(initial, source, metric, eigenvectors, eigenvalues):
    solution = initial
    local_res = source - apply_operator(solution, metric)
    deeper = extended_2(local_res, (("gx", 0), ("gy", 1), ("gz", 2)), 2)
    widened = assemble(deeper, 2)
    extended = widen(widened)
    corrected = fast_solve(extended, eigenvectors, eigenvalues)
    padded = extended_2(corrected, (("gx", 0), ("gy", 1), ("gz", 2)), 2)
    correction = return_axis(return_axis(return_axis(padded, 0), 1), 2)
    solution = solution + correction
    return solution


AXES = ("gx", "gy", "gz")
VMEM = pl.BlockSpec(memory_space=pltpu.VMEM)
HBM = pl.BlockSpec(memory_space=pltpu.HBM)
VMEM_LIMIT = 16 * 2**20
f32 = jnp.float32
bf16 = jnp.bfloat16


def call(kernel, outs, args, flops=0, scratch=(), where=VMEM):
    moved = sum(int(np.prod(a.shape)) * a.dtype.itemsize for a in (*args, *outs))
    return pl.pallas_call(
        kernel,
        out_shape=outs,
        in_specs=[where] * len(args),
        out_specs=[VMEM] * len(outs),
        scratch_shapes=scratch,
        compiler_params=pltpu.CompilerParams(vmem_limit_bytes=VMEM_LIMIT),
        cost_estimate=pl.CostEstimate(flops=flops, bytes_accessed=moved, transcendentals=0),
    )(*args)


def shaped(shape, dtype=f32):
    return jax.ShapeDtypeStruct(shape, dtype)


def split2(value):
    high = value.astype(bf16)
    return high, (value - high.astype(f32)).astype(bf16)


def split3(value):
    high = value.astype(bf16)
    rest = value - high.astype(f32)
    middle = rest.astype(bf16)
    return high, middle, (rest - middle.astype(f32)).astype(bf16)


def table_split2(table):
    table = np.asarray(table, np.float32)
    high = table.astype(ml_dtypes.bfloat16)
    return high, (table - high.astype(np.float32)).astype(ml_dtypes.bfloat16)


def dot(left, right, transposed=False):
    dims = (((1,), (1 if transposed else 0,)), ((), ()))
    return lax.dot_general(left, right, dims, preferred_element_type=f32)


def operator_tables(count_y, length_z):
    table = np.asarray(derivative_table(), np.float32)
    nodes = table.shape[0]
    along_y = np.kron(np.eye(nodes), table)
    along_z = np.kron(np.eye(length_z // nodes), table.T)
    tables = []
    for matrix in (along_y, along_y.T):
        high, low = table_split2(matrix)
        tables.append(np.concatenate([high, high, low], axis=1))
    for matrix in (along_z, along_z.T):
        high, low = table_split2(matrix)
        tables.append(np.concatenate([high, high, low], axis=0))
    return [jnp.asarray(t) for t in tables]


def residual_kernel(*refs):
    count = (len(refs) - 2) // 2
    copies = [
        pltpu.make_async_copy(refs[k], refs[count + 1 + k], refs[-1].at[k]) for k in range(count)
    ]
    out_ref = refs[count]
    u_ref, source_ref, metric_ref, ay, ayt, bz, bzt = refs[count + 1 : -1]
    for copy in copies:
        copy.start()
    for copy in copies:
        copy.wait()
    nodes, rows, width = u_ref.shape
    table = np.asarray(derivative_table(), np.float32)

    def stacked(value, axis):
        high, low = split2(value)
        return jnp.concatenate([high, low, high], axis=axis)

    flat = u_ref[...].reshape(nodes * rows, width)
    along_y = dot(ay[...], stacked(flat, 0)) * metric_ref[1].reshape(flat.shape)
    along_z = dot(stacked(flat, 1), bz[...]) * metric_ref[2].reshape(flat.shape)
    total = dot(ayt[...], stacked(along_y, 0)) + dot(stacked(along_z, 1), bzt[...])
    total = total.reshape(nodes, rows, width)
    layers = [u_ref[j] for j in range(nodes)]
    fluxes = []
    for i in range(nodes):
        gradient = sum(float(table[i, j]) * layers[j] for j in range(nodes))
        fluxes.append(metric_ref[0, i] * gradient)
    for j in range(nodes):
        applied = sum(float(table[i, j]) * fluxes[i] for i in range(nodes))
        out_ref[j] = source_ref[j] - (applied + total[j])


def spread_tables(blocks, ext):
    lanes = np.arange(blocks * ext)
    repeat = (lanes[None, :] // ext == np.arange(blocks)[:, None]).astype(np.float32)
    repeat = np.concatenate([repeat] * 3, axis=0)
    rows = np.arange(ext * ext)
    mask = (rows[:, None] % ext == lanes[None, :] % ext).astype(np.float32)
    gather = (rows[None, :] // ext == np.arange(ext)[:, None]).astype(np.float32)
    gather = np.concatenate([gather] * 3, axis=1)
    padded = 2 * (ext - 2)
    order = list(range(1, ext - 1)) + [0, ext - 1]
    forward = np.zeros((ext, padded, ext * ext), np.float32)
    backward = np.zeros((ext, padded, ext * ext), np.float32)
    for first in range(ext):
        for second in range(ext):
            forward[first, second, first * ext + second] = 1
            backward[first, second, order[second] * ext + first] = 1
    both = np.concatenate([forward.reshape(-1, ext * ext), backward.reshape(-1, ext * ext)])
    both = np.concatenate([both] * 3, axis=1)
    return [
        jnp.asarray(repeat, bf16),
        jnp.asarray(mask),
        jnp.asarray(gather, bf16),
        jnp.asarray(both, bf16),
    ]


def coefficients_kernel(
    vec_ref, val_ref, repeat, mask, gather, both, after_ref, cx_ref, cy_ref, rate_ref, mz_ref
):
    ext = rate_ref.shape[0]
    square = ext * ext
    padded, lanes = rate_ref.shape[1:]
    blocks = lanes // ext
    nodes = ext - 2
    core = lax.axis_index("gz")

    def spread(ref, first, count):
        value = ref[first : first + count].reshape(count, blocks)
        return dot(jnp.concatenate(split3(value), axis=1), repeat[...])

    cx_ref[...] = spread(vec_ref, 0, square)
    along_y = spread(vec_ref, square, square)
    cy_ref[...] = dot(both[...], jnp.concatenate(split3(along_y), axis=0)).reshape(cy_ref.shape)
    along_z = spread(vec_ref, 2 * square, square) * mask[...]
    along_z = dot(gather[...], jnp.concatenate(split3(along_z), axis=0))

    rate_x = spread(val_ref, 0, ext)
    rate_y = spread(val_ref, ext, ext)
    rate_z = jnp.sum(spread(val_ref, 2 * ext, ext) * mask[0:ext, :], axis=0, keepdims=True)
    rate_y = jnp.concatenate([rate_y, jnp.ones((padded - ext, lanes), f32)], axis=0)
    for p in range(ext):
        rate_ref[p] = 1.0 / (rate_x[p : p + 1] + rate_y + rate_z)

    zeros = jnp.zeros((nodes - 2, lanes), f32)
    own = along_z[1 : nodes + 1]
    below = jnp.concatenate([zeros, along_z[0:2]], axis=0)
    above = jnp.concatenate([along_z[nodes : nodes + 2], zeros], axis=0)
    element = lax.broadcasted_iota(jnp.int32, (nodes, lanes), 1) // ext
    zero = jnp.zeros_like(own)
    for half in range(2):
        shift = 0 if half == 0 else jnp.where(core == 0, blocks, -blocks)
        for first in range(0, blocks, 2):
            pair = []
            for block in (first + shift, first + 1 + shift):
                value = jnp.where(element == block, own, zero)
                value = value + jnp.where(element == block + 1, below, zero)
                pair.append(value + jnp.where(element == block - 1, above, zero))
            high, low = split2(jnp.concatenate(pair, axis=0))
            start = (half * blocks + first) * nodes
            mz_ref[0, start : start + 2 * nodes, :] = high
            mz_ref[1, start : start + 2 * nodes, :] = low


def both_sides(core, direct, passed):
    low = [jnp.where(core == 0, direct[h], passed[1 - h]) for h in range(2)]
    high = [jnp.where(core == 0, passed[1 - h], direct[h]) for h in range(2)]
    return low, high


def edges(axis):
    place, size = lax.axis_index(axis), lax.axis_size(axis)
    return place > 0, place < size - 1


def layers_kernel(own_ref, partner_ref, out_ref):
    start = lax.axis_index("gz") * (own_ref.shape[0] - 2)
    for half, ref in enumerate((partner_ref, own_ref)):
        for layer in range(2):
            out_ref[half, layer] = ref[start + layer]


def x_layers(core, own_ref, partner_ref, direct_ref, passed_ref):
    has_low, has_high = edges("gx")
    length = own_ref.shape[0]

    def at(layer):
        if 2 <= layer < length + 2:
            return own_ref[layer - 2], partner_ref[layer - 2]
        slot = layer if layer < 2 else layer - length - 2
        direct = [direct_ref[h, slot] for h in range(2)]
        passed = [passed_ref[h, slot] for h in range(2)]
        low, high = both_sides(core, direct, passed)
        side, valid = (low, has_low) if layer < 2 else (high, has_high)
        return [jnp.where(valid, v, jnp.zeros_like(v)) for v in side]

    return at


def rows_kernel(own_ref, partner_ref, direct_ref, passed_ref, out_ref):
    core = lax.axis_index("gz")
    length, rows, _ = own_ref.shape
    at = x_layers(core, own_ref, partner_ref, direct_ref, passed_ref)
    for layer in range(length + 4):
        own, partner = at(layer)
        for half, value in enumerate((partner, own)):
            row = layer * 4 + half * 2
            out_ref[row // 8, row % 8 : row % 8 + 2, :] = jnp.where(
                core == 0, value[0:2], value[rows - 2 : rows]
            )


def solve_kernel(
    own_ref, partner_ref, xd_ref, xp_ref, yd_ref, yp_ref, cx, cy, rate, mz, out_ref, grid, spectral
):
    core = lax.axis_index("gz")
    length, rows, width = own_ref.shape
    ext, padded, lanes = rate.shape
    has_low, has_high = edges("gy")
    at = x_layers(core, own_ref, partner_ref, xd_ref, xp_ref)
    nothing = jnp.zeros((padded - rows - 4, width), f32)
    for layer in range(length + 4):
        place, row = divmod(layer * 4, 8)
        direct = [yd_ref[place, row + 2 * h : row + 2 * h + 2, :] for h in range(2)]
        passed = [yp_ref[place, row + 2 * h : row + 2 * h + 2, :] for h in range(2)]
        low, high = both_sides(core, direct, passed)
        for half, value in enumerate(at(layer)):
            before = jnp.where(has_low, low[half], jnp.zeros_like(low[half]))
            after = jnp.where(has_high, high[half], jnp.zeros_like(high[half]))
            at_lanes = slice(half * width, (half + 1) * width)
            grid[layer, 0:rows, at_lanes] = value
            grid[layer, rows:padded, at_lanes] = jnp.concatenate([before, after, nothing], axis=0)

    high, low = split2(grid[...].reshape((length + 4) * padded, 2 * width))
    along_z = dot(high, mz[0]) + (dot(low, mz[0]) + dot(high, mz[1]))
    along_z = along_z.reshape(length + 4, padded, lanes)
    block = [along_z[0], along_z[1] + along_z[2]]
    block += [along_z[k] for k in range(3, length + 1)]
    block += [along_z[length + 1] + along_z[length + 2], along_z[length + 3]]

    places = [(rows,), (rows + 1, 0)] + [(k,) for k in range(1, rows - 1)]
    places += [(rows - 1, rows + 2), (rows + 3,)]
    for p in range(ext):
        value = sum(cx[a * ext + p : a * ext + p + 1, :] * block[a] for a in range(ext))
        total = None
        for b in range(ext):
            row = sum(value[k : k + 1] for k in places[b])
            term = cy[0, b] * row
            total = term if total is None else total + term
        total = total * rate[p]
        spectral[p] = sum(cy[1, q] * total[q : q + 1] for q in range(ext))
    back = []
    for a in range(ext):
        back.append(sum(cx[a * ext + p : a * ext + p + 1, :] * spectral[p] for p in range(ext)))
    high, low = split2(jnp.concatenate(back, axis=0))
    result = dot(high, mz[0], True) + (dot(low, mz[0], True) + dot(high, mz[1], True))
    out_ref[...] = result.reshape(out_ref.shape)


def totals(layer, mine_ref, other_ref, width, rows=slice(None)):
    own = mine_ref[layer, rows, 0:width] + other_ref[layer, rows, width:]
    partner = mine_ref[layer, rows, width:] + other_ref[layer, rows, 0:width]
    return own, partner


def return_layers_kernel(mine_ref, other_ref, out_ref):
    ext, padded, width = mine_ref.shape
    nodes, width = ext - 2, width // 2
    start = lax.axis_index("gz") * nodes
    for layer in range(2):
        own, partner = totals(start + layer, mine_ref, other_ref, width)
        for half, value in enumerate((partner, own)):
            place = half * 2 + layer
            out_ref[place] = value[0:nodes]
            out_ref[4, 2 * place : 2 * place + 2, :] = value[nodes : nodes + 2]


def interior_kernel(mine_ref, other_ref, after_ref, out_ref):
    ext, padded, width = mine_ref.shape
    for layer in range(1, ext - 1):
        own, partner = totals(layer, mine_ref, other_ref, width // 2)
        out_ref[0, layer - 1] = own
        out_ref[1, layer - 1] = partner


def return_rows_kernel(initial_ref, inner_ref, direct_ref, passed_ref, out_ref, base_ref):
    core = lax.axis_index("gz")
    has_low, has_high = edges("gx")
    nodes, rows, _ = initial_ref.shape
    for layer in range(nodes):
        values = [inner_ref[h, layer] for h in range(2)]
        outer = [values[h][rows : rows + 2] for h in range(2)]
        values = [values[h][0:rows] for h in range(2)]
        if layer < 2 or layer >= nodes - 2:
            slot = layer if layer < 2 else layer - (nodes - 2)

            def parts(ref, h, slot=slot):
                place = 2 * h + slot
                return ref[place], ref[4, 2 * place : 2 * place + 2, :]

            direct = [parts(direct_ref, h) for h in range(2)]
            passed = [parts(passed_ref, h) for h in range(2)]
            side = 0 if layer < 2 else 1
            valid = (has_low, has_high)[side]
            for k, target in enumerate((values, outer)):
                both = both_sides(core, [d[k] for d in direct], [d[k] for d in passed])[side]
                for h in range(2):
                    target[h] = target[h] + jnp.where(valid, both[h], jnp.zeros_like(both[h]))
        base_ref[layer] = initial_ref[layer] + values[0]
        for place, h in enumerate((1, 0)):
            row = layer * 4 + place * 2
            first = jnp.where(core == 0, outer[h][0:1], values[h][rows - 1 : rows])
            second = jnp.where(core == 0, values[h][0:1], outer[h][1:2])
            out_ref[row // 8, row % 8 : row % 8 + 1, :] = first
            out_ref[row // 8, row % 8 + 1 : row % 8 + 2, :] = second


def result_kernel(base_ref, direct_ref, passed_ref, out_ref):
    core = lax.axis_index("gz")
    has_low, has_high = edges("gy")
    nodes, rows, _ = base_ref.shape
    for layer in range(nodes):
        place, row = divmod(layer * 4, 8)
        direct = direct_ref[place, row : row + 2, :]
        passed = passed_ref[place, row + 2 : row + 4, :]
        low = jnp.where(core == 0, direct, passed)
        high = jnp.where(core == 0, passed, direct)
        low = jnp.where(has_low, low, jnp.zeros_like(low))
        high = jnp.where(has_high, high, jnp.zeros_like(high))
        between = jnp.zeros((rows - 4, low.shape[1]), f32)
        out_ref[layer] = base_ref[layer] + jnp.concatenate([low, between, high], axis=0)


def swap_pairs(axis):
    sizes = [lax.axis_size(name) for name in AXES]
    along, across = (0, 1) if axis == "gx" else (1, 0)

    def number(place, other, core):
        spot = (place, other) if along == 0 else (other, place)
        return (spot[0] * sizes[1] + spot[1]) * 2 + core

    pairs = []
    for other in range(sizes[across]):
        for place in range(sizes[along] - 1):
            here, there = number(place, other, 1), number(place + 1, other, 0)
            pairs += [(here, there), (there, here)]
        if other ^ 1 < sizes[across]:
            for place, core in ((0, 0), (sizes[along] - 1, 1)):
                pairs.append((number(place, other, core), number(place, other ^ 1, core)))
    return pairs


def swap(value, axis):
    if axis == "gz":
        return lax.ppermute(value, "gz", [(0, 1), (1, 0)])
    return lax.ppermute(value, AXES, swap_pairs(axis))


def paired_body(initial, source, metric, eigenvectors, eigenvalues):
    nodes, rows, width = initial.shape
    ext = eigenvectors.shape[1]
    blocks = width // nodes
    lanes = blocks * ext
    padded = 2 * rows

    inputs = [initial, source, metric, *operator_tables(rows, width)]
    own = call(
        residual_kernel,
        [shaped(initial.shape)],
        inputs,
        scratch=[
            *(pltpu.VMEM(value.shape, value.dtype) for value in inputs),
            pltpu.SemaphoreType.DMA((len(inputs),)),
        ],
        where=HBM,
    )[0]
    vectors = eigenvectors.reshape(3 * ext * ext, 1, blocks)
    values = eigenvalues.reshape(3 * ext, 1, blocks)
    cx, cy, rate, mz = call(
        coefficients_kernel,
        [
            shaped((ext * ext, lanes)),
            shaped((2, ext, padded, lanes)),
            shaped((ext, padded, lanes)),
            shaped((2, 2 * width, lanes), bf16),
        ],
        [vectors, values, *spread_tables(blocks, ext), own],
    )
    partner = swap(own, "gz")
    sent = call(layers_kernel, [shaped((2, 2, rows, width))], [own, partner])[0]
    x_direct = swap(sent, "gx")
    x_passed = swap(x_direct, "gz")
    sent = call(
        rows_kernel,
        [shaped(((nodes + 4) * 4 // 8, 8, width))],
        [own, partner, x_direct, x_passed],
    )[0]
    y_direct = swap(sent, "gy")
    y_passed = swap(y_direct, "gz")
    mine = call(
        solve_kernel,
        [shaped((ext, padded, 2 * width))],
        [own, partner, x_direct, x_passed, y_direct, y_passed, cx, cy, rate, mz],
        scratch=[
            pltpu.VMEM((nodes + 4, padded, 2 * width), f32),
            pltpu.VMEM((ext, padded, lanes), f32),
        ],
    )[0]

    other = swap(mine, "gz")
    sent = call(return_layers_kernel, [shaped((5, rows, width))], [mine, other])[0]
    inner = call(interior_kernel, [shaped((2, nodes, padded, width))], [mine, other, sent])[0]
    x_direct = swap(sent, "gx")
    x_passed = swap(x_direct, "gz")
    sent, base = call(
        return_rows_kernel,
        [shaped((nodes * 4 // 8, 8, width)), shaped(initial.shape)],
        [initial, inner, x_direct, x_passed],
    )
    y_direct = swap(sent, "gy")
    y_passed = swap(y_direct, "gz")
    return call(result_kernel, [shaped(initial.shape)], [base, y_direct, y_passed])[0]


def body(initial, source, metric, eigenvectors, eigenvalues):
    nodes = gll_points.shape[0]
    one_element = initial.shape[0] == nodes and initial.shape[1] == nodes
    if lax.axis_size("gz") == 2 and one_element and initial.shape[2] % 128 == 0:
        return paired_body(initial, source, metric, eigenvectors, eigenvalues)
    return general_body(initial, source, metric, eigenvectors, eigenvalues)


def solution(mesh):
    placed = (
        P("gx", "gy", "gz"),
        P("gx", "gy", "gz"),
        P(None, "gx", "gy", "gz"),
        P(None, None, None, "gx", "gy", "gz"),
        P(None, None, "gx", "gy", "gz"),
    )
    return jax.shard_map(
        body, mesh=mesh, in_specs=placed, out_specs=P("gx", "gy", "gz"), check_vma=False
    )
```

```python
import functools

import jax
import jax.numpy as jnp
import ml_dtypes
import numpy as np
from jax import lax
from jax.experimental import pallas as pl
from jax.experimental.pallas import tpu as pltpu
from jax.sharding import PartitionSpec as P

gll_points = np.array(
    [
        -1.0,
        -0.8717401485096066,
        -0.5917001814331423,
        -0.2092992179024789,
        0.2092992179024789,
        0.5917001814331423,
        0.8717401485096066,
        1.0,
    ]
)


def extended_2(value, sides, width):
    for axis, dim in sides:
        size, length = (lax.axis_size(axis), value.shape[dim])
        up = [(i, (i + 1) % size) for i in range(size - 1)]
        down = [(j, i) for i, j in up]
        last = lax.slice_in_dim(value, length - width, length, axis=dim)
        first = lax.slice_in_dim(value, 0, width, axis=dim)
        before = lax.ppermute(last, axis, up)
        after = lax.ppermute(first, axis, down)
        value = jnp.concatenate([before, value, after], axis=dim)
    return value


def derivative_table():
    number = gll_points.shape[0]
    products = np.array(
        [
            np.prod(
                [
                    gll_points[row_index] - gll_points[other]
                    for other in range(number)
                    if other != row_index
                ]
            )
            for row_index in range(number)
        ]
    )
    matrix_out = np.zeros((number, number))
    for row_index in range(number):
        for col_index in range(number):
            if row_index != col_index:
                matrix_out[row_index, col_index] = (
                    products[row_index]
                    / products[col_index]
                    / (gll_points[row_index] - gll_points[col_index])
                )
        matrix_out[row_index, row_index] = -np.sum(matrix_out[row_index])
    return matrix_out


def apply_along(values, matrix, direction):
    block_size = matrix.shape[1]
    old_shape = values.shape
    pieces_shape = (
        old_shape[:direction]
        + (old_shape[direction] // block_size, block_size)
        + old_shape[direction + 1 :]
    )
    result = jnp.tensordot(
        values.reshape(pieces_shape),
        matrix,
        axes=((direction + 1,), (1,)),
        precision=lax.Precision.HIGHEST,
    )
    result = jnp.moveaxis(result, -1, direction + 1)
    return result.reshape(
        old_shape[:direction]
        + (old_shape[direction] // block_size * matrix.shape[0],)
        + old_shape[direction + 1 :]
    )


def apply_operator(values, metric):
    deriv_table = jnp.asarray(derivative_table(), jnp.float32)
    summed = jnp.zeros_like(values)
    for direction in range(3):
        gradient = apply_along(values, deriv_table, direction)
        summed = summed + apply_along(metric[direction] * gradient, deriv_table.T, direction)
    return summed


def assemble(padded, offset):
    result = padded
    for direction in range(3):
        length = result.shape[direction]
        view_shape = [1, 1, 1]
        view_shape[direction] = length
        node_index = ((jnp.arange(length) - offset) % 8).reshape(view_shape)
        edge_zero = jnp.zeros_like(lax.slice_in_dim(result, 0, 1, axis=direction))
        upward = jnp.concatenate(
            [lax.slice_in_dim(result, 1, length, axis=direction), edge_zero], axis=direction
        )
        downward = jnp.concatenate(
            [edge_zero, lax.slice_in_dim(result, 0, length - 1, axis=direction)], axis=direction
        )
        result = (
            result
            + jnp.where(node_index == 7, upward, 0.0)
            + jnp.where(node_index == 0, downward, 0.0)
        )
    return result


def extend_axis(padded, direction):
    shifted = jnp.moveaxis(padded, direction, 0)
    blocks = (shifted.shape[0] - 4) // 8
    trailing = shifted.shape[1:]
    middle = shifted[2:-2].reshape((blocks, 8) + trailing)
    lowest = shifted[0 : 8 * blocks : 8][:, None]
    beyond = shifted[11::8][:, None]
    joined = jnp.concatenate([lowest, middle, beyond], axis=1).reshape((blocks * 10,) + trailing)
    return jnp.moveaxis(joined, 0, direction)


def widen(padded):
    return extend_axis(extend_axis(extend_axis(padded, 0), 1), 2)


def fast_solve(extended, eigenvectors, eigenvalues):
    count_x, count_y, count_z = eigenvectors.shape[3:]
    precise = lax.Precision.HIGHEST
    spectral = extended.reshape(count_x, 10, count_y, 10, count_z, 10)
    spectral = jnp.einsum("apxyz,xaybzc->xpybzc", eigenvectors[0], spectral, precision=precise)
    spectral = jnp.einsum("bqxyz,xpybzc->xpyqzc", eigenvectors[1], spectral, precision=precise)
    spectral = jnp.einsum("csxyz,xpyqzc->xpyqzs", eigenvectors[2], spectral, precision=precise)
    rate_x = jnp.transpose(eigenvalues[0], (1, 0, 2, 3))[:, :, :, None, :, None]
    rate_y = jnp.transpose(eigenvalues[1], (1, 2, 0, 3))[:, None, :, :, :, None]
    rate_z = jnp.transpose(eigenvalues[2], (1, 2, 3, 0))[:, None, :, None, :, :]
    spectral = spectral / (rate_x + rate_y + rate_z)
    spectral = jnp.einsum("csxyz,xpyqzs->xpyqzc", eigenvectors[2], spectral, precision=precise)
    spectral = jnp.einsum("bqxyz,xpyqzc->xpybzc", eigenvectors[1], spectral, precision=precise)
    spectral = jnp.einsum("apxyz,xpybzc->xaybzc", eigenvectors[0], spectral, precision=precise)
    return spectral.reshape(count_x * 10, count_y * 10, count_z * 10)


def return_axis(padded, direction):
    shifted = jnp.moveaxis(padded, direction, 0)
    blocks = (shifted.shape[0] - 4) // 10
    trailing = shifted.shape[1:]
    owned = shifted[2:-2].reshape((blocks, 10) + trailing)[:, 1:9]
    before = shifted[0 : 10 * blocks].reshape((blocks, 10) + trailing)[:, 0:2]
    following = shifted[4:].reshape((blocks, 10) + trailing)[:, 8:10]
    middle = jnp.zeros((blocks, 4) + trailing, shifted.dtype)
    summed = owned + jnp.concatenate([before, middle, following], axis=1)
    return jnp.moveaxis(summed.reshape((blocks * 8,) + trailing), 0, direction)


def general_body(initial, source, metric, eigenvectors, eigenvalues):
    solution = initial
    local_res = source - apply_operator(solution, metric)
    deeper = extended_2(local_res, (("gx", 0), ("gy", 1), ("gz", 2)), 2)
    widened = assemble(deeper, 2)
    extended = widen(widened)
    corrected = fast_solve(extended, eigenvectors, eigenvalues)
    padded = extended_2(corrected, (("gx", 0), ("gy", 1), ("gz", 2)), 2)
    correction = return_axis(return_axis(return_axis(padded, 0), 1), 2)
    solution = solution + correction
    return solution


AXES = ("gx", "gy", "gz")
VMEM = pl.BlockSpec(memory_space=pltpu.VMEM)
HBM = pl.BlockSpec(memory_space=pltpu.HBM)
VMEM_LIMIT = 16 * 2**20
f32 = jnp.float32
bf16 = jnp.bfloat16


def call(kernel, outs, args, flops=0, scratch=(), where=VMEM):
    moved = sum(int(np.prod(a.shape)) * a.dtype.itemsize for a in (*args, *outs))
    return pl.pallas_call(
        kernel,
        out_shape=outs,
        in_specs=[where] * len(args),
        out_specs=[VMEM] * len(outs),
        scratch_shapes=scratch,
        compiler_params=pltpu.CompilerParams(vmem_limit_bytes=VMEM_LIMIT),
        cost_estimate=pl.CostEstimate(flops=flops, bytes_accessed=moved, transcendentals=0),
    )(*args)


def shaped(shape, dtype=f32):
    return jax.ShapeDtypeStruct(shape, dtype)


def split2(value):
    high = value.astype(bf16)
    return high, (value - high.astype(f32)).astype(bf16)


def split3(value):
    high = value.astype(bf16)
    rest = value - high.astype(f32)
    middle = rest.astype(bf16)
    return high, middle, (rest - middle.astype(f32)).astype(bf16)


def table_split2(table):
    table = np.asarray(table, np.float32)
    high = table.astype(ml_dtypes.bfloat16)
    return high, (table - high.astype(np.float32)).astype(ml_dtypes.bfloat16)


def dot(left, right, transposed=False):
    dims = (((1,), (1 if transposed else 0,)), ((), ()))
    return lax.dot_general(left, right, dims, preferred_element_type=f32)


def operator_tables(count_y, length_z):
    table = np.asarray(derivative_table(), np.float32)
    nodes = table.shape[0]
    along_y = np.kron(np.eye(nodes), table)
    along_z = np.kron(np.eye(length_z // nodes), table.T)
    tables = []
    for matrix in (along_y, along_y.T):
        high, low = table_split2(matrix)
        tables.append(np.concatenate([high, high, low], axis=1))
    for matrix in (along_z, along_z.T):
        high, low = table_split2(matrix)
        tables.append(np.concatenate([high, high, low], axis=0))
    return [jnp.asarray(t) for t in tables]


def residual_kernel(*refs):
    count = (len(refs) - 2) // 2
    copies = [
        pltpu.make_async_copy(refs[k], refs[count + 1 + k], refs[-1].at[k]) for k in range(count)
    ]
    out_ref = refs[count]
    u_ref, source_ref, metric_ref, ay, ayt, bz, bzt = refs[count + 1 : -1]
    for copy in copies:
        copy.start()
    for copy in copies:
        copy.wait()
    nodes, rows, width = u_ref.shape
    table = np.asarray(derivative_table(), np.float32)

    def stacked(value, axis):
        high, low = split2(value)
        return jnp.concatenate([high, low, high], axis=axis)

    flat = u_ref[...].reshape(nodes * rows, width)
    along_y = dot(ay[...], stacked(flat, 0)) * metric_ref[1].reshape(flat.shape)
    along_z = dot(stacked(flat, 1), bz[...]) * metric_ref[2].reshape(flat.shape)
    total = dot(ayt[...], stacked(along_y, 0)) + dot(stacked(along_z, 1), bzt[...])
    total = total.reshape(nodes, rows, width)
    layers = [u_ref[j] for j in range(nodes)]
    fluxes = []
    for i in range(nodes):
        gradient = sum(float(table[i, j]) * layers[j] for j in range(nodes))
        fluxes.append(metric_ref[0, i] * gradient)
    for j in range(nodes):
        applied = sum(float(table[i, j]) * fluxes[i] for i in range(nodes))
        out_ref[j] = source_ref[j] - (applied + total[j])


def spread_tables(blocks, ext):
    lanes = np.arange(blocks * ext)
    repeat = (lanes[None, :] // ext == np.arange(blocks)[:, None]).astype(np.float32)
    repeat = np.concatenate([repeat] * 3, axis=0)
    rows = np.arange(ext * ext)
    mask = (rows[:, None] % ext == lanes[None, :] % ext).astype(np.float32)
    gather = (rows[None, :] // ext == np.arange(ext)[:, None]).astype(np.float32)
    gather = np.concatenate([gather] * 3, axis=1)
    padded = 2 * (ext - 2)
    order = list(range(1, ext - 1)) + [0, ext - 1]
    forward = np.zeros((ext, padded, ext * ext), np.float32)
    backward = np.zeros((ext, padded, ext * ext), np.float32)
    for first in range(ext):
        for second in range(ext):
            forward[first, second, first * ext + second] = 1
            backward[first, second, order[second] * ext + first] = 1
    both = np.concatenate([forward.reshape(-1, ext * ext), backward.reshape(-1, ext * ext)])
    both = np.concatenate([both] * 3, axis=1)
    return [
        jnp.asarray(repeat, bf16),
        jnp.asarray(mask),
        jnp.asarray(gather, bf16),
        jnp.asarray(both, bf16),
    ]


def coefficients_kernel(
    vec_ref, val_ref, repeat, mask, gather, both, after_ref, cx_ref, cy_ref, rate_ref, mz_ref
):
    ext = rate_ref.shape[0]
    square = ext * ext
    padded, lanes = rate_ref.shape[1:]
    blocks = lanes // ext
    nodes = ext - 2
    core = lax.axis_index("gz")

    def spread(ref, first, count):
        value = ref[first : first + count].reshape(count, blocks)
        return dot(jnp.concatenate(split3(value), axis=1), repeat[...])

    cx_ref[...] = spread(vec_ref, 0, square)
    along_y = spread(vec_ref, square, square)
    cy_ref[...] = dot(both[...], jnp.concatenate(split3(along_y), axis=0)).reshape(cy_ref.shape)
    along_z = spread(vec_ref, 2 * square, square) * mask[...]
    along_z = dot(gather[...], jnp.concatenate(split3(along_z), axis=0))

    rate_x = spread(val_ref, 0, ext)
    rate_y = spread(val_ref, ext, ext)
    rate_z = jnp.sum(spread(val_ref, 2 * ext, ext) * mask[0:ext, :], axis=0, keepdims=True)
    rate_y = jnp.concatenate([rate_y, jnp.ones((padded - ext, lanes), f32)], axis=0)
    for p in range(ext):
        rate_ref[p] = 1.0 / (rate_x[p : p + 1] + rate_y + rate_z)

    zeros = jnp.zeros((nodes - 2, lanes), f32)
    own = along_z[1 : nodes + 1]
    below = jnp.concatenate([zeros, along_z[0:2]], axis=0)
    above = jnp.concatenate([along_z[nodes : nodes + 2], zeros], axis=0)
    element = lax.broadcasted_iota(jnp.int32, (nodes, lanes), 1) // ext
    zero = jnp.zeros_like(own)
    for half in range(2):
        shift = 0 if half == 0 else jnp.where(core == 0, blocks, -blocks)
        for first in range(0, blocks, 2):
            pair = []
            for block in (first + shift, first + 1 + shift):
                value = jnp.where(element == block, own, zero)
                value = value + jnp.where(element == block + 1, below, zero)
                pair.append(value + jnp.where(element == block - 1, above, zero))
            high, low = split2(jnp.concatenate(pair, axis=0))
            start = (half * blocks + first) * nodes
            mz_ref[0, start : start + 2 * nodes, :] = high
            mz_ref[1, start : start + 2 * nodes, :] = low


def both_sides(core, direct, passed):
    low = [jnp.where(core == 0, direct[h], passed[1 - h]) for h in range(2)]
    high = [jnp.where(core == 0, passed[1 - h], direct[h]) for h in range(2)]
    return low, high


def edges(axis):
    place, size = lax.axis_index(axis), lax.axis_size(axis)
    return place > 0, place < size - 1


def layers_kernel(own_ref, partner_ref, out_ref):
    start = lax.axis_index("gz") * (own_ref.shape[0] - 2)
    for half, ref in enumerate((partner_ref, own_ref)):
        for layer in range(2):
            out_ref[half, layer] = ref[start + layer]


def x_layers(core, own_ref, partner_ref, direct_ref, passed_ref):
    has_low, has_high = edges("gx")
    length = own_ref.shape[0]

    def at(layer):
        if 2 <= layer < length + 2:
            return own_ref[layer - 2], partner_ref[layer - 2]
        slot = layer if layer < 2 else layer - length - 2
        direct = [direct_ref[h, slot] for h in range(2)]
        passed = [passed_ref[h, slot] for h in range(2)]
        low, high = both_sides(core, direct, passed)
        side, valid = (low, has_low) if layer < 2 else (high, has_high)
        return [jnp.where(valid, v, jnp.zeros_like(v)) for v in side]

    return at


def rows_kernel(own_ref, partner_ref, direct_ref, passed_ref, out_ref):
    core = lax.axis_index("gz")
    length, rows, _ = own_ref.shape
    at = x_layers(core, own_ref, partner_ref, direct_ref, passed_ref)
    for layer in range(length + 4):
        own, partner = at(layer)
        for half, value in enumerate((partner, own)):
            row = layer * 4 + half * 2
            out_ref[row // 8, row % 8 : row % 8 + 2, :] = jnp.where(
                core == 0, value[0:2], value[rows - 2 : rows]
            )


def solve_kernel(
    own_ref, partner_ref, xd_ref, xp_ref, yd_ref, yp_ref, cx, cy, rate, mz, out_ref, grid, spectral
):
    core = lax.axis_index("gz")
    length, rows, width = own_ref.shape
    ext, padded, lanes = rate.shape
    has_low, has_high = edges("gy")
    at = x_layers(core, own_ref, partner_ref, xd_ref, xp_ref)
    nothing = jnp.zeros((padded - rows - 4, width), f32)
    for layer in range(length + 4):
        place, row = divmod(layer * 4, 8)
        direct = [yd_ref[place, row + 2 * h : row + 2 * h + 2, :] for h in range(2)]
        passed = [yp_ref[place, row + 2 * h : row + 2 * h + 2, :] for h in range(2)]
        low, high = both_sides(core, direct, passed)
        for half, value in enumerate(at(layer)):
            before = jnp.where(has_low, low[half], jnp.zeros_like(low[half]))
            after = jnp.where(has_high, high[half], jnp.zeros_like(high[half]))
            at_lanes = slice(half * width, (half + 1) * width)
            grid[layer, 0:rows, at_lanes] = value
            grid[layer, rows:padded, at_lanes] = jnp.concatenate([before, after, nothing], axis=0)

    high, low = split2(grid[...].reshape((length + 4) * padded, 2 * width))
    along_z = dot(high, mz[0]) + (dot(low, mz[0]) + dot(high, mz[1]))
    along_z = along_z.reshape(length + 4, padded, lanes)
    block = [along_z[0], along_z[1] + along_z[2]]
    block += [along_z[k] for k in range(3, length + 1)]
    block += [along_z[length + 1] + along_z[length + 2], along_z[length + 3]]

    places = [(rows,), (rows + 1, 0)] + [(k,) for k in range(1, rows - 1)]
    places += [(rows - 1, rows + 2), (rows + 3,)]
    for p in range(ext):
        value = sum(cx[a * ext + p : a * ext + p + 1, :] * block[a] for a in range(ext))
        total = None
        for b in range(ext):
            row = sum(value[k : k + 1] for k in places[b])
            term = cy[0, b] * row
            total = term if total is None else total + term
        total = total * rate[p]
        spectral[p] = sum(cy[1, q] * total[q : q + 1] for q in range(ext))
    back = []
    for a in range(ext):
        back.append(sum(cx[a * ext + p : a * ext + p + 1, :] * spectral[p] for p in range(ext)))
    high, low = split2(jnp.concatenate(back, axis=0))
    result = dot(high, mz[0], True) + (dot(low, mz[0], True) + dot(high, mz[1], True))
    out_ref[...] = result.reshape(out_ref.shape)


def totals(layer, mine_ref, other_ref, width, rows=slice(None)):
    own = mine_ref[layer, rows, 0:width] + other_ref[layer, rows, width:]
    partner = mine_ref[layer, rows, width:] + other_ref[layer, rows, 0:width]
    return own, partner


def return_layers_kernel(mine_ref, other_ref, out_ref):
    ext, padded, width = mine_ref.shape
    nodes, width = ext - 2, width // 2
    start = lax.axis_index("gz") * nodes
    for layer in range(2):
        own, partner = totals(start + layer, mine_ref, other_ref, width)
        for half, value in enumerate((partner, own)):
            place = half * 2 + layer
            out_ref[place] = value[0:nodes]
            out_ref[4, 2 * place : 2 * place + 2, :] = value[nodes : nodes + 2]


def interior_kernel(mine_ref, other_ref, after_ref, out_ref):
    ext, padded, width = mine_ref.shape
    for layer in range(1, ext - 1):
        own, partner = totals(layer, mine_ref, other_ref, width // 2)
        out_ref[0, layer - 1] = own
        out_ref[1, layer - 1] = partner


def return_rows_kernel(initial_ref, inner_ref, direct_ref, passed_ref, out_ref, base_ref):
    core = lax.axis_index("gz")
    has_low, has_high = edges("gx")
    nodes, rows, _ = initial_ref.shape
    for layer in range(nodes):
        values = [inner_ref[h, layer] for h in range(2)]
        outer = [values[h][rows : rows + 2] for h in range(2)]
        values = [values[h][0:rows] for h in range(2)]
        if layer < 2 or layer >= nodes - 2:
            slot = layer if layer < 2 else layer - (nodes - 2)

            def parts(ref, h, slot=slot):
                place = 2 * h + slot
                return ref[place], ref[4, 2 * place : 2 * place + 2, :]

            direct = [parts(direct_ref, h) for h in range(2)]
            passed = [parts(passed_ref, h) for h in range(2)]
            side = 0 if layer < 2 else 1
            valid = (has_low, has_high)[side]
            for k, target in enumerate((values, outer)):
                both = both_sides(core, [d[k] for d in direct], [d[k] for d in passed])[side]
                for h in range(2):
                    target[h] = target[h] + jnp.where(valid, both[h], jnp.zeros_like(both[h]))
        base_ref[layer] = initial_ref[layer] + values[0]
        for place, h in enumerate((1, 0)):
            row = layer * 4 + place * 2
            first = jnp.where(core == 0, outer[h][0:1], values[h][rows - 1 : rows])
            second = jnp.where(core == 0, values[h][0:1], outer[h][1:2])
            out_ref[row // 8, row % 8 : row % 8 + 1, :] = first
            out_ref[row // 8, row % 8 + 1 : row % 8 + 2, :] = second


def result_kernel(base_ref, direct_ref, passed_ref, out_ref):
    core = lax.axis_index("gz")
    has_low, has_high = edges("gy")
    nodes, rows, _ = base_ref.shape
    for layer in range(nodes):
        place, row = divmod(layer * 4, 8)
        direct = direct_ref[place, row : row + 2, :]
        passed = passed_ref[place, row + 2 : row + 4, :]
        low = jnp.where(core == 0, direct, passed)
        high = jnp.where(core == 0, passed, direct)
        low = jnp.where(has_low, low, jnp.zeros_like(low))
        high = jnp.where(has_high, high, jnp.zeros_like(high))
        between = jnp.zeros((rows - 4, low.shape[1]), f32)
        out_ref[layer] = base_ref[layer] + jnp.concatenate([low, between, high], axis=0)


def swap_pairs(axis):
    sizes = [lax.axis_size(name) for name in AXES]
    along, across = (0, 1) if axis == "gx" else (1, 0)

    def number(place, other, core):
        spot = (place, other) if along == 0 else (other, place)
        return (spot[0] * sizes[1] + spot[1]) * 2 + core

    pairs = []
    for other in range(sizes[across]):
        for place in range(sizes[along] - 1):
            here, there = number(place, other, 1), number(place + 1, other, 0)
            pairs += [(here, there), (there, here)]
        if other ^ 1 < sizes[across]:
            for place, core in ((0, 0), (sizes[along] - 1, 1)):
                pairs.append((number(place, other, core), number(place, other ^ 1, core)))
    return pairs


def swap(value, axis):
    if axis == "gz":
        return lax.ppermute(value, "gz", [(0, 1), (1, 0)])
    return lax.ppermute(value, AXES, swap_pairs(axis))


def paired_body(initial, source, metric, eigenvectors, eigenvalues):
    nodes, rows, width = initial.shape
    ext = eigenvectors.shape[1]
    blocks = width // nodes
    lanes = blocks * ext
    padded = 2 * rows

    inputs = [initial, source, metric, *operator_tables(rows, width)]
    inputs = [pltpu.with_memory_space_constraint(value, pltpu.HBM) for value in inputs]
    own = call(
        residual_kernel,
        [shaped(initial.shape)],
        inputs,
        scratch=[
            *(pltpu.VMEM(value.shape, value.dtype) for value in inputs),
            pltpu.SemaphoreType.DMA((len(inputs),)),
        ],
        where=HBM,
    )[0]
    vectors = eigenvectors.reshape(3 * ext * ext, 1, blocks)
    values = eigenvalues.reshape(3 * ext, 1, blocks)
    cx, cy, rate, mz = call(
        coefficients_kernel,
        [
            shaped((ext * ext, lanes)),
            shaped((2, ext, padded, lanes)),
            shaped((ext, padded, lanes)),
            shaped((2, 2 * width, lanes), bf16),
        ],
        [vectors, values, *spread_tables(blocks, ext), own],
    )
    partner = swap(own, "gz")
    sent = call(layers_kernel, [shaped((2, 2, rows, width))], [own, partner])[0]
    x_direct = swap(sent, "gx")
    x_passed = swap(x_direct, "gz")
    sent = call(
        rows_kernel,
        [shaped(((nodes + 4) * 4 // 8, 8, width))],
        [own, partner, x_direct, x_passed],
    )[0]
    y_direct = swap(sent, "gy")
    y_passed = swap(y_direct, "gz")
    mine = call(
        solve_kernel,
        [shaped((ext, padded, 2 * width))],
        [own, partner, x_direct, x_passed, y_direct, y_passed, cx, cy, rate, mz],
        scratch=[
            pltpu.VMEM((nodes + 4, padded, 2 * width), f32),
            pltpu.VMEM((ext, padded, lanes), f32),
        ],
    )[0]

    other = swap(mine, "gz")
    sent = call(return_layers_kernel, [shaped((5, rows, width))], [mine, other])[0]
    inner = call(interior_kernel, [shaped((2, nodes, padded, width))], [mine, other, sent])[0]
    x_direct = swap(sent, "gx")
    x_passed = swap(x_direct, "gz")
    sent, base = call(
        return_rows_kernel,
        [shaped((nodes * 4 // 8, 8, width)), shaped(initial.shape)],
        [initial, inner, x_direct, x_passed],
    )
    y_direct = swap(sent, "gy")
    y_passed = swap(y_direct, "gz")
    return call(result_kernel, [shaped(initial.shape)], [base, y_direct, y_passed])[0]


def body(initial, source, metric, eigenvectors, eigenvalues):
    nodes = gll_points.shape[0]
    one_element = initial.shape[0] == nodes and initial.shape[1] == nodes
    if lax.axis_size("gz") == 2 and one_element and initial.shape[2] % 128 == 0:
        return paired_body(initial, source, metric, eigenvectors, eigenvalues)
    return general_body(initial, source, metric, eigenvectors, eigenvalues)


def solution(mesh):
    placed = (
        P("gx", "gy", "gz"),
        P("gx", "gy", "gz"),
        P(None, "gx", "gy", "gz"),
        P(None, None, None, "gx", "gy", "gz"),
        P(None, None, "gx", "gy", "gz"),
    )
    return jax.shard_map(
        body, mesh=mesh, in_specs=placed, out_specs=P("gx", "gy", "gz"), check_vma=False
    )
```

```python
import functools

import jax
import jax.numpy as jnp
import numpy as np
from jax import lax
from jax.experimental import pallas as pl
from jax.experimental.pallas import tpu as pltpu
from jax.sharding import PartitionSpec as P

gll_points = np.array(
    [
        -1.0,
        -0.8717401485096066,
        -0.5917001814331423,
        -0.2092992179024789,
        0.2092992179024789,
        0.5917001814331423,
        0.8717401485096066,
        1.0,
    ]
)


def extended_2(value, sides, width):
    for axis, dim in sides:
        size, length = (lax.axis_size(axis), value.shape[dim])
        up = [(i, (i + 1) % size) for i in range(size - 1)]
        down = [(j, i) for i, j in up]
        last = lax.slice_in_dim(value, length - width, length, axis=dim)
        first = lax.slice_in_dim(value, 0, width, axis=dim)
        before = lax.ppermute(last, axis, up)
        after = lax.ppermute(first, axis, down)
        value = jnp.concatenate([before, value, after], axis=dim)
    return value


def derivative_table():
    number = gll_points.shape[0]
    products = np.array(
        [
            np.prod(
                [
                    gll_points[row_index] - gll_points[other]
                    for other in range(number)
                    if other != row_index
                ]
            )
            for row_index in range(number)
        ]
    )
    matrix_out = np.zeros((number, number))
    for row_index in range(number):
        for col_index in range(number):
            if row_index != col_index:
                matrix_out[row_index, col_index] = (
                    products[row_index]
                    / products[col_index]
                    / (gll_points[row_index] - gll_points[col_index])
                )
        matrix_out[row_index, row_index] = -np.sum(matrix_out[row_index])
    return matrix_out


def apply_along(values, matrix, direction):
    block_size = matrix.shape[1]
    old_shape = values.shape
    pieces_shape = (
        old_shape[:direction]
        + (old_shape[direction] // block_size, block_size)
        + old_shape[direction + 1 :]
    )
    result = jnp.tensordot(
        values.reshape(pieces_shape),
        matrix,
        axes=((direction + 1,), (1,)),
        precision=lax.Precision.HIGHEST,
    )
    result = jnp.moveaxis(result, -1, direction + 1)
    return result.reshape(
        old_shape[:direction]
        + (old_shape[direction] // block_size * matrix.shape[0],)
        + old_shape[direction + 1 :]
    )


def apply_operator(values, metric):
    deriv_table = jnp.asarray(derivative_table(), jnp.float32)
    summed = jnp.zeros_like(values)
    for direction in range(3):
        gradient = apply_along(values, deriv_table, direction)
        summed = summed + apply_along(metric[direction] * gradient, deriv_table.T, direction)
    return summed


def assemble(padded, offset):
    result = padded
    for direction in range(3):
        length = result.shape[direction]
        view_shape = [1, 1, 1]
        view_shape[direction] = length
        node_index = ((jnp.arange(length) - offset) % 8).reshape(view_shape)
        edge_zero = jnp.zeros_like(lax.slice_in_dim(result, 0, 1, axis=direction))
        upward = jnp.concatenate(
            [lax.slice_in_dim(result, 1, length, axis=direction), edge_zero], axis=direction
        )
        downward = jnp.concatenate(
            [edge_zero, lax.slice_in_dim(result, 0, length - 1, axis=direction)], axis=direction
        )
        result = (
            result
            + jnp.where(node_index == 7, upward, 0.0)
            + jnp.where(node_index == 0, downward, 0.0)
        )
    return result


def extend_axis(padded, direction):
    shifted = jnp.moveaxis(padded, direction, 0)
    blocks = (shifted.shape[0] - 4) // 8
    trailing = shifted.shape[1:]
    middle = shifted[2:-2].reshape((blocks, 8) + trailing)
    lowest = shifted[0 : 8 * blocks : 8][:, None]
    beyond = shifted[11::8][:, None]
    joined = jnp.concatenate([lowest, middle, beyond], axis=1).reshape((blocks * 10,) + trailing)
    return jnp.moveaxis(joined, 0, direction)


def widen(padded):
    return extend_axis(extend_axis(extend_axis(padded, 0), 1), 2)


def fast_solve(extended, eigenvectors, eigenvalues):
    count_x, count_y, count_z = eigenvectors.shape[3:]
    precise = lax.Precision.HIGHEST
    spectral = extended.reshape(count_x, 10, count_y, 10, count_z, 10)
    spectral = jnp.einsum("apxyz,xaybzc->xpybzc", eigenvectors[0], spectral, precision=precise)
    spectral = jnp.einsum("bqxyz,xpybzc->xpyqzc", eigenvectors[1], spectral, precision=precise)
    spectral = jnp.einsum("csxyz,xpyqzc->xpyqzs", eigenvectors[2], spectral, precision=precise)
    rate_x = jnp.transpose(eigenvalues[0], (1, 0, 2, 3))[:, :, :, None, :, None]
    rate_y = jnp.transpose(eigenvalues[1], (1, 2, 0, 3))[:, None, :, :, :, None]
    rate_z = jnp.transpose(eigenvalues[2], (1, 2, 3, 0))[:, None, :, None, :, :]
    spectral = spectral / (rate_x + rate_y + rate_z)
    spectral = jnp.einsum("csxyz,xpyqzs->xpyqzc", eigenvectors[2], spectral, precision=precise)
    spectral = jnp.einsum("bqxyz,xpyqzc->xpybzc", eigenvectors[1], spectral, precision=precise)
    spectral = jnp.einsum("apxyz,xpybzc->xaybzc", eigenvectors[0], spectral, precision=precise)
    return spectral.reshape(count_x * 10, count_y * 10, count_z * 10)


def return_axis(padded, direction):
    shifted = jnp.moveaxis(padded, direction, 0)
    blocks = (shifted.shape[0] - 4) // 10
    trailing = shifted.shape[1:]
    owned = shifted[2:-2].reshape((blocks, 10) + trailing)[:, 1:9]
    before = shifted[0 : 10 * blocks].reshape((blocks, 10) + trailing)[:, 0:2]
    following = shifted[4:].reshape((blocks, 10) + trailing)[:, 8:10]
    middle = jnp.zeros((blocks, 4) + trailing, shifted.dtype)
    summed = owned + jnp.concatenate([before, middle, following], axis=1)
    return jnp.moveaxis(summed.reshape((blocks * 8,) + trailing), 0, direction)


def general_body(initial, source, metric, eigenvectors, eigenvalues):
    solution = initial
    local_res = source - apply_operator(solution, metric)
    deeper = extended_2(local_res, (("gx", 0), ("gy", 1), ("gz", 2)), 2)
    widened = assemble(deeper, 2)
    extended = widen(widened)
    corrected = fast_solve(extended, eigenvectors, eigenvalues)
    padded = extended_2(corrected, (("gx", 0), ("gy", 1), ("gz", 2)), 2)
    correction = return_axis(return_axis(return_axis(padded, 0), 1), 2)
    solution = solution + correction
    return solution


AXES = ("gx", "gy", "gz")
VMEM = pl.BlockSpec(memory_space=pltpu.VMEM)
HBM = pl.BlockSpec(memory_space=pltpu.HBM)
VMEM_LIMIT = 16 * 2**20
f32 = jnp.float32
bf16 = jnp.bfloat16


def call(kernel, outs, args, scratch=(), where=VMEM):
    moved = sum(int(np.prod(a.shape)) * a.dtype.itemsize for a in (*args, *outs))
    return pl.pallas_call(
        kernel,
        out_shape=outs,
        in_specs=[where] * len(args),
        out_specs=[VMEM] * len(outs),
        scratch_shapes=scratch,
        compiler_params=pltpu.CompilerParams(vmem_limit_bytes=VMEM_LIMIT),
        cost_estimate=pl.CostEstimate(flops=0, bytes_accessed=moved, transcendentals=0),
    )(*args)


def shaped(shape, dtype=f32):
    return jax.ShapeDtypeStruct(shape, dtype)


def counted(shape, axis):
    return lax.broadcasted_iota(jnp.int32, shape, axis)


def split2(value):
    high = value.astype(bf16)
    return high, (value - high.astype(f32)).astype(bf16)


def split3(value):
    high = value.astype(bf16)
    rest = value - high.astype(f32)
    middle = rest.astype(bf16)
    return high, middle, (rest - middle.astype(f32)).astype(bf16)


def dot(left, right, transposed=False):
    dims = (((1,), (1 if transposed else 0,)), ((), ()))
    return lax.dot_general(left, right, dims, preferred_element_type=f32)


def repeated_table(table, width):
    nodes = table.shape[0]
    row, column = counted((nodes, width), 0), counted((nodes, width), 1) % nodes
    tile = jnp.zeros((nodes, width), f32)
    for j in range(nodes):
        values = jnp.zeros((nodes, width), f32)
        for i in range(nodes):
            values = jnp.where(row == i, float(table[i, j]), values)
        tile = jnp.where(column == j, values, tile)
    return tile


def residual_kernel(u_hbm, source_hbm, metric_hbm, out_ref, u_ref, source_ref, metric_ref, sems):
    copies = [pltpu.make_async_copy(u_hbm, u_ref, sems.at[0])]
    copies += [
        pltpu.make_async_copy(metric_hbm.at[d], metric_ref.at[d], sems.at[1 + d])
        for d in range(metric_hbm.shape[0])
    ]
    copies.append(pltpu.make_async_copy(source_hbm, source_ref, sems.at[len(copies)]))
    for copy in copies:
        copy.start()
    nodes, rows, width = u_ref.shape
    flat_rows = nodes * rows
    table = np.asarray(derivative_table(), np.float32)
    along_y, along_z = [], []
    for t in range(2):
        tile = repeated_table(table if t == 0 else table.T, width)
        high = tile.astype(bf16).astype(f32)
        low = tile - high
        group = counted((nodes, width), 1) // nodes
        zero = jnp.zeros_like(tile)
        for part in (high, low):
            bands = [jnp.where(group == k, part, zero) for k in range(width // nodes)]
            along_z.append(jnp.concatenate(bands, axis=0).astype(bf16))
        group = group[:, 0 : 2 * flat_rows]
        high, low, zero = (v[:, 0 : 2 * flat_rows] for v in (high, low, zero))
        bands = [jnp.where(group % rows == k, high, zero) for k in range(nodes)]
        bands += [jnp.where(group == k, low, zero) for k in range(nodes)]
        along_y.append(jnp.concatenate(bands, axis=0).astype(bf16))

    def by_y(value, t):
        both = dot(along_y[t], jnp.concatenate(split2(value), axis=0))
        return both[0:flat_rows] + both[flat_rows:]

    def by_z(value, t):
        high, low = split2(value)
        both = dot(jnp.concatenate([high, low], axis=0), along_z[2 * t])
        return both[0:flat_rows] + (both[flat_rows:] + dot(high, along_z[2 * t + 1]))

    copies[0].wait()
    flat = u_ref[...].reshape(flat_rows, width)
    flux_y, flux_z = by_y(flat, 0), by_z(flat, 1)
    layers = [u_ref[j] for j in range(nodes)]
    flux_x = [sum(float(table[i, j]) * layers[j] for j in range(nodes)) for i in range(nodes)]
    for copy in copies[1:]:
        copy.wait()
    total = by_y(flux_y * metric_ref[1].reshape(flat.shape), 1)
    total = total + by_z(flux_z * metric_ref[2].reshape(flat.shape), 0)
    total = total.reshape(nodes, rows, width)
    flux_x = [metric_ref[0, i] * flux_x[i] for i in range(nodes)]
    for j in range(nodes):
        applied = sum(float(table[i, j]) * flux_x[i] for i in range(nodes))
        out_ref[j] = source_ref[j] - (applied + total[j])


def layers_kernel(own_ref, partner_ref, out_ref):
    start = lax.axis_index("gz") * (own_ref.shape[0] - 2)
    for half, ref in enumerate((partner_ref, own_ref)):
        for layer in range(2):
            out_ref[half, layer] = ref[start + layer]


def spread(own_ref, partner_ref, first, count, ext):
    blocks = own_ref.shape[2]
    parts = []
    for ref in (own_ref, partner_ref):
        parts += split3(ref[first : first + count].reshape(count, blocks))
    shape = (blocks, 2 * blocks * ext)
    repeat = []
    for half in range(2):
        element = counted(shape, 1) // ext - half * blocks
        repeat += [(element == counted(shape, 0)).astype(f32).astype(bf16)] * 3
    return dot(jnp.concatenate(parts, axis=1), jnp.concatenate(repeat, axis=0))


def gathered(choice, value):
    choice = choice.astype(f32).astype(bf16)
    high, middle, low = split3(value)
    return dot(choice, high) + (dot(choice, middle) + dot(choice, low))


def xy_coefficients_kernel(own_ref, partner_ref, after_ref, cx_ref, cy_ref):
    square = cx_ref.shape[0]
    ext, padded = cy_ref.shape[1:3]
    cx_ref[...] = spread(own_ref, partner_ref, 0, square, ext)
    along_y = spread(own_ref, partner_ref, square, square, ext)
    shape = (ext * padded, square)
    first, second, entry = counted(shape, 0) // padded, counted(shape, 0) % padded, counted(shape, 1)
    forward = (second < ext) & (entry == first * ext + second)
    position = jnp.where(second < ext - 2, second + 1, jnp.where(second == ext - 2, 0, ext - 1))
    backward = (second < ext) & (entry == position * ext + first)
    for k, choice in enumerate((forward, backward)):
        cy_ref[k] = gathered(choice, along_y).reshape(cy_ref.shape[1:])


def z_coefficients_kernel(
    own_vec, partner_vec, own_val, partner_val, after_ref, rate_ref, mz_ref
):
    ext, padded, lanes = rate_ref.shape
    square = ext * ext
    half = lanes // 2
    blocks = half // ext
    nodes = ext - 2
    core = lax.axis_index("gz")
    shape = (square, lanes)
    same = counted(shape, 0) % ext == counted(shape, 1) % ext
    along_z = spread(own_vec, partner_vec, 2 * square, square, ext)
    along_z = jnp.where(same, along_z, jnp.zeros_like(along_z))
    shape = (ext, square)
    along_z = gathered(counted(shape, 1) // ext == counted(shape, 0), along_z)

    rates = spread(own_val, partner_val, 0, 3 * ext, ext)
    rate_z = rates[2 * ext : 3 * ext]
    rate_z = jnp.where(same[0:ext], rate_z, jnp.zeros_like(rate_z))
    rate_z = jnp.sum(rate_z, axis=0, keepdims=True)
    rate_y = jnp.concatenate([rates[ext : 2 * ext], jnp.ones((padded - ext, lanes), f32)], axis=0)
    for p in range(ext):
        rate_ref[p] = 1.0 / (rates[p : p + 1] + rate_y + rate_z)

    zeros = jnp.zeros((nodes - 2, lanes), f32)
    own = along_z[1 : nodes + 1]
    below = jnp.concatenate([zeros, along_z[0:2]], axis=0)
    above = jnp.concatenate([along_z[nodes : nodes + 2], zeros], axis=0)
    lane = lax.broadcasted_iota(jnp.int32, (nodes, lanes), 1)
    first_own = core * blocks
    first_partner = blocks - first_own
    element = jnp.where(
        lane < half, lane // ext + first_own, (lane - half) // ext + first_partner
    )
    zero = jnp.zeros_like(own)
    for place in range(0, 2 * blocks, 2):
        first = place + first_own if place < blocks else place - blocks + first_partner
        pair = []
        for block in (first, first + 1):
            value = jnp.where(element == block, own, zero)
            value = value + jnp.where(element == block + 1, below, zero)
            pair.append(value + jnp.where(element == block - 1, above, zero))
        high, low = split2(jnp.concatenate(pair, axis=0))
        mz_ref[0, place * nodes : (place + 2) * nodes, :] = high
        mz_ref[1, place * nodes : (place + 2) * nodes, :] = low


def both_sides(core, direct, passed):
    low = [jnp.where(core == 0, direct[h], passed[1 - h]) for h in range(2)]
    high = [jnp.where(core == 0, passed[1 - h], direct[h]) for h in range(2)]
    return low, high


def edges(axis):
    place, size = lax.axis_index(axis), lax.axis_size(axis)
    return place > 0, place < size - 1


def x_layers(core, own_ref, partner_ref, direct_ref, passed_ref):
    has_low, has_high = edges("gx")
    length = own_ref.shape[0]

    def at(layer):
        if 2 <= layer < length + 2:
            return own_ref[layer - 2], partner_ref[layer - 2]
        slot = layer if layer < 2 else layer - length - 2
        direct = [direct_ref[h, slot] for h in range(2)]
        passed = [passed_ref[h, slot] for h in range(2)]
        low, high = both_sides(core, direct, passed)
        side, valid = (low, has_low) if layer < 2 else (high, has_high)
        return [jnp.where(valid, v, jnp.zeros_like(v)) for v in side]

    return at


def rows_kernel(own_ref, partner_ref, direct_ref, passed_ref, after_x, after_z, out_ref):
    core = lax.axis_index("gz")
    length, rows, width = own_ref.shape
    at = x_layers(core, own_ref, partner_ref, direct_ref, passed_ref)
    for layer in range(length + 4):
        own, partner = at(layer)
        for half, value in enumerate((partner, own)):
            out_ref[layer, :, half * width : (half + 1) * width] = jnp.where(
                core == 0, value[0:2], value[rows - 2 : rows]
            )


def by_z(value, mz):
    high, low = split2(value)
    return dot(high, mz[0]) + (dot(low, mz[0]) + dot(high, mz[1]))


def back_by_z(value, mz):
    high, low = split2(value)
    return dot(high, mz[0], True) + (dot(low, mz[0], True) + dot(high, mz[1], True))


def by_x(along_z, cx, ext):
    last = along_z.shape[0] - 1
    block = [along_z[0], along_z[1] + along_z[2]]
    block += [along_z[k] for k in range(3, last - 2)]
    block += [along_z[last - 2] + along_z[last - 1], along_z[last]]
    for p in range(ext):
        yield sum(cx[a * ext + p : a * ext + p + 1, :] * block[a] for a in range(ext))


def interior_solve_kernel(
    own_ref, partner_ref, xd_ref, xp_ref, after_ref, cx, cy, mz, out_ref, grid
):
    core = lax.axis_index("gz")
    length, rows, width = own_ref.shape
    ext = out_ref.shape[0]
    at = x_layers(core, own_ref, partner_ref, xd_ref, xp_ref)
    for layer in range(length + 4):
        for half, value in enumerate(at(layer)):
            grid[layer, :, half * width : (half + 1) * width] = value
    along_z = by_z(grid[...].reshape((length + 4) * rows, 2 * width), mz)
    along_z = along_z.reshape(length + 4, rows, along_z.shape[1])
    for p, value in enumerate(by_x(along_z, cx, ext)):
        out_ref[p] = sum(cy[0, b + 1] * value[b : b + 1] for b in range(rows))


def solve_kernel(yd_ref, yp_ref, part_ref, cx, cy, rate, mz, spectral, sent_ref, grid):
    core = lax.axis_index("gz")
    length, _, both = yd_ref.shape
    width = both // 2
    ext, padded, lanes = rate.shape
    nodes = ext - 2
    has_low, has_high = edges("gy")
    use_direct = jnp.where(core == 0, has_low, has_high)
    use_passed = jnp.where(core == 0, has_high, has_low)
    nothing = jnp.zeros((nodes - 4, both), f32)
    for layer in range(length):
        direct = yd_ref[layer]
        passed = jnp.concatenate([yp_ref[layer, :, width:], yp_ref[layer, :, 0:width]], axis=1)
        direct = jnp.where(use_direct, direct, jnp.zeros_like(direct))
        passed = jnp.where(use_passed, passed, jnp.zeros_like(passed))
        grid[layer] = jnp.concatenate([direct, passed, nothing], axis=0)
    along_z = by_z(grid[...].reshape(length * nodes, both), mz)
    along_z = along_z.reshape(length, nodes, lanes)
    places = [core * nodes, core * nodes + 1, (1 - core) * nodes, (1 - core) * nodes + 1]
    coefficients = [cy[0, place] for place in places]
    for p, value in enumerate(by_x(along_z, cx, ext)):
        total = part_ref[p] + sum(coefficients[k] * value[k : k + 1] for k in range(4))
        total = total * rate[p]
        spectral[p] = sum(cy[1, q] * total[q : q + 1] for q in range(ext))
    layers = []
    for layer in range(2):
        value = None
        for p in range(ext):
            row = layer * ext + p
            coefficient = jnp.where(
                core == 0, cx[row : row + 1, :], cx[row + nodes * ext : row + nodes * ext + 1, :]
            )
            term = coefficient * spectral[p]
            value = term if value is None else value + term
        layers.append(value)
    result = back_by_z(jnp.concatenate(layers, axis=0), mz)
    for layer in range(2):
        for half in range(2):
            lanes_at = slice((1 - half) * width, (2 - half) * width)
            place = half * 2 + layer
            value = result[layer * padded : layer * padded + nodes + 2, lanes_at]
            sent_ref[place] = value[0:nodes]
            sent_ref[4, 2 * place : 2 * place + 2, :] = value[nodes : nodes + 2]


def interior_kernel(spectral, cx, mz, after_ref, out_ref):
    ext, padded, lanes = spectral.shape
    nodes, _, both = out_ref.shape
    layers = []
    for a in range(1, ext - 1):
        layers.append(
            sum(cx[a * ext + p : a * ext + p + 1, :] * spectral[p] for p in range(ext))
        )
    result = back_by_z(jnp.concatenate(layers, axis=0), mz)
    out_ref[...] = result.reshape(nodes, padded, both)


def return_rows_kernel(initial_ref, inner_ref, direct_ref, passed_ref, out_ref, base_ref):
    core = lax.axis_index("gz")
    has_low, has_high = edges("gx")
    nodes, rows, width = initial_ref.shape
    for layer in range(nodes):
        lanes = [slice(0, width), slice(width, 2 * width)]
        outer = [inner_ref[layer, rows : rows + 2, lanes[h]] for h in range(2)]
        values = [inner_ref[layer, 0:rows, lanes[h]] for h in range(2)]
        if layer < 2 or layer >= nodes - 2:
            slot = layer if layer < 2 else layer - (nodes - 2)

            def parts(ref, h, slot=slot):
                place = 2 * h + slot
                return ref[place], ref[4, 2 * place : 2 * place + 2, :]

            direct = [parts(direct_ref, h) for h in range(2)]
            passed = [parts(passed_ref, h) for h in range(2)]
            side = 0 if layer < 2 else 1
            valid = (has_low, has_high)[side]
            for k, target in enumerate((values, outer)):
                both = both_sides(core, [d[k] for d in direct], [d[k] for d in passed])[side]
                for h in range(2):
                    target[h] = target[h] + jnp.where(valid, both[h], jnp.zeros_like(both[h]))
        base_ref[layer] = initial_ref[layer] + values[0]
        for place, h in enumerate((1, 0)):
            first = jnp.where(core == 0, outer[h][0:1], values[h][rows - 1 : rows])
            second = jnp.where(core == 0, values[h][0:1], outer[h][1:2])
            out_ref[layer, :, lanes[place]] = jnp.concatenate([first, second], axis=0)


def result_kernel(base_ref, direct_ref, passed_ref, out_ref):
    core = lax.axis_index("gz")
    has_low, has_high = edges("gy")
    nodes, rows, width = base_ref.shape
    for layer in range(nodes):
        direct = direct_ref[layer, :, 0:width]
        passed = passed_ref[layer, :, width:]
        low = jnp.where(core == 0, direct, passed)
        high = jnp.where(core == 0, passed, direct)
        low = jnp.where(has_low, low, jnp.zeros_like(low))
        high = jnp.where(has_high, high, jnp.zeros_like(high))
        between = jnp.zeros((rows - 4, low.shape[1]), f32)
        out_ref[layer] = base_ref[layer] + jnp.concatenate([low, between, high], axis=0)


def swap_pairs(axis):
    sizes = [lax.axis_size(name) for name in AXES]
    along, across = (0, 1) if axis == "gx" else (1, 0)

    def number(place, other, core):
        spot = (place, other) if along == 0 else (other, place)
        return (spot[0] * sizes[1] + spot[1]) * 2 + core

    pairs = []
    for other in range(sizes[across]):
        for place in range(sizes[along] - 1):
            here, there = number(place, other, 1), number(place + 1, other, 0)
            pairs += [(here, there), (there, here)]
        if other ^ 1 < sizes[across]:
            for place, core in ((0, 0), (sizes[along] - 1, 1)):
                pairs.append((number(place, other, core), number(place, other ^ 1, core)))
    return pairs


def swap(value, axis):
    if axis == "gz":
        return lax.ppermute(value, "gz", [(0, 1), (1, 0)])
    return lax.ppermute(value, AXES, swap_pairs(axis))


def paired_body(initial, source, metric, eigenvectors, eigenvalues):
    nodes, rows, width = initial.shape
    ext = eigenvectors.shape[1]
    blocks = width // nodes
    lanes = 2 * blocks * ext
    padded = 2 * rows
    vectors = eigenvectors.reshape(3 * ext * ext, 1, blocks)
    values = eigenvalues.reshape(3 * ext, 1, blocks)
    inputs = [
        pltpu.with_memory_space_constraint(value, pltpu.HBM)
        for value in (initial, source, metric)
    ]
    own = call(
        residual_kernel,
        [shaped(initial.shape)],
        inputs,
        scratch=[
            *(pltpu.VMEM(value.shape, value.dtype) for value in inputs),
            pltpu.SemaphoreType.DMA((2 + metric.shape[0],)),
        ],
        where=HBM,
    )[0]
    partner = swap(own, "gz")
    partner_vectors = swap(lax.optimization_barrier((vectors, own))[0], "gz")
    sent = call(layers_kernel, [shaped((2, 2, rows, width))], [own, partner])[0]
    x_direct = swap(sent, "gx")
    partner_values = swap(lax.optimization_barrier((values, sent))[0], "gz")
    cx, cy = call(
        xy_coefficients_kernel,
        [shaped((ext * ext, lanes)), shaped((2, ext, padded, lanes))],
        [vectors, partner_vectors, sent],
    )
    x_direct, cx, partner_values = lax.optimization_barrier((x_direct, cx, partner_values))
    x_passed = swap(x_direct, "gz")
    rate, mz = call(
        z_coefficients_kernel,
        [shaped((ext, padded, lanes)), shaped((2, 2 * width, lanes), bf16)],
        [vectors, partner_vectors, values, partner_values, x_direct],
    )
    sent = call(
        rows_kernel,
        [shaped((nodes + 4, 2, 2 * width))],
        [own, partner, x_direct, x_passed, cx, mz],
    )[0]
    y_direct = swap(sent, "gy")
    part = call(
        interior_solve_kernel,
        [shaped((ext, padded, lanes))],
        [own, partner, x_direct, x_passed, sent, cx, cy, mz],
        scratch=[pltpu.VMEM((nodes + 4, rows, 2 * width), f32)],
    )[0]
    y_passed = swap(y_direct, "gz")
    spectral, sent = call(
        solve_kernel,
        [shaped((ext, padded, lanes)), shaped((5, rows, width))],
        [y_direct, y_passed, part, cx, cy, rate, mz],
        scratch=[pltpu.VMEM((nodes + 4, rows, 2 * width), f32)],
    )

    x_direct = swap(sent, "gx")
    inner = call(interior_kernel, [shaped((nodes, padded, 2 * width))], [spectral, cx, mz, sent])[0]
    x_passed = swap(x_direct, "gz")
    sent, base = call(
        return_rows_kernel,
        [shaped((nodes, 2, 2 * width)), shaped(initial.shape)],
        [initial, inner, x_direct, x_passed],
    )
    y_direct = swap(sent, "gy")
    y_passed = swap(y_direct, "gz")
    return call(result_kernel, [shaped(initial.shape)], [base, y_direct, y_passed])[0]


def body(initial, source, metric, eigenvectors, eigenvalues):
    nodes = gll_points.shape[0]
    one_element = initial.shape[0] == nodes and initial.shape[1] == nodes
    if lax.axis_size("gz") == 2 and one_element and initial.shape[2] % 128 == 0:
        return paired_body(initial, source, metric, eigenvectors, eigenvalues)
    return general_body(initial, source, metric, eigenvectors, eigenvalues)


def solution(mesh):
    placed = (
        P("gx", "gy", "gz"),
        P("gx", "gy", "gz"),
        P(None, "gx", "gy", "gz"),
        P(None, None, None, "gx", "gy", "gz"),
        P(None, None, "gx", "gy", "gz"),
    )
    return jax.shard_map(
        body, mesh=mesh, in_specs=placed, out_specs=P("gx", "gy", "gz"), check_vma=False
    )
```

```python
import functools

import jax
import jax.numpy as jnp
import numpy as np
from jax import lax
from jax.experimental import pallas as pl
from jax.experimental.pallas import tpu as pltpu
from jax.sharding import PartitionSpec as P

gll_points = np.array(
    [
        -1.0,
        -0.8717401485096066,
        -0.5917001814331423,
        -0.2092992179024789,
        0.2092992179024789,
        0.5917001814331423,
        0.8717401485096066,
        1.0,
    ]
)


def extended_2(value, sides, width):
    for axis, dim in sides:
        size, length = (lax.axis_size(axis), value.shape[dim])
        up = [(i, (i + 1) % size) for i in range(size - 1)]
        down = [(j, i) for i, j in up]
        last = lax.slice_in_dim(value, length - width, length, axis=dim)
        first = lax.slice_in_dim(value, 0, width, axis=dim)
        before = lax.ppermute(last, axis, up)
        after = lax.ppermute(first, axis, down)
        value = jnp.concatenate([before, value, after], axis=dim)
    return value


def derivative_table():
    number = gll_points.shape[0]
    products = np.array(
        [
            np.prod(
                [
                    gll_points[row_index] - gll_points[other]
                    for other in range(number)
                    if other != row_index
                ]
            )
            for row_index in range(number)
        ]
    )
    matrix_out = np.zeros((number, number))
    for row_index in range(number):
        for col_index in range(number):
            if row_index != col_index:
                matrix_out[row_index, col_index] = (
                    products[row_index]
                    / products[col_index]
                    / (gll_points[row_index] - gll_points[col_index])
                )
        matrix_out[row_index, row_index] = -np.sum(matrix_out[row_index])
    return matrix_out


def apply_along(values, matrix, direction):
    block_size = matrix.shape[1]
    old_shape = values.shape
    pieces_shape = (
        old_shape[:direction]
        + (old_shape[direction] // block_size, block_size)
        + old_shape[direction + 1 :]
    )
    result = jnp.tensordot(
        values.reshape(pieces_shape),
        matrix,
        axes=((direction + 1,), (1,)),
        precision=lax.Precision.HIGHEST,
    )
    result = jnp.moveaxis(result, -1, direction + 1)
    return result.reshape(
        old_shape[:direction]
        + (old_shape[direction] // block_size * matrix.shape[0],)
        + old_shape[direction + 1 :]
    )


def apply_operator(values, metric):
    deriv_table = jnp.asarray(derivative_table(), jnp.float32)
    summed = jnp.zeros_like(values)
    for direction in range(3):
        gradient = apply_along(values, deriv_table, direction)
        summed = summed + apply_along(metric[direction] * gradient, deriv_table.T, direction)
    return summed


def assemble(padded, offset):
    result = padded
    for direction in range(3):
        length = result.shape[direction]
        view_shape = [1, 1, 1]
        view_shape[direction] = length
        node_index = ((jnp.arange(length) - offset) % 8).reshape(view_shape)
        edge_zero = jnp.zeros_like(lax.slice_in_dim(result, 0, 1, axis=direction))
        upward = jnp.concatenate(
            [lax.slice_in_dim(result, 1, length, axis=direction), edge_zero], axis=direction
        )
        downward = jnp.concatenate(
            [edge_zero, lax.slice_in_dim(result, 0, length - 1, axis=direction)], axis=direction
        )
        result = (
            result
            + jnp.where(node_index == 7, upward, 0.0)
            + jnp.where(node_index == 0, downward, 0.0)
        )
    return result


def extend_axis(padded, direction):
    shifted = jnp.moveaxis(padded, direction, 0)
    blocks = (shifted.shape[0] - 4) // 8
    trailing = shifted.shape[1:]
    middle = shifted[2:-2].reshape((blocks, 8) + trailing)
    lowest = shifted[0 : 8 * blocks : 8][:, None]
    beyond = shifted[11::8][:, None]
    joined = jnp.concatenate([lowest, middle, beyond], axis=1).reshape((blocks * 10,) + trailing)
    return jnp.moveaxis(joined, 0, direction)


def widen(padded):
    return extend_axis(extend_axis(extend_axis(padded, 0), 1), 2)


def fast_solve(extended, eigenvectors, eigenvalues):
    count_x, count_y, count_z = eigenvectors.shape[3:]
    precise = lax.Precision.HIGHEST
    spectral = extended.reshape(count_x, 10, count_y, 10, count_z, 10)
    spectral = jnp.einsum("apxyz,xaybzc->xpybzc", eigenvectors[0], spectral, precision=precise)
    spectral = jnp.einsum("bqxyz,xpybzc->xpyqzc", eigenvectors[1], spectral, precision=precise)
    spectral = jnp.einsum("csxyz,xpyqzc->xpyqzs", eigenvectors[2], spectral, precision=precise)
    rate_x = jnp.transpose(eigenvalues[0], (1, 0, 2, 3))[:, :, :, None, :, None]
    rate_y = jnp.transpose(eigenvalues[1], (1, 2, 0, 3))[:, None, :, :, :, None]
    rate_z = jnp.transpose(eigenvalues[2], (1, 2, 3, 0))[:, None, :, None, :, :]
    spectral = spectral / (rate_x + rate_y + rate_z)
    spectral = jnp.einsum("csxyz,xpyqzs->xpyqzc", eigenvectors[2], spectral, precision=precise)
    spectral = jnp.einsum("bqxyz,xpyqzc->xpybzc", eigenvectors[1], spectral, precision=precise)
    spectral = jnp.einsum("apxyz,xpybzc->xaybzc", eigenvectors[0], spectral, precision=precise)
    return spectral.reshape(count_x * 10, count_y * 10, count_z * 10)


def return_axis(padded, direction):
    shifted = jnp.moveaxis(padded, direction, 0)
    blocks = (shifted.shape[0] - 4) // 10
    trailing = shifted.shape[1:]
    owned = shifted[2:-2].reshape((blocks, 10) + trailing)[:, 1:9]
    before = shifted[0 : 10 * blocks].reshape((blocks, 10) + trailing)[:, 0:2]
    following = shifted[4:].reshape((blocks, 10) + trailing)[:, 8:10]
    middle = jnp.zeros((blocks, 4) + trailing, shifted.dtype)
    summed = owned + jnp.concatenate([before, middle, following], axis=1)
    return jnp.moveaxis(summed.reshape((blocks * 8,) + trailing), 0, direction)


def general_body(initial, source, metric, eigenvectors, eigenvalues):
    solution = initial
    local_res = source - apply_operator(solution, metric)
    deeper = extended_2(local_res, (("gx", 0), ("gy", 1), ("gz", 2)), 2)
    widened = assemble(deeper, 2)
    extended = widen(widened)
    corrected = fast_solve(extended, eigenvectors, eigenvalues)
    padded = extended_2(corrected, (("gx", 0), ("gy", 1), ("gz", 2)), 2)
    correction = return_axis(return_axis(return_axis(padded, 0), 1), 2)
    solution = solution + correction
    return solution


AXES = ("gx", "gy", "gz")
VMEM = pl.BlockSpec(memory_space=pltpu.VMEM)
HBM = pl.BlockSpec(memory_space=pltpu.HBM)
VMEM_LIMIT = 16 * 2**20
f32 = jnp.float32
bf16 = jnp.bfloat16


def call(kernel, outs, args, scratch=(), where=VMEM):
    moved = sum(int(np.prod(a.shape)) * a.dtype.itemsize for a in (*args, *outs))
    return pl.pallas_call(
        kernel,
        out_shape=outs,
        in_specs=[where] * len(args),
        out_specs=[VMEM] * len(outs),
        scratch_shapes=scratch,
        compiler_params=pltpu.CompilerParams(vmem_limit_bytes=VMEM_LIMIT),
        cost_estimate=pl.CostEstimate(flops=0, bytes_accessed=moved, transcendentals=0),
    )(*args)


def shaped(shape, dtype=f32):
    return jax.ShapeDtypeStruct(shape, dtype)


def counted(shape, axis):
    return lax.broadcasted_iota(jnp.int32, shape, axis)


def split2(value):
    high = value.astype(bf16)
    return high, (value - high.astype(f32)).astype(bf16)


def split3(value):
    high = value.astype(bf16)
    rest = value - high.astype(f32)
    middle = rest.astype(bf16)
    return high, middle, (rest - middle.astype(f32)).astype(bf16)


def dot(left, right, transposed=False):
    dims = (((1,), (1 if transposed else 0,)), ((), ()))
    return lax.dot_general(left, right, dims, preferred_element_type=f32)


def repeated_table(table, width):
    nodes = table.shape[0]
    row, column = counted((nodes, width), 0), counted((nodes, width), 1) % nodes
    tile = jnp.zeros((nodes, width), f32)
    for j in range(nodes):
        values = jnp.zeros((nodes, width), f32)
        for i in range(nodes):
            values = jnp.where(row == i, float(table[i, j]), values)
        tile = jnp.where(column == j, values, tile)
    return tile


def residual_kernel(
    u_hbm, source_hbm, metric_hbm, val_hbm, out_ref, u_ref, source_ref, metric_ref, val_ref, sems
):
    copies = [pltpu.make_async_copy(u_hbm, u_ref, sems.at[0])]
    copies += [
        pltpu.make_async_copy(metric_hbm.at[d], metric_ref.at[d], sems.at[1 + d])
        for d in range(metric_hbm.shape[0])
    ]
    copies.append(pltpu.make_async_copy(source_hbm, source_ref, sems.at[len(copies)]))
    copies.append(pltpu.make_async_copy(val_hbm, val_ref, sems.at[len(copies)]))
    for copy in copies:
        copy.start()
    nodes, rows, width = u_ref.shape
    flat_rows = nodes * rows
    table = np.asarray(derivative_table(), np.float32)
    along_y, along_z = [], []
    for t in range(2):
        tile = repeated_table(table if t == 0 else table.T, width)
        high = tile.astype(bf16).astype(f32)
        low = tile - high
        group = counted((nodes, width), 1) // nodes
        zero = jnp.zeros_like(tile)
        for part in (high, low):
            bands = [jnp.where(group == k, part, zero) for k in range(width // nodes)]
            along_z.append(jnp.concatenate(bands, axis=0).astype(bf16))
        group = group[:, 0 : 2 * flat_rows]
        high, low, zero = (v[:, 0 : 2 * flat_rows] for v in (high, low, zero))
        bands = [jnp.where(group % rows == k, high, zero) for k in range(nodes)]
        bands += [jnp.where(group == k, low, zero) for k in range(nodes)]
        along_y.append(jnp.concatenate(bands, axis=0).astype(bf16))

    def by_y(value, t):
        both = dot(along_y[t], jnp.concatenate(split2(value), axis=0))
        return both[0:flat_rows] + both[flat_rows:]

    def by_z(value, t):
        high, low = split2(value)
        both = dot(jnp.concatenate([high, low], axis=0), along_z[2 * t])
        return both[0:flat_rows] + (both[flat_rows:] + dot(high, along_z[2 * t + 1]))

    copies[0].wait()
    flat = u_ref[...].reshape(flat_rows, width)
    flux_y, flux_z = by_y(flat, 0), by_z(flat, 1)
    layers = [u_ref[j] for j in range(nodes)]
    flux_x = [sum(float(table[i, j]) * layers[j] for j in range(nodes)) for i in range(nodes)]
    for copy in copies[1:]:
        copy.wait()
    total = by_y(flux_y * metric_ref[1].reshape(flat.shape), 1)
    total = total + by_z(flux_z * metric_ref[2].reshape(flat.shape), 0)
    total = total.reshape(nodes, rows, width)
    flux_x = [metric_ref[0, i] * flux_x[i] for i in range(nodes)]
    for j in range(nodes):
        applied = sum(float(table[i, j]) * flux_x[i] for i in range(nodes))
        out_ref[j] = source_ref[j] - (applied + total[j])
    count, _, blocks = val_ref.shape
    values = val_ref[...].reshape(count, blocks)
    for first in range(0, count, rows):
        last = min(first + rows, count)
        out_ref[nodes + first // rows, 0 : last - first, 0:blocks] = values[first:last]


def layers_kernel(own_ref, partner_ref, out_ref):
    start = lax.axis_index("gz") * (out_ref.shape[2] - 2)
    for half, ref in enumerate((partner_ref, own_ref)):
        for layer in range(2):
            out_ref[half, layer] = ref[start + layer]


def taken(ref, first, count):
    return ref[first : first + count].reshape(count, ref.shape[2])


def spread(own, partner, ext):
    blocks = own.shape[1]
    parts = [*split3(own), *split3(partner)]
    shape = (blocks, 2 * blocks * ext)
    repeat = []
    for half in range(2):
        element = counted(shape, 1) // ext - half * blocks
        repeat += [(element == counted(shape, 0)).astype(f32).astype(bf16)] * 3
    return dot(jnp.concatenate(parts, axis=1), jnp.concatenate(repeat, axis=0))


def gathered(choice, value):
    choice = choice.astype(f32).astype(bf16)
    high, middle, low = split3(value)
    return dot(choice, high) + (dot(choice, middle) + dot(choice, low))


def x_coefficients_kernel(
    own_vec, partner_vec, own_ref, partner_ref, after_ref, cx_ref, cx_rows_ref, rate_ref
):
    ext, padded, lanes = rate_ref.shape
    blocks = own_vec.shape[2]
    nodes = ext - 2
    square = ext * ext
    along_x = spread(taken(own_vec, 0, square), taken(partner_vec, 0, square), ext)
    cx_ref[...] = along_x
    shape = (cx_rows_ref.shape[0], square)
    place = counted(shape, 0) % (shape[0] // ext) // 2
    choice = (place < ext) & (counted(shape, 1) == place * ext + counted(shape, 0) // (shape[0] // ext))
    cx_rows_ref[...] = gathered(choice, along_x)
    rates = []
    for ref in (own_ref, partner_ref):
        tiles = ref[nodes : ref.shape[0]]
        rates.append(tiles.reshape(-1, tiles.shape[2])[0 : 3 * ext, 0:blocks])
    rates = spread(*rates, ext)
    shape = (ext, lanes)
    rate_z = rates[2 * ext : 3 * ext]
    same = counted(shape, 0) == counted(shape, 1) % ext
    rate_z = jnp.sum(jnp.where(same, rate_z, jnp.zeros_like(rate_z)), axis=0, keepdims=True)
    rate_y = jnp.concatenate([rates[ext : 2 * ext], jnp.ones((padded - ext, lanes), f32)], axis=0)
    for p in range(ext):
        rate_ref[p] = 1.0 / (rates[p : p + 1] + rate_y + rate_z)


def y_coefficients_kernel(own_vec, partner_vec, after_ref, cy_ref):
    ext, padded = cy_ref.shape[1:3]
    square = ext * ext
    along_y = spread(taken(own_vec, square, square), taken(partner_vec, square, square), ext)
    shape = (ext * padded, square)
    first, second, entry = counted(shape, 0) // padded, counted(shape, 0) % padded, counted(shape, 1)
    forward = (second < ext) & (entry == first * ext + second)
    position = jnp.where(second < ext - 2, second + 1, jnp.where(second == ext - 2, 0, ext - 1))
    backward = (second < ext) & (entry == position * ext + first)
    for k, choice in enumerate((forward, backward)):
        cy_ref[k] = gathered(choice, along_y).reshape(cy_ref.shape[1:])


def z_coefficients_kernel(own_vec, partner_vec, after_ref, mz_ref):
    blocks = own_vec.shape[2]
    lanes = mz_ref.shape[2]
    half = lanes // 2
    ext = half // blocks
    square = ext * ext
    nodes = ext - 2
    core = lax.axis_index("gz")
    shape = (square, lanes)
    same = counted(shape, 0) % ext == counted(shape, 1) % ext
    along_z = spread(
        taken(own_vec, 2 * square, square), taken(partner_vec, 2 * square, square), ext
    )
    along_z = jnp.where(same, along_z, jnp.zeros_like(along_z))
    shape = (ext, square)
    along_z = gathered(counted(shape, 1) // ext == counted(shape, 0), along_z)

    zeros = jnp.zeros((nodes - 2, lanes), f32)
    own = along_z[1 : nodes + 1]
    below = jnp.concatenate([zeros, along_z[0:2]], axis=0)
    above = jnp.concatenate([along_z[nodes : nodes + 2], zeros], axis=0)
    lane = counted((nodes, lanes), 1)
    first_own = core * blocks
    first_partner = blocks - first_own
    element = jnp.where(lane < half, lane // ext + first_own, (lane - half) // ext + first_partner)
    zero = jnp.zeros_like(own)
    for place in range(0, 2 * blocks, 2):
        first = place + first_own if place < blocks else place - blocks + first_partner
        pair = []
        for block in (first, first + 1):
            value = jnp.where(element == block, own, zero)
            value = value + jnp.where(element == block + 1, below, zero)
            pair.append(value + jnp.where(element == block - 1, above, zero))
        high, low = split2(jnp.concatenate(pair, axis=0))
        mz_ref[0, place * nodes : (place + 2) * nodes, :] = high
        mz_ref[1, place * nodes : (place + 2) * nodes, :] = low


def both_sides(core, direct, passed):
    low = [jnp.where(core == 0, direct[h], passed[1 - h]) for h in range(2)]
    high = [jnp.where(core == 0, passed[1 - h], direct[h]) for h in range(2)]
    return low, high


def edges(axis):
    place, size = lax.axis_index(axis), lax.axis_size(axis)
    return place > 0, place < size - 1


def x_positions(core, own_ref, partner_ref, direct_ref, passed_ref):
    has_low, has_high = edges("gx")
    length = own_ref.shape[1]
    sides = []
    for slot in range(2):
        direct = [direct_ref[h, slot] for h in range(2)]
        passed = [passed_ref[h, slot] for h in range(2)]
        low, high = both_sides(core, direct, passed)
        low = [jnp.where(has_low, v, jnp.zeros_like(v)) for v in low]
        high = [jnp.where(has_high, v, jnp.zeros_like(v)) for v in high]
        sides.append((low, high))
    positions = [sides[0][0]]
    for layer in range(length):
        value = [own_ref[layer], partner_ref[layer]]
        if layer == 0:
            value = [v + w for v, w in zip(sides[1][0], value)]
        if layer == length - 1:
            value = [v + w for v, w in zip(value, sides[0][1])]
        positions.append(value)
    return positions + [sides[1][1]]


def rows_kernel(own_ref, partner_ref, direct_ref, passed_ref, after_ref, out_ref):
    core = lax.axis_index("gz")
    _, rows, width = own_ref.shape
    positions = x_positions(core, own_ref, partner_ref, direct_ref, passed_ref)
    out_ref[out_ref.shape[0] - 1] = jnp.zeros(out_ref.shape[1:], f32)
    for a, (own, partner) in enumerate(positions):
        row = 2 * a % rows
        for half, value in enumerate((partner, own)):
            out_ref[2 * a // rows, row : row + 2, half * width : (half + 1) * width] = jnp.where(
                core == 0, value[0:2], value[rows - 2 : rows]
            )


def by_z(value, mz):
    high, low = split2(value)
    return dot(high, mz[0]) + (dot(low, mz[0]) + dot(high, mz[1]))


def back_by_z(value, mz):
    high, low = split2(value)
    return dot(high, mz[0], True) + (dot(low, mz[0], True) + dot(high, mz[1], True))


def from_rows(value, use, mz, cx_rows, ext):
    count, rows, both = value.shape
    value = jnp.where(use, value, jnp.zeros_like(value))
    along_z = by_z(value.reshape(count * rows, both), mz)
    for p in range(ext):
        total = sum(
            cx_rows[(p * count + t) * rows : (p * count + t + 1) * rows, :]
            * along_z[t * rows : (t + 1) * rows]
            for t in range(count)
        )
        shift = 2
        while shift < rows:
            total = total + pltpu.roll(total, shift, 0)
            shift *= 2
        yield total


def interior_solve_kernel(
    own_ref, partner_ref, xd_ref, xp_ref, yd_ref, cx, cx_rows, cy, mz, out_ref, grid
):
    core = lax.axis_index("gz")
    _, rows, width = own_ref.shape
    ext, padded, lanes = out_ref.shape
    nodes = ext - 2
    has_low, has_high = edges("gy")
    positions = x_positions(core, own_ref, partner_ref, xd_ref, xp_ref)
    for a, halves in enumerate(positions):
        for half, value in enumerate(halves):
            grid[a, :, half * width : (half + 1) * width] = value
    along_z = by_z(grid[...].reshape(ext * rows, 2 * width), mz)
    along_z = along_z.reshape(ext, rows, lanes)
    use = jnp.where(core == 0, has_low, has_high)
    outer = [cy[0, core * nodes + k] for k in range(2)]
    for p, value in enumerate(from_rows(yd_ref[...], use, mz, cx_rows, ext)):
        inner = sum(cx[a * ext + p : a * ext + p + 1, :] * along_z[a] for a in range(ext))
        total = sum(cy[0, b + 1] * inner[b : b + 1] for b in range(rows))
        out_ref[p] = total + sum(outer[k] * value[k : k + 1] for k in range(2))


def back_by_x(spectral, coefficients):
    return sum(c * spectral[p] for p, c in enumerate(coefficients))


def back_by_y(value, cy, ext):
    return sum(cy[1, q] * value[q : q + 1] for q in range(ext))


def solve_kernel(yp_ref, part_ref, cx, cx_rows, cy, rate, mz, spectral, sent_ref):
    core = lax.axis_index("gz")
    width = yp_ref.shape[2] // 2
    ext, padded, lanes = rate.shape
    nodes = ext - 2
    has_low, has_high = edges("gy")
    passed = jnp.concatenate([yp_ref[:, :, width:], yp_ref[:, :, 0:width]], axis=2)
    use = jnp.where(core == 0, has_high, has_low)
    outer = [cy[0, (1 - core) * nodes + k] for k in range(2)]
    for p, value in enumerate(from_rows(passed, use, mz, cx_rows, ext)):
        total = part_ref[p] + sum(outer[k] * value[k : k + 1] for k in range(2))
        spectral[p] = total * rate[p]
    layers = []
    for layer in range(2):
        rows = [layer * ext + p for p in range(ext)]
        last = [r + nodes * ext for r in rows]
        coefficients = [
            jnp.where(core == 0, cx[r : r + 1, :], cx[k : k + 1, :]) for r, k in zip(rows, last)
        ]
        layers.append(back_by_y(back_by_x(spectral, coefficients), cy, ext))
    result = back_by_z(jnp.concatenate(layers, axis=0), mz)
    for layer in range(2):
        for half in range(2):
            lanes_at = slice((1 - half) * width, (2 - half) * width)
            place = half * 2 + layer
            value = result[layer * padded : layer * padded + nodes + 2, lanes_at]
            sent_ref[place] = value[0:nodes]
            sent_ref[4, 2 * place : 2 * place + 2, :] = value[nodes : nodes + 2]


def interior_kernel(spectral, cx, cy, mz, after_ref, out_ref):
    ext, padded, lanes = spectral.shape
    nodes, _, both = out_ref.shape
    layers = []
    for a in range(1, ext - 1):
        coefficients = [cx[a * ext + p : a * ext + p + 1, :] for p in range(ext)]
        layers.append(back_by_y(back_by_x(spectral, coefficients), cy, ext))
    result = back_by_z(jnp.concatenate(layers, axis=0), mz)
    out_ref[...] = result.reshape(nodes, padded, both)


def return_rows_kernel(initial_ref, inner_ref, direct_ref, passed_ref, out_ref, base_ref):
    core = lax.axis_index("gz")
    has_low, has_high = edges("gx")
    nodes, rows, width = initial_ref.shape
    for layer in range(nodes):
        lanes = [slice(0, width), slice(width, 2 * width)]
        outer = [inner_ref[layer, rows : rows + 2, lanes[h]] for h in range(2)]
        values = [inner_ref[layer, 0:rows, lanes[h]] for h in range(2)]
        if layer < 2 or layer >= nodes - 2:
            slot = layer if layer < 2 else layer - (nodes - 2)

            def parts(ref, h, slot=slot):
                place = 2 * h + slot
                return ref[place], ref[4, 2 * place : 2 * place + 2, :]

            direct = [parts(direct_ref, h) for h in range(2)]
            passed = [parts(passed_ref, h) for h in range(2)]
            side = 0 if layer < 2 else 1
            valid = (has_low, has_high)[side]
            for k, target in enumerate((values, outer)):
                both = both_sides(core, [d[k] for d in direct], [d[k] for d in passed])[side]
                for h in range(2):
                    target[h] = target[h] + jnp.where(valid, both[h], jnp.zeros_like(both[h]))
        base_ref[layer] = initial_ref[layer] + values[0]
        for place, h in enumerate((1, 0)):
            first = jnp.where(core == 0, outer[h][0:1], values[h][rows - 1 : rows])
            second = jnp.where(core == 0, values[h][0:1], outer[h][1:2])
            out_ref[layer, :, lanes[place]] = jnp.concatenate([first, second], axis=0)


def result_kernel(base_ref, direct_ref, passed_ref, out_ref):
    core = lax.axis_index("gz")
    has_low, has_high = edges("gy")
    nodes, rows, width = base_ref.shape
    for layer in range(nodes):
        direct = direct_ref[layer, :, 0:width]
        passed = passed_ref[layer, :, width:]
        low = jnp.where(core == 0, direct, passed)
        high = jnp.where(core == 0, passed, direct)
        low = jnp.where(has_low, low, jnp.zeros_like(low))
        high = jnp.where(has_high, high, jnp.zeros_like(high))
        between = jnp.zeros((rows - 4, low.shape[1]), f32)
        out_ref[layer] = base_ref[layer] + jnp.concatenate([low, between, high], axis=0)


def swap_pairs(axis):
    sizes = [lax.axis_size(name) for name in AXES]
    along, across = (0, 1) if axis == "gx" else (1, 0)

    def number(place, other, core):
        spot = (place, other) if along == 0 else (other, place)
        return (spot[0] * sizes[1] + spot[1]) * 2 + core

    pairs = []
    for other in range(sizes[across]):
        for place in range(sizes[along] - 1):
            here, there = number(place, other, 1), number(place + 1, other, 0)
            pairs += [(here, there), (there, here)]
        if other ^ 1 < sizes[across]:
            for place, core in ((0, 0), (sizes[along] - 1, 1)):
                pairs.append((number(place, other, core), number(place, other ^ 1, core)))
    return pairs


def swap(value, axis):
    if axis == "gz":
        return lax.ppermute(value, "gz", [(0, 1), (1, 0)])
    return lax.ppermute(value, AXES, swap_pairs(axis))


def paired_body(initial, source, metric, eigenvectors, eigenvalues):
    nodes, rows, width = initial.shape
    ext = eigenvectors.shape[1]
    blocks = width // nodes
    lanes = 2 * blocks * ext
    padded = 2 * rows
    vectors = eigenvectors.reshape(3 * ext * ext, 1, blocks)
    values = eigenvalues.reshape(3 * ext, 1, blocks)
    inputs = [
        pltpu.with_memory_space_constraint(value, pltpu.HBM)
        for value in (initial, source, metric, values)
    ]
    own = call(
        residual_kernel,
        [shaped((nodes + -(-3 * ext // rows), rows, width))],
        inputs,
        scratch=[
            *(pltpu.VMEM(value.shape, value.dtype) for value in inputs),
            pltpu.SemaphoreType.DMA((3 + metric.shape[0],)),
        ],
        where=HBM,
    )[0]
    partner = swap(own, "gz")
    vectors, own = lax.optimization_barrier((vectors, own))
    partner_vectors = swap(vectors, "gz")
    sent = call(layers_kernel, [shaped((2, 2, rows, width))], [own, partner])[0]
    x_direct = swap(sent, "gx")
    tiles = -(-2 * ext // rows)
    cx, cx_rows, rate = call(
        x_coefficients_kernel,
        [
            shaped((ext * ext, lanes)),
            shaped((ext * tiles * rows, lanes)),
            shaped((ext, padded, lanes)),
        ],
        [vectors, partner_vectors, own, partner, sent],
    )
    x_direct, cx, rate = lax.optimization_barrier((x_direct, cx, rate))
    x_passed = swap(x_direct, "gz")
    mz = call(
        z_coefficients_kernel,
        [shaped((2, 2 * width, lanes), bf16)],
        [vectors, partner_vectors, x_direct],
    )[0]
    sent = call(
        rows_kernel,
        [shaped((tiles, rows, 2 * width))],
        [own, partner, x_direct, x_passed, mz],
    )[0]
    y_direct = swap(sent, "gy")
    cy = call(
        y_coefficients_kernel,
        [shaped((2, ext, padded, lanes))],
        [vectors, partner_vectors, sent],
    )[0]
    y_direct, cy = lax.optimization_barrier((y_direct, cy))
    y_passed = swap(y_direct, "gz")
    part = call(
        interior_solve_kernel,
        [shaped((ext, padded, lanes))],
        [own, partner, x_direct, x_passed, y_direct, cx, cx_rows, cy, mz],
        scratch=[pltpu.VMEM((ext, rows, 2 * width), f32)],
    )[0]
    spectral, sent = call(
        solve_kernel,
        [shaped((ext, padded, lanes)), shaped((5, rows, width))],
        [y_passed, part, cx, cx_rows, cy, rate, mz],
    )

    x_direct = swap(sent, "gx")
    inner = call(interior_kernel, [shaped((nodes, padded, 2 * width))], [spectral, cx, cy, mz, sent])[0]
    x_passed = swap(x_direct, "gz")
    sent, base = call(
        return_rows_kernel,
        [shaped((nodes, 2, 2 * width)), shaped(initial.shape)],
        [initial, inner, x_direct, x_passed],
    )
    y_direct = swap(sent, "gy")
    y_passed = swap(y_direct, "gz")
    return call(result_kernel, [shaped(initial.shape)], [base, y_direct, y_passed])[0]


def body(initial, source, metric, eigenvectors, eigenvalues):
    nodes = gll_points.shape[0]
    one_element = initial.shape[0] == nodes and initial.shape[1] == nodes
    if lax.axis_size("gz") == 2 and one_element and initial.shape[2] % 128 == 0:
        return paired_body(initial, source, metric, eigenvectors, eigenvalues)
    return general_body(initial, source, metric, eigenvectors, eigenvalues)


def solution(mesh):
    placed = (
        P("gx", "gy", "gz"),
        P("gx", "gy", "gz"),
        P(None, "gx", "gy", "gz"),
        P(None, None, None, "gx", "gy", "gz"),
        P(None, None, "gx", "gy", "gz"),
    )
    return jax.shard_map(
        body, mesh=mesh, in_specs=placed, out_specs=P("gx", "gy", "gz"), check_vma=False
    )
```

```python
import functools

import jax
import jax.numpy as jnp
import numpy as np
from jax import lax
from jax.experimental import pallas as pl
from jax.experimental.pallas import tpu as pltpu
from jax.sharding import PartitionSpec as P

gll_points = np.array(
    [
        -1.0,
        -0.8717401485096066,
        -0.5917001814331423,
        -0.2092992179024789,
        0.2092992179024789,
        0.5917001814331423,
        0.8717401485096066,
        1.0,
    ]
)


def extended_2(value, sides, width):
    for axis, dim in sides:
        size, length = (lax.axis_size(axis), value.shape[dim])
        up = [(i, (i + 1) % size) for i in range(size - 1)]
        down = [(j, i) for i, j in up]
        last = lax.slice_in_dim(value, length - width, length, axis=dim)
        first = lax.slice_in_dim(value, 0, width, axis=dim)
        before = lax.ppermute(last, axis, up)
        after = lax.ppermute(first, axis, down)
        value = jnp.concatenate([before, value, after], axis=dim)
    return value


def derivative_table():
    number = gll_points.shape[0]
    products = np.array(
        [
            np.prod(
                [
                    gll_points[row_index] - gll_points[other]
                    for other in range(number)
                    if other != row_index
                ]
            )
            for row_index in range(number)
        ]
    )
    matrix_out = np.zeros((number, number))
    for row_index in range(number):
        for col_index in range(number):
            if row_index != col_index:
                matrix_out[row_index, col_index] = (
                    products[row_index]
                    / products[col_index]
                    / (gll_points[row_index] - gll_points[col_index])
                )
        matrix_out[row_index, row_index] = -np.sum(matrix_out[row_index])
    return matrix_out


def apply_along(values, matrix, direction):
    block_size = matrix.shape[1]
    old_shape = values.shape
    pieces_shape = (
        old_shape[:direction]
        + (old_shape[direction] // block_size, block_size)
        + old_shape[direction + 1 :]
    )
    result = jnp.tensordot(
        values.reshape(pieces_shape),
        matrix,
        axes=((direction + 1,), (1,)),
        precision=lax.Precision.HIGHEST,
    )
    result = jnp.moveaxis(result, -1, direction + 1)
    return result.reshape(
        old_shape[:direction]
        + (old_shape[direction] // block_size * matrix.shape[0],)
        + old_shape[direction + 1 :]
    )


def apply_operator(values, metric):
    deriv_table = jnp.asarray(derivative_table(), jnp.float32)
    summed = jnp.zeros_like(values)
    for direction in range(3):
        gradient = apply_along(values, deriv_table, direction)
        summed = summed + apply_along(metric[direction] * gradient, deriv_table.T, direction)
    return summed


def assemble(padded, offset):
    result = padded
    for direction in range(3):
        length = result.shape[direction]
        view_shape = [1, 1, 1]
        view_shape[direction] = length
        node_index = ((jnp.arange(length) - offset) % 8).reshape(view_shape)
        edge_zero = jnp.zeros_like(lax.slice_in_dim(result, 0, 1, axis=direction))
        upward = jnp.concatenate(
            [lax.slice_in_dim(result, 1, length, axis=direction), edge_zero], axis=direction
        )
        downward = jnp.concatenate(
            [edge_zero, lax.slice_in_dim(result, 0, length - 1, axis=direction)], axis=direction
        )
        result = (
            result
            + jnp.where(node_index == 7, upward, 0.0)
            + jnp.where(node_index == 0, downward, 0.0)
        )
    return result


def extend_axis(padded, direction):
    shifted = jnp.moveaxis(padded, direction, 0)
    blocks = (shifted.shape[0] - 4) // 8
    trailing = shifted.shape[1:]
    middle = shifted[2:-2].reshape((blocks, 8) + trailing)
    lowest = shifted[0 : 8 * blocks : 8][:, None]
    beyond = shifted[11::8][:, None]
    joined = jnp.concatenate([lowest, middle, beyond], axis=1).reshape((blocks * 10,) + trailing)
    return jnp.moveaxis(joined, 0, direction)


def widen(padded):
    return extend_axis(extend_axis(extend_axis(padded, 0), 1), 2)


def fast_solve(extended, eigenvectors, eigenvalues):
    count_x, count_y, count_z = eigenvectors.shape[3:]
    precise = lax.Precision.HIGHEST
    spectral = extended.reshape(count_x, 10, count_y, 10, count_z, 10)
    spectral = jnp.einsum("apxyz,xaybzc->xpybzc", eigenvectors[0], spectral, precision=precise)
    spectral = jnp.einsum("bqxyz,xpybzc->xpyqzc", eigenvectors[1], spectral, precision=precise)
    spectral = jnp.einsum("csxyz,xpyqzc->xpyqzs", eigenvectors[2], spectral, precision=precise)
    rate_x = jnp.transpose(eigenvalues[0], (1, 0, 2, 3))[:, :, :, None, :, None]
    rate_y = jnp.transpose(eigenvalues[1], (1, 2, 0, 3))[:, None, :, :, :, None]
    rate_z = jnp.transpose(eigenvalues[2], (1, 2, 3, 0))[:, None, :, None, :, :]
    spectral = spectral / (rate_x + rate_y + rate_z)
    spectral = jnp.einsum("csxyz,xpyqzs->xpyqzc", eigenvectors[2], spectral, precision=precise)
    spectral = jnp.einsum("bqxyz,xpyqzc->xpybzc", eigenvectors[1], spectral, precision=precise)
    spectral = jnp.einsum("apxyz,xpybzc->xaybzc", eigenvectors[0], spectral, precision=precise)
    return spectral.reshape(count_x * 10, count_y * 10, count_z * 10)


def return_axis(padded, direction):
    shifted = jnp.moveaxis(padded, direction, 0)
    blocks = (shifted.shape[0] - 4) // 10
    trailing = shifted.shape[1:]
    owned = shifted[2:-2].reshape((blocks, 10) + trailing)[:, 1:9]
    before = shifted[0 : 10 * blocks].reshape((blocks, 10) + trailing)[:, 0:2]
    following = shifted[4:].reshape((blocks, 10) + trailing)[:, 8:10]
    middle = jnp.zeros((blocks, 4) + trailing, shifted.dtype)
    summed = owned + jnp.concatenate([before, middle, following], axis=1)
    return jnp.moveaxis(summed.reshape((blocks * 8,) + trailing), 0, direction)


def general_body(initial, source, metric, eigenvectors, eigenvalues):
    solution = initial
    local_res = source - apply_operator(solution, metric)
    deeper = extended_2(local_res, (("gx", 0), ("gy", 1), ("gz", 2)), 2)
    widened = assemble(deeper, 2)
    extended = widen(widened)
    corrected = fast_solve(extended, eigenvectors, eigenvalues)
    padded = extended_2(corrected, (("gx", 0), ("gy", 1), ("gz", 2)), 2)
    correction = return_axis(return_axis(return_axis(padded, 0), 1), 2)
    solution = solution + correction
    return solution


AXES = ("gx", "gy", "gz")
VMEM = pl.BlockSpec(memory_space=pltpu.VMEM)
HBM = pl.BlockSpec(memory_space=pltpu.HBM)
VMEM_LIMIT = 16 * 2**20
f32 = jnp.float32
bf16 = jnp.bfloat16


def call(kernel, outs, args, scratch=(), where=VMEM):
    moved = sum(int(np.prod(a.shape)) * a.dtype.itemsize for a in (*args, *outs))
    return pl.pallas_call(
        kernel,
        out_shape=outs,
        in_specs=[where] * len(args),
        out_specs=[VMEM] * len(outs),
        scratch_shapes=scratch,
        compiler_params=pltpu.CompilerParams(vmem_limit_bytes=VMEM_LIMIT),
        cost_estimate=pl.CostEstimate(flops=0, bytes_accessed=moved, transcendentals=0),
    )(*args)


def shaped(shape, dtype=f32):
    return jax.ShapeDtypeStruct(shape, dtype)


def counted(shape, axis):
    return lax.broadcasted_iota(jnp.int32, shape, axis)


def split2(value):
    high = value.astype(bf16)
    return high, (value - high.astype(f32)).astype(bf16)


def split3(value):
    high = value.astype(bf16)
    rest = value - high.astype(f32)
    middle = rest.astype(bf16)
    return high, middle, (rest - middle.astype(f32)).astype(bf16)


def dot(left, right, transposed=False):
    dims = (((1,), (1 if transposed else 0,)), ((), ()))
    return lax.dot_general(left, right, dims, preferred_element_type=f32)


def repeated_table(table, width):
    nodes = table.shape[0]
    row, column = counted((nodes, width), 0), counted((nodes, width), 1) % nodes
    tile = jnp.zeros((nodes, width), f32)
    for j in range(nodes):
        values = jnp.zeros((nodes, width), f32)
        for i in range(nodes):
            values = jnp.where(row == i, float(table[i, j]), values)
        tile = jnp.where(column == j, values, tile)
    return tile


def residual_kernel(
    u_hbm, source_hbm, metric_hbm, val_hbm, out_ref, u_ref, source_ref, metric_ref, val_ref, sems
):
    copies = [pltpu.make_async_copy(u_hbm, u_ref, sems.at[0])]
    copies += [
        pltpu.make_async_copy(metric_hbm.at[d], metric_ref.at[d], sems.at[1 + d])
        for d in range(metric_hbm.shape[0])
    ]
    copies.append(pltpu.make_async_copy(source_hbm, source_ref, sems.at[len(copies)]))
    copies.append(pltpu.make_async_copy(val_hbm, val_ref, sems.at[len(copies)]))
    for copy in copies:
        copy.start()
    nodes, rows, width = u_ref.shape
    flat_rows = nodes * rows
    table = np.asarray(derivative_table(), np.float32)
    along_y, along_z = [], []
    for t in range(2):
        tile = repeated_table(table if t == 0 else table.T, width)
        high = tile.astype(bf16).astype(f32)
        low = tile - high
        group = counted((nodes, width), 1) // nodes
        zero = jnp.zeros_like(tile)
        for part in (high, low):
            bands = [jnp.where(group == k, part, zero) for k in range(width // nodes)]
            along_z.append(jnp.concatenate(bands, axis=0).astype(bf16))
        group = group[:, 0 : 2 * flat_rows]
        high, low, zero = (v[:, 0 : 2 * flat_rows] for v in (high, low, zero))
        bands = [jnp.where(group % rows == k, high, zero) for k in range(nodes)]
        bands += [jnp.where(group == k, low, zero) for k in range(nodes)]
        along_y.append(jnp.concatenate(bands, axis=0).astype(bf16))

    def by_y(value, t):
        both = dot(along_y[t], jnp.concatenate(split2(value), axis=0))
        return both[0:flat_rows] + both[flat_rows:]

    def by_z(value, t):
        high, low = split2(value)
        both = dot(jnp.concatenate([high, low], axis=0), along_z[2 * t])
        return both[0:flat_rows] + (both[flat_rows:] + dot(high, along_z[2 * t + 1]))

    copies[0].wait()
    flat = u_ref[...].reshape(flat_rows, width)
    flux_y, flux_z = by_y(flat, 0), by_z(flat, 1)
    layers = [u_ref[j] for j in range(nodes)]
    flux_x = [sum(float(table[i, j]) * layers[j] for j in range(nodes)) for i in range(nodes)]
    for copy in copies[1:]:
        copy.wait()
    total = by_y(flux_y * metric_ref[1].reshape(flat.shape), 1)
    total = total + by_z(flux_z * metric_ref[2].reshape(flat.shape), 0)
    total = total.reshape(nodes, rows, width)
    flux_x = [metric_ref[0, i] * flux_x[i] for i in range(nodes)]
    for j in range(nodes):
        applied = sum(float(table[i, j]) * flux_x[i] for i in range(nodes))
        out_ref[j] = source_ref[j] - (applied + total[j])
    count, _, blocks = val_ref.shape
    values = val_ref[...].reshape(count, blocks)
    for first in range(0, count, rows):
        last = min(first + rows, count)
        out_ref[nodes + first // rows, 0 : last - first, 0:blocks] = values[first:last]


def layers_kernel(own_ref, partner_ref, out_ref):
    start = lax.axis_index("gz") * (out_ref.shape[2] - 2)
    for half, ref in enumerate((partner_ref, own_ref)):
        for layer in range(2):
            out_ref[half, layer] = ref[start + layer]


def taken(ref, first, count):
    return ref[first : first + count].reshape(count, ref.shape[2])


def spread(own, partner, ext):
    blocks = own.shape[1]
    parts = [*split3(own), *split3(partner)]
    shape = (blocks, 2 * blocks * ext)
    repeat = []
    for half in range(2):
        element = counted(shape, 1) // ext - half * blocks
        repeat += [(element == counted(shape, 0)).astype(f32).astype(bf16)] * 3
    return dot(jnp.concatenate(parts, axis=1), jnp.concatenate(repeat, axis=0))


def gathered(choice, value):
    choice = choice.astype(f32).astype(bf16)
    high, middle, low = split3(value)
    return dot(choice, high) + (dot(choice, middle) + dot(choice, low))


def x_coefficients_kernel(
    own_vec, partner_vec, own_ref, partner_ref, after_ref, cx_ref, cx_rows_ref, rate_ref
):
    ext, padded, lanes = rate_ref.shape
    blocks = own_vec.shape[2]
    nodes = ext - 2
    square = ext * ext
    along_x = spread(taken(own_vec, 0, square), taken(partner_vec, 0, square), ext)
    cx_ref[...] = along_x
    shape = (cx_rows_ref.shape[0], square)
    place = counted(shape, 0) % (shape[0] // ext) // 2
    choice = (place < ext) & (counted(shape, 1) == place * ext + counted(shape, 0) // (shape[0] // ext))
    cx_rows_ref[...] = gathered(choice, along_x)
    rates = []
    for ref in (own_ref, partner_ref):
        tiles = ref[nodes : ref.shape[0]]
        rates.append(tiles.reshape(-1, tiles.shape[2])[0 : 3 * ext, 0:blocks])
    rates = spread(*rates, ext)
    shape = (ext, lanes)
    rate_z = rates[2 * ext : 3 * ext]
    same = counted(shape, 0) == counted(shape, 1) % ext
    rate_z = jnp.sum(jnp.where(same, rate_z, jnp.zeros_like(rate_z)), axis=0, keepdims=True)
    rate_y = jnp.concatenate([rates[ext : 2 * ext], jnp.ones((padded - ext, lanes), f32)], axis=0)
    for p in range(ext):
        rate_ref[p] = 1.0 / (rates[p : p + 1] + rate_y + rate_z)


def y_coefficients_kernel(own_vec, partner_vec, after_ref, cy_ref):
    ext, padded = cy_ref.shape[1:3]
    square = ext * ext
    along_y = spread(taken(own_vec, square, square), taken(partner_vec, square, square), ext)
    shape = (ext * padded, square)
    first, second, entry = counted(shape, 0) // padded, counted(shape, 0) % padded, counted(shape, 1)
    forward = (second < ext) & (entry == first * ext + second)
    position = jnp.where(second < ext - 2, second + 1, jnp.where(second == ext - 2, 0, ext - 1))
    backward = (second < ext) & (entry == position * ext + first)
    for k, choice in enumerate((forward, backward)):
        cy_ref[k] = gathered(choice, along_y).reshape(cy_ref.shape[1:])


def z_coefficients_kernel(own_vec, partner_vec, after_ref, mz_ref):
    blocks = own_vec.shape[2]
    lanes = mz_ref.shape[2]
    half = lanes // 2
    ext = half // blocks
    square = ext * ext
    nodes = ext - 2
    core = lax.axis_index("gz")
    shape = (square, lanes)
    same = counted(shape, 0) % ext == counted(shape, 1) % ext
    along_z = spread(
        taken(own_vec, 2 * square, square), taken(partner_vec, 2 * square, square), ext
    )
    along_z = jnp.where(same, along_z, jnp.zeros_like(along_z))
    shape = (ext, square)
    along_z = gathered(counted(shape, 1) // ext == counted(shape, 0), along_z)

    zeros = jnp.zeros((nodes - 2, lanes), f32)
    own = along_z[1 : nodes + 1]
    below = jnp.concatenate([zeros, along_z[0:2]], axis=0)
    above = jnp.concatenate([along_z[nodes : nodes + 2], zeros], axis=0)
    lane = counted((nodes, lanes), 1)
    first_own = core * blocks
    first_partner = blocks - first_own
    element = jnp.where(lane < half, lane // ext + first_own, (lane - half) // ext + first_partner)
    zero = jnp.zeros_like(own)
    for place in range(0, 2 * blocks, 2):
        first = place + first_own if place < blocks else place - blocks + first_partner
        pair = []
        for block in (first, first + 1):
            value = jnp.where(element == block, own, zero)
            value = value + jnp.where(element == block + 1, below, zero)
            pair.append(value + jnp.where(element == block - 1, above, zero))
        high, low = split2(jnp.concatenate(pair, axis=0))
        mz_ref[0, place * nodes : (place + 2) * nodes, :] = high
        mz_ref[1, place * nodes : (place + 2) * nodes, :] = low


def trade_cores(axis, place):
    return (place % 2, place % 2) if axis == "gx" else (0, 1)


def trades_below(axis):
    core, place = lax.axis_index("gz"), lax.axis_index(axis)
    return core != place % 2 if axis == "gx" else core == 1


def sides(below, direct, passed):
    low = [jnp.where(below, direct[h], passed[1 - h]) for h in range(2)]
    high = [jnp.where(below, passed[1 - h], direct[h]) for h in range(2)]
    return low, high


def edges(axis):
    place, size = lax.axis_index(axis), lax.axis_size(axis)
    return place > 0, place < size - 1


def layers_kernel(own_ref, partner_ref, out_ref):
    start = jnp.where(trades_below("gx"), 0, out_ref.shape[2] - 2)
    for half, ref in enumerate((own_ref, partner_ref)):
        for layer in range(2):
            out_ref[half, layer] = ref[start + layer]


def x_positions(own_ref, partner_ref, direct_ref, passed_ref):
    has_low, has_high = edges("gx")
    length = own_ref.shape[1]
    below = trades_below("gx")
    outer = []
    for slot in range(2):
        direct = [direct_ref[h, slot] for h in range(2)]
        passed = [passed_ref[h, slot] for h in range(2)]
        low, high = sides(below, direct, passed)
        low = [jnp.where(has_low, v, jnp.zeros_like(v)) for v in low]
        high = [jnp.where(has_high, v, jnp.zeros_like(v)) for v in high]
        outer.append((low, high))
    positions = [outer[0][0]]
    for layer in range(length):
        value = [own_ref[layer], partner_ref[layer]]
        if layer == 0:
            value = [v + w for v, w in zip(outer[1][0], value)]
        if layer == length - 1:
            value = [v + w for v, w in zip(value, outer[0][1])]
        positions.append(value)
    return positions + [outer[1][1]]


def rows_kernel(own_ref, partner_ref, direct_ref, passed_ref, after_ref, out_ref):
    _, rows, width = own_ref.shape
    below = trades_below("gy")
    positions = x_positions(own_ref, partner_ref, direct_ref, passed_ref)
    out_ref[out_ref.shape[0] - 1] = jnp.zeros(out_ref.shape[1:], f32)
    for a, (own, partner) in enumerate(positions):
        row = 2 * a % rows
        for half, value in enumerate((partner, own)):
            out_ref[2 * a // rows, row : row + 2, half * width : (half + 1) * width] = jnp.where(
                below, value[0:2], value[rows - 2 : rows]
            )


def by_parts(value, mz, transposed):
    rows = value.shape[0]
    spare = -rows % 16
    if spare:
        value = jnp.concatenate([value, jnp.zeros((spare, value.shape[1]), f32)], axis=0)
    high, low = split2(value)
    both = dot(jnp.concatenate([high, low], axis=0), mz[0], transposed)
    total = both[0 : rows + spare] + (both[rows + spare :] + dot(high, mz[1], transposed))
    return total[0:rows]


def by_z(value, mz):
    return by_parts(value, mz, False)


def back_by_z(value, mz):
    return by_parts(value, mz, True)


def from_rows(value, use, mz, cx_rows, ext):
    count, rows, both = value.shape
    value = jnp.where(use, value, jnp.zeros_like(value))
    along_z = by_z(value.reshape(count * rows, both), mz)
    for p in range(ext):
        total = sum(
            cx_rows[(p * count + t) * rows : (p * count + t + 1) * rows, :]
            * along_z[t * rows : (t + 1) * rows]
            for t in range(count)
        )
        shift = 2
        while shift < rows:
            total = total + pltpu.roll(total, shift, 0)
            shift *= 2
        yield total


def interior_solve_kernel(
    own_ref, partner_ref, xd_ref, xp_ref, yd_ref, cx, cx_rows, cy, mz, out_ref, grid
):
    _, rows, width = own_ref.shape
    ext, padded, lanes = out_ref.shape
    nodes = ext - 2
    has_low, has_high = edges("gy")
    positions = x_positions(own_ref, partner_ref, xd_ref, xp_ref)
    for a, halves in enumerate(positions):
        for half, value in enumerate(halves):
            grid[a, :, half * width : (half + 1) * width] = value
    along_z = by_z(grid[...].reshape(ext * rows, 2 * width), mz)
    along_z = along_z.reshape(ext, rows, lanes)
    below = trades_below("gy")
    use = jnp.where(below, has_low, has_high)
    outer = [cy[0, jnp.where(below, 0, nodes) + k] for k in range(2)]
    for p, value in enumerate(from_rows(yd_ref[...], use, mz, cx_rows, ext)):
        inner = sum(cx[a * ext + p : a * ext + p + 1, :] * along_z[a] for a in range(ext))
        total = sum(cy[0, b + 1] * inner[b : b + 1] for b in range(rows))
        out_ref[p] = total + sum(outer[k] * value[k : k + 1] for k in range(2))


def back_by_x(spectral, coefficients):
    return sum(c * spectral[p] for p, c in enumerate(coefficients))


def back_by_y(value, cy, ext):
    return sum(cy[1, q] * value[q : q + 1] for q in range(ext))


def solve_kernel(yp_ref, part_ref, cx, cx_rows, cy, rate, mz, spectral, sent_ref):
    below = trades_below("gy")
    width = yp_ref.shape[2] // 2
    ext, padded, lanes = rate.shape
    nodes = ext - 2
    has_low, has_high = edges("gy")
    passed = jnp.concatenate([yp_ref[:, :, width:], yp_ref[:, :, 0:width]], axis=2)
    use = jnp.where(below, has_high, has_low)
    outer = [cy[0, jnp.where(below, nodes, 0) + k] for k in range(2)]
    for p, value in enumerate(from_rows(passed, use, mz, cx_rows, ext)):
        total = part_ref[p] + sum(outer[k] * value[k : k + 1] for k in range(2))
        spectral[p] = total * rate[p]
    layers = []
    for layer in range(2):
        rows = [layer * ext + p for p in range(ext)]
        last = [r + nodes * ext for r in rows]
        coefficients = [
            jnp.where(trades_below("gx"), cx[r : r + 1, :], cx[k : k + 1, :])
            for r, k in zip(rows, last)
        ]
        layers.append(back_by_y(back_by_x(spectral, coefficients), cy, ext))
    result = back_by_z(jnp.concatenate(layers, axis=0), mz)
    for layer in range(2):
        for half in range(2):
            lanes_at = slice(half * width, (half + 1) * width)
            place = half * 2 + layer
            value = result[layer * padded : layer * padded + nodes + 2, lanes_at]
            sent_ref[place] = value[0:nodes]
            sent_ref[4, 2 * place : 2 * place + 2, :] = value[nodes : nodes + 2]


def interior_kernel(spectral, cx, cy, mz, after_ref, out_ref):
    ext, padded, lanes = spectral.shape
    nodes, _, both = out_ref.shape
    layers = []
    for a in range(1, ext - 1):
        coefficients = [cx[a * ext + p : a * ext + p + 1, :] for p in range(ext)]
        layers.append(back_by_y(back_by_x(spectral, coefficients), cy, ext))
    result = back_by_z(jnp.concatenate(layers, axis=0), mz)
    out_ref[...] = result.reshape(nodes, padded, both)


def return_rows_kernel(initial_ref, inner_ref, direct_ref, passed_ref, out_ref, base_ref):
    has_low, has_high = edges("gx")
    below_x, below_y = trades_below("gx"), trades_below("gy")
    nodes, rows, width = initial_ref.shape
    for layer in range(nodes):
        lanes = [slice(0, width), slice(width, 2 * width)]
        outer = [inner_ref[layer, rows : rows + 2, lanes[h]] for h in range(2)]
        values = [inner_ref[layer, 0:rows, lanes[h]] for h in range(2)]
        if layer < 2 or layer >= nodes - 2:
            slot = layer if layer < 2 else layer - (nodes - 2)

            def parts(ref, h, slot=slot):
                place = 2 * h + slot
                return ref[place], ref[4, 2 * place : 2 * place + 2, :]

            direct = [parts(direct_ref, h) for h in range(2)]
            passed = [parts(passed_ref, h) for h in range(2)]
            side = 0 if layer < 2 else 1
            valid = (has_low, has_high)[side]
            for k, target in enumerate((values, outer)):
                both = sides(below_x, [d[k] for d in direct], [d[k] for d in passed])[side]
                for h in range(2):
                    target[h] = target[h] + jnp.where(valid, both[h], jnp.zeros_like(both[h]))
        base_ref[layer] = initial_ref[layer] + values[0]
        for place, h in enumerate((1, 0)):
            first = jnp.where(below_y, outer[h][0:1], values[h][rows - 1 : rows])
            second = jnp.where(below_y, values[h][0:1], outer[h][1:2])
            out_ref[layer, :, lanes[place]] = jnp.concatenate([first, second], axis=0)


def result_kernel(base_ref, direct_ref, passed_ref, out_ref):
    below = trades_below("gy")
    has_low, has_high = edges("gy")
    nodes, rows, width = base_ref.shape
    for layer in range(nodes):
        direct = direct_ref[layer, :, 0:width]
        passed = passed_ref[layer, :, width:]
        low = jnp.where(below, direct, passed)
        high = jnp.where(below, passed, direct)
        low = jnp.where(has_low, low, jnp.zeros_like(low))
        high = jnp.where(has_high, high, jnp.zeros_like(high))
        between = jnp.zeros((rows - 4, low.shape[1]), f32)
        out_ref[layer] = base_ref[layer] + jnp.concatenate([low, between, high], axis=0)


def swap_pairs(axis):
    sizes = [lax.axis_size(name) for name in AXES]
    along, across = (0, 1) if axis == "gx" else (1, 0)

    def number(place, other, core):
        spot = (place, other) if along == 0 else (other, place)
        return (spot[0] * sizes[1] + spot[1]) * 2 + core

    pairs = []
    last = sizes[along] - 1
    for other in range(sizes[across]):
        for place in range(last):
            here, there = trade_cores(axis, place)
            here, there = number(place, other, here), number(place + 1, other, there)
            pairs += [(here, there), (there, here)]
        if other ^ 1 < sizes[across]:
            idle = [(place, core) for place in {0, last} for core in range(2)]
            if last > 0:
                idle.remove((0, trade_cores(axis, 0)[0]))
                idle.remove((last, trade_cores(axis, last - 1)[1]))
            for place, core in sorted(idle):
                pairs.append((number(place, other, core), number(place, other ^ 1, core)))
    return pairs


def swap(value, axis):
    if axis == "gz":
        return lax.ppermute(value, "gz", [(0, 1), (1, 0)])
    return lax.ppermute(value, AXES, swap_pairs(axis))


def paired_body(initial, source, metric, eigenvectors, eigenvalues):
    nodes, rows, width = initial.shape
    ext = eigenvectors.shape[1]
    blocks = width // nodes
    lanes = 2 * blocks * ext
    padded = 2 * rows
    vectors = eigenvectors.reshape(3 * ext * ext, 1, blocks)
    values = eigenvalues.reshape(3 * ext, 1, blocks)
    inputs = [
        pltpu.with_memory_space_constraint(value, pltpu.HBM)
        for value in (initial, source, metric, values)
    ]
    own = call(
        residual_kernel,
        [shaped((nodes + -(-3 * ext // rows), rows, width))],
        inputs,
        scratch=[
            *(pltpu.VMEM(value.shape, value.dtype) for value in inputs),
            pltpu.SemaphoreType.DMA((3 + metric.shape[0],)),
        ],
        where=HBM,
    )[0]
    partner = swap(own, "gz")
    vectors, own = lax.optimization_barrier((vectors, own))
    partner_vectors = swap(vectors, "gz")
    sent = call(layers_kernel, [shaped((2, 2, rows, width))], [own, partner])[0]
    x_direct = swap(sent, "gx")
    tiles = -(-2 * ext // rows)
    cx, cx_rows, rate = call(
        x_coefficients_kernel,
        [
            shaped((ext * ext, lanes)),
            shaped((ext * tiles * rows, lanes)),
            shaped((ext, padded, lanes)),
        ],
        [vectors, partner_vectors, own, partner, sent],
    )
    x_direct, cx, rate = lax.optimization_barrier((x_direct, cx, rate))
    x_passed = swap(x_direct, "gz")
    mz = call(
        z_coefficients_kernel,
        [shaped((2, 2 * width, lanes), bf16)],
        [vectors, partner_vectors, x_direct],
    )[0]
    sent = call(
        rows_kernel,
        [shaped((tiles, rows, 2 * width))],
        [own, partner, x_direct, x_passed, mz],
    )[0]
    y_direct = swap(sent, "gy")
    cy = call(
        y_coefficients_kernel,
        [shaped((2, ext, padded, lanes))],
        [vectors, partner_vectors, sent],
    )[0]
    y_direct, cy = lax.optimization_barrier((y_direct, cy))
    y_passed = swap(y_direct, "gz")
    part = call(
        interior_solve_kernel,
        [shaped((ext, padded, lanes))],
        [own, partner, x_direct, x_passed, y_direct, cx, cx_rows, cy, mz],
        scratch=[pltpu.VMEM((ext, rows, 2 * width), f32)],
    )[0]
    spectral, sent = call(
        solve_kernel,
        [shaped((ext, padded, lanes)), shaped((5, rows, width))],
        [y_passed, part, cx, cx_rows, cy, rate, mz],
    )

    x_direct = swap(sent, "gx")
    inner = call(interior_kernel, [shaped((nodes, padded, 2 * width))], [spectral, cx, cy, mz, sent])[0]
    x_passed = swap(x_direct, "gz")
    sent, base = call(
        return_rows_kernel,
        [shaped((nodes, 2, 2 * width)), shaped(initial.shape)],
        [initial, inner, x_direct, x_passed],
    )
    y_direct = swap(sent, "gy")
    y_passed = swap(y_direct, "gz")
    return call(result_kernel, [shaped(initial.shape)], [base, y_direct, y_passed])[0]


def body(initial, source, metric, eigenvectors, eigenvalues):
    nodes = gll_points.shape[0]
    one_element = initial.shape[0] == nodes and initial.shape[1] == nodes
    if lax.axis_size("gz") == 2 and one_element and initial.shape[2] % 128 == 0:
        return paired_body(initial, source, metric, eigenvectors, eigenvalues)
    return general_body(initial, source, metric, eigenvectors, eigenvalues)


def solution(mesh):
    placed = (
        P("gx", "gy", "gz"),
        P("gx", "gy", "gz"),
        P(None, "gx", "gy", "gz"),
        P(None, None, None, "gx", "gy", "gz"),
        P(None, None, "gx", "gy", "gz"),
    )
    return jax.shard_map(
        body, mesh=mesh, in_specs=placed, out_specs=P("gx", "gy", "gz"), check_vma=False
    )
```

```python
import functools

import jax
import jax.numpy as jnp
import numpy as np
from jax import lax
from jax.experimental import pallas as pl
from jax.experimental.pallas import tpu as pltpu
from jax.sharding import PartitionSpec as P

gll_points = np.array(
    [
        -1.0,
        -0.8717401485096066,
        -0.5917001814331423,
        -0.2092992179024789,
        0.2092992179024789,
        0.5917001814331423,
        0.8717401485096066,
        1.0,
    ]
)


def extended_2(value, sides, width):
    for axis, dim in sides:
        size, length = (lax.axis_size(axis), value.shape[dim])
        up = [(i, (i + 1) % size) for i in range(size - 1)]
        down = [(j, i) for i, j in up]
        last = lax.slice_in_dim(value, length - width, length, axis=dim)
        first = lax.slice_in_dim(value, 0, width, axis=dim)
        before = lax.ppermute(last, axis, up)
        after = lax.ppermute(first, axis, down)
        value = jnp.concatenate([before, value, after], axis=dim)
    return value


def derivative_table():
    number = gll_points.shape[0]
    products = np.array(
        [
            np.prod(
                [
                    gll_points[row_index] - gll_points[other]
                    for other in range(number)
                    if other != row_index
                ]
            )
            for row_index in range(number)
        ]
    )
    matrix_out = np.zeros((number, number))
    for row_index in range(number):
        for col_index in range(number):
            if row_index != col_index:
                matrix_out[row_index, col_index] = (
                    products[row_index]
                    / products[col_index]
                    / (gll_points[row_index] - gll_points[col_index])
                )
        matrix_out[row_index, row_index] = -np.sum(matrix_out[row_index])
    return matrix_out


def apply_along(values, matrix, direction):
    block_size = matrix.shape[1]
    old_shape = values.shape
    pieces_shape = (
        old_shape[:direction]
        + (old_shape[direction] // block_size, block_size)
        + old_shape[direction + 1 :]
    )
    result = jnp.tensordot(
        values.reshape(pieces_shape),
        matrix,
        axes=((direction + 1,), (1,)),
        precision=lax.Precision.HIGHEST,
    )
    result = jnp.moveaxis(result, -1, direction + 1)
    return result.reshape(
        old_shape[:direction]
        + (old_shape[direction] // block_size * matrix.shape[0],)
        + old_shape[direction + 1 :]
    )


def apply_operator(values, metric):
    deriv_table = jnp.asarray(derivative_table(), jnp.float32)
    summed = jnp.zeros_like(values)
    for direction in range(3):
        gradient = apply_along(values, deriv_table, direction)
        summed = summed + apply_along(metric[direction] * gradient, deriv_table.T, direction)
    return summed


def assemble(padded, offset):
    result = padded
    for direction in range(3):
        length = result.shape[direction]
        view_shape = [1, 1, 1]
        view_shape[direction] = length
        node_index = ((jnp.arange(length) - offset) % 8).reshape(view_shape)
        edge_zero = jnp.zeros_like(lax.slice_in_dim(result, 0, 1, axis=direction))
        upward = jnp.concatenate(
            [lax.slice_in_dim(result, 1, length, axis=direction), edge_zero], axis=direction
        )
        downward = jnp.concatenate(
            [edge_zero, lax.slice_in_dim(result, 0, length - 1, axis=direction)], axis=direction
        )
        result = (
            result
            + jnp.where(node_index == 7, upward, 0.0)
            + jnp.where(node_index == 0, downward, 0.0)
        )
    return result


def extend_axis(padded, direction):
    shifted = jnp.moveaxis(padded, direction, 0)
    blocks = (shifted.shape[0] - 4) // 8
    trailing = shifted.shape[1:]
    middle = shifted[2:-2].reshape((blocks, 8) + trailing)
    lowest = shifted[0 : 8 * blocks : 8][:, None]
    beyond = shifted[11::8][:, None]
    joined = jnp.concatenate([lowest, middle, beyond], axis=1).reshape((blocks * 10,) + trailing)
    return jnp.moveaxis(joined, 0, direction)


def widen(padded):
    return extend_axis(extend_axis(extend_axis(padded, 0), 1), 2)


def fast_solve(extended, eigenvectors, eigenvalues):
    count_x, count_y, count_z = eigenvectors.shape[3:]
    precise = lax.Precision.HIGHEST
    spectral = extended.reshape(count_x, 10, count_y, 10, count_z, 10)
    spectral = jnp.einsum("apxyz,xaybzc->xpybzc", eigenvectors[0], spectral, precision=precise)
    spectral = jnp.einsum("bqxyz,xpybzc->xpyqzc", eigenvectors[1], spectral, precision=precise)
    spectral = jnp.einsum("csxyz,xpyqzc->xpyqzs", eigenvectors[2], spectral, precision=precise)
    rate_x = jnp.transpose(eigenvalues[0], (1, 0, 2, 3))[:, :, :, None, :, None]
    rate_y = jnp.transpose(eigenvalues[1], (1, 2, 0, 3))[:, None, :, :, :, None]
    rate_z = jnp.transpose(eigenvalues[2], (1, 2, 3, 0))[:, None, :, None, :, :]
    spectral = spectral / (rate_x + rate_y + rate_z)
    spectral = jnp.einsum("csxyz,xpyqzs->xpyqzc", eigenvectors[2], spectral, precision=precise)
    spectral = jnp.einsum("bqxyz,xpyqzc->xpybzc", eigenvectors[1], spectral, precision=precise)
    spectral = jnp.einsum("apxyz,xpybzc->xaybzc", eigenvectors[0], spectral, precision=precise)
    return spectral.reshape(count_x * 10, count_y * 10, count_z * 10)


def return_axis(padded, direction):
    shifted = jnp.moveaxis(padded, direction, 0)
    blocks = (shifted.shape[0] - 4) // 10
    trailing = shifted.shape[1:]
    owned = shifted[2:-2].reshape((blocks, 10) + trailing)[:, 1:9]
    before = shifted[0 : 10 * blocks].reshape((blocks, 10) + trailing)[:, 0:2]
    following = shifted[4:].reshape((blocks, 10) + trailing)[:, 8:10]
    middle = jnp.zeros((blocks, 4) + trailing, shifted.dtype)
    summed = owned + jnp.concatenate([before, middle, following], axis=1)
    return jnp.moveaxis(summed.reshape((blocks * 8,) + trailing), 0, direction)


def general_body(initial, source, metric, eigenvectors, eigenvalues):
    solution = initial
    local_res = source - apply_operator(solution, metric)
    deeper = extended_2(local_res, (("gx", 0), ("gy", 1), ("gz", 2)), 2)
    widened = assemble(deeper, 2)
    extended = widen(widened)
    corrected = fast_solve(extended, eigenvectors, eigenvalues)
    padded = extended_2(corrected, (("gx", 0), ("gy", 1), ("gz", 2)), 2)
    correction = return_axis(return_axis(return_axis(padded, 0), 1), 2)
    solution = solution + correction
    return solution


AXES = ("gx", "gy", "gz")
VMEM = pl.BlockSpec(memory_space=pltpu.VMEM)
HBM = pl.BlockSpec(memory_space=pltpu.HBM)
VMEM_LIMIT = 16 * 2**20
f32 = jnp.float32
bf16 = jnp.bfloat16


def call(kernel, outs, args, scratch=(), where=VMEM):
    moved = sum(int(np.prod(a.shape)) * a.dtype.itemsize for a in (*args, *outs))
    return pl.pallas_call(
        kernel,
        out_shape=outs,
        in_specs=[where] * len(args),
        out_specs=[VMEM] * len(outs),
        scratch_shapes=scratch,
        compiler_params=pltpu.CompilerParams(vmem_limit_bytes=VMEM_LIMIT),
        cost_estimate=pl.CostEstimate(flops=0, bytes_accessed=moved, transcendentals=0),
    )(*args)


def shaped(shape, dtype=f32):
    return jax.ShapeDtypeStruct(shape, dtype)


def counted(shape, axis):
    return lax.broadcasted_iota(jnp.int32, shape, axis)


def split2(value):
    high = value.astype(bf16)
    return high, (value - high.astype(f32)).astype(bf16)


def split3(value):
    high = value.astype(bf16)
    rest = value - high.astype(f32)
    middle = rest.astype(bf16)
    return high, middle, (rest - middle.astype(f32)).astype(bf16)


def dot(left, right, transposed=False):
    dims = (((1,), (1 if transposed else 0,)), ((), ()))
    return lax.dot_general(left, right, dims, preferred_element_type=f32)


def repeated_table(table, width):
    nodes = table.shape[0]
    row, column = counted((nodes, width), 0), counted((nodes, width), 1) % nodes
    tile = jnp.zeros((nodes, width), f32)
    for j in range(nodes):
        values = jnp.zeros((nodes, width), f32)
        for i in range(nodes):
            values = jnp.where(row == i, float(table[i, j]), values)
        tile = jnp.where(column == j, values, tile)
    return tile


def residual_kernel(
    u_hbm, source_hbm, metric_hbm, val_hbm, out_ref, u_ref, source_ref, metric_ref, val_ref, sems
):
    copies = [pltpu.make_async_copy(u_hbm, u_ref, sems.at[0])]
    copies += [
        pltpu.make_async_copy(metric_hbm.at[d], metric_ref.at[d], sems.at[1 + d])
        for d in range(metric_hbm.shape[0])
    ]
    copies.append(pltpu.make_async_copy(source_hbm, source_ref, sems.at[len(copies)]))
    copies.append(pltpu.make_async_copy(val_hbm, val_ref, sems.at[len(copies)]))
    for copy in copies:
        copy.start()
    nodes, rows, width = u_ref.shape
    flat_rows = nodes * rows
    table = np.asarray(derivative_table(), np.float32)
    along_y, along_z = [], []
    for t in range(2):
        tile = repeated_table(table if t == 0 else table.T, width)
        high = tile.astype(bf16).astype(f32)
        low = tile - high
        group = counted((nodes, width), 1) // nodes
        zero = jnp.zeros_like(tile)
        for part in (high, low):
            bands = [jnp.where(group == k, part, zero) for k in range(width // nodes)]
            along_z.append(jnp.concatenate(bands, axis=0).astype(bf16))
        group = group[:, 0 : 2 * flat_rows]
        high, low, zero = (v[:, 0 : 2 * flat_rows] for v in (high, low, zero))
        bands = [jnp.where(group % rows == k, high, zero) for k in range(nodes)]
        bands += [jnp.where(group == k, low, zero) for k in range(nodes)]
        along_y.append(jnp.concatenate(bands, axis=0).astype(bf16))

    def by_y(value, t):
        both = dot(along_y[t], jnp.concatenate(split2(value), axis=0))
        return both[0:flat_rows] + both[flat_rows:]

    def by_z(value, t):
        high, low = split2(value)
        both = dot(jnp.concatenate([high, low], axis=0), along_z[2 * t])
        return both[0:flat_rows] + (both[flat_rows:] + dot(high, along_z[2 * t + 1]))

    copies[0].wait()
    flat = u_ref[...].reshape(flat_rows, width)
    flux_y, flux_z = by_y(flat, 0), by_z(flat, 1)
    layers = [u_ref[j] for j in range(nodes)]
    flux_x = [sum(float(table[i, j]) * layers[j] for j in range(nodes)) for i in range(nodes)]
    for copy in copies[1:]:
        copy.wait()
    total = by_y(flux_y * metric_ref[1].reshape(flat.shape), 1)
    total = total + by_z(flux_z * metric_ref[2].reshape(flat.shape), 0)
    total = total.reshape(nodes, rows, width)
    flux_x = [metric_ref[0, i] * flux_x[i] for i in range(nodes)]
    for j in range(nodes):
        applied = sum(float(table[i, j]) * flux_x[i] for i in range(nodes))
        out_ref[j] = source_ref[j] - (applied + total[j])
    count, _, blocks = val_ref.shape
    values = val_ref[...].reshape(count, blocks)
    for first in range(0, count, rows):
        last = min(first + rows, count)
        out_ref[nodes + first // rows, 0 : last - first, 0:blocks] = values[first:last]


def layers_kernel(own_ref, partner_ref, out_ref):
    start = lax.axis_index("gz") * (out_ref.shape[2] - 2)
    for half, ref in enumerate((partner_ref, own_ref)):
        for layer in range(2):
            out_ref[half, layer] = ref[start + layer]


def taken(ref, first, count):
    return ref[first : first + count].reshape(count, ref.shape[2])


def spread(own, partner, ext):
    blocks = own.shape[1]
    parts = [*split3(own), *split3(partner)]
    shape = (blocks, 2 * blocks * ext)
    repeat = []
    for half in range(2):
        element = counted(shape, 1) // ext - half * blocks
        repeat += [(element == counted(shape, 0)).astype(f32).astype(bf16)] * 3
    return dot(jnp.concatenate(parts, axis=1), jnp.concatenate(repeat, axis=0))


def gathered(choice, value):
    choice = choice.astype(f32).astype(bf16)
    high, middle, low = split3(value)
    return dot(choice, high) + (dot(choice, middle) + dot(choice, low))


def x_coefficients_kernel(
    own_vec, partner_vec, own_ref, partner_ref, after_ref, cx_ref, cx_rows_ref, rate_ref
):
    ext, padded, lanes = rate_ref.shape
    blocks = own_vec.shape[2]
    nodes = ext - 2
    square = ext * ext
    along_x = spread(taken(own_vec, 0, square), taken(partner_vec, 0, square), ext)
    cx_ref[...] = along_x
    shape = (cx_rows_ref.shape[0], square)
    place = counted(shape, 0) % (shape[0] // ext) // 2
    choice = (place < ext) & (counted(shape, 1) == place * ext + counted(shape, 0) // (shape[0] // ext))
    cx_rows_ref[...] = gathered(choice, along_x)
    rates = []
    for ref in (own_ref, partner_ref):
        tiles = ref[nodes : ref.shape[0]]
        rates.append(tiles.reshape(-1, tiles.shape[2])[0 : 3 * ext, 0:blocks])
    rates = spread(*rates, ext)
    shape = (ext, lanes)
    rate_z = rates[2 * ext : 3 * ext]
    same = counted(shape, 0) == counted(shape, 1) % ext
    rate_z = jnp.sum(jnp.where(same, rate_z, jnp.zeros_like(rate_z)), axis=0, keepdims=True)
    rate_y = jnp.concatenate([rates[ext : 2 * ext], jnp.ones((padded - ext, lanes), f32)], axis=0)
    for p in range(ext):
        rate_ref[p] = 1.0 / (rates[p : p + 1] + rate_y + rate_z)


def y_coefficients_kernel(own_vec, partner_vec, after_ref, cy_ref):
    ext, padded = cy_ref.shape[1:3]
    square = ext * ext
    along_y = spread(taken(own_vec, square, square), taken(partner_vec, square, square), ext)
    shape = (ext * padded, square)
    first, second, entry = counted(shape, 0) // padded, counted(shape, 0) % padded, counted(shape, 1)
    forward = (second < ext) & (entry == first * ext + second)
    position = jnp.where(second < ext - 2, second + 1, jnp.where(second == ext - 2, 0, ext - 1))
    backward = (second < ext) & (entry == position * ext + first)
    for k, choice in enumerate((forward, backward)):
        cy_ref[k] = gathered(choice, along_y).reshape(cy_ref.shape[1:])


def z_coefficients_kernel(own_vec, partner_vec, after_ref, mz_ref):
    blocks = own_vec.shape[2]
    lanes = mz_ref.shape[2]
    half = lanes // 2
    ext = half // blocks
    square = ext * ext
    nodes = ext - 2
    core = lax.axis_index("gz")
    shape = (square, lanes)
    same = counted(shape, 0) % ext == counted(shape, 1) % ext
    along_z = spread(
        taken(own_vec, 2 * square, square), taken(partner_vec, 2 * square, square), ext
    )
    along_z = jnp.where(same, along_z, jnp.zeros_like(along_z))
    shape = (ext, square)
    along_z = gathered(counted(shape, 1) // ext == counted(shape, 0), along_z)

    zeros = jnp.zeros((nodes - 2, lanes), f32)
    own = along_z[1 : nodes + 1]
    below = jnp.concatenate([zeros, along_z[0:2]], axis=0)
    above = jnp.concatenate([along_z[nodes : nodes + 2], zeros], axis=0)
    lane = counted((nodes, lanes), 1)
    first_own = core * blocks
    first_partner = blocks - first_own
    element = jnp.where(lane < half, lane // ext + first_own, (lane - half) // ext + first_partner)
    zero = jnp.zeros_like(own)
    for place in range(0, 2 * blocks, 2):
        first = place + first_own if place < blocks else place - blocks + first_partner
        pair = []
        for block in (first, first + 1):
            value = jnp.where(element == block, own, zero)
            value = value + jnp.where(element == block + 1, below, zero)
            pair.append(value + jnp.where(element == block - 1, above, zero))
        high, low = split2(jnp.concatenate(pair, axis=0))
        mz_ref[0, place * nodes : (place + 2) * nodes, :] = high
        mz_ref[1, place * nodes : (place + 2) * nodes, :] = low


def trade_cores(axis, place, other):
    if axis == "gx":
        return (place % 2, place % 2)
    return (0, 1) if other % 2 == 0 else (1, 0)


def trades_below():
    return lax.axis_index("gz") != lax.axis_index("gx") % 2


def sides(below, direct, passed):
    low = [jnp.where(below, direct[h], passed[1 - h]) for h in range(2)]
    high = [jnp.where(below, passed[1 - h], direct[h]) for h in range(2)]
    return low, high


def edges(axis):
    place, size = lax.axis_index(axis), lax.axis_size(axis)
    return place > 0, place < size - 1


def layers_kernel(own_ref, partner_ref, out_ref):
    start = jnp.where(trades_below(), 0, out_ref.shape[2] - 2)
    for half, ref in enumerate((own_ref, partner_ref)):
        for layer in range(2):
            out_ref[half, layer] = ref[start + layer]


def x_positions(own_ref, partner_ref, direct_ref, passed_ref):
    has_low, has_high = edges("gx")
    length = own_ref.shape[1]
    below = trades_below()
    outer = []
    for slot in range(2):
        direct = [direct_ref[h, slot] for h in range(2)]
        passed = [passed_ref[h, slot] for h in range(2)]
        low, high = sides(below, direct, passed)
        low = [jnp.where(has_low, v, jnp.zeros_like(v)) for v in low]
        high = [jnp.where(has_high, v, jnp.zeros_like(v)) for v in high]
        outer.append((low, high))
    positions = [outer[0][0]]
    for layer in range(length):
        value = [own_ref[layer], partner_ref[layer]]
        if layer == 0:
            value = [v + w for v, w in zip(outer[1][0], value)]
        if layer == length - 1:
            value = [v + w for v, w in zip(value, outer[0][1])]
        positions.append(value)
    return positions + [outer[1][1]]


def rows_kernel(own_ref, partner_ref, direct_ref, passed_ref, after_ref, out_ref):
    _, rows, width = own_ref.shape
    below = trades_below()
    positions = x_positions(own_ref, partner_ref, direct_ref, passed_ref)
    out_ref[out_ref.shape[0] - 1] = jnp.zeros(out_ref.shape[1:], f32)
    for a, (own, partner) in enumerate(positions):
        row = 2 * a % rows
        for half, value in enumerate((partner, own)):
            out_ref[2 * a // rows, row : row + 2, half * width : (half + 1) * width] = jnp.where(
                below, value[0:2], value[rows - 2 : rows]
            )


def by_parts(value, mz, transposed):
    rows = value.shape[0]
    spare = -rows % 16
    if spare:
        value = jnp.concatenate([value, jnp.zeros((spare, value.shape[1]), f32)], axis=0)
    high, low = split2(value)
    both = dot(jnp.concatenate([high, low], axis=0), mz[0], transposed)
    total = both[0 : rows + spare] + (both[rows + spare :] + dot(high, mz[1], transposed))
    return total[0:rows]


def by_z(value, mz):
    return by_parts(value, mz, False)


def back_by_z(value, mz):
    return by_parts(value, mz, True)


def from_rows(value, use, mz, cx_rows, ext):
    count, rows, both = value.shape
    value = jnp.where(use, value, jnp.zeros_like(value))
    along_z = by_z(value.reshape(count * rows, both), mz)
    for p in range(ext):
        total = sum(
            cx_rows[(p * count + t) * rows : (p * count + t + 1) * rows, :]
            * along_z[t * rows : (t + 1) * rows]
            for t in range(count)
        )
        shift = 2
        while shift < rows:
            total = total + pltpu.roll(total, shift, 0)
            shift *= 2
        yield total


def interior_solve_kernel(
    own_ref, partner_ref, xd_ref, xp_ref, yd_ref, cx, cx_rows, cy, mz, out_ref, grid
):
    _, rows, width = own_ref.shape
    ext, padded, lanes = out_ref.shape
    nodes = ext - 2
    has_low, has_high = edges("gy")
    positions = x_positions(own_ref, partner_ref, xd_ref, xp_ref)
    for a, halves in enumerate(positions):
        for half, value in enumerate(halves):
            grid[a, :, half * width : (half + 1) * width] = value
    along_z = by_z(grid[...].reshape(ext * rows, 2 * width), mz)
    along_z = along_z.reshape(ext, rows, lanes)
    below = trades_below()
    use = jnp.where(below, has_low, has_high)
    outer = [cy[0, jnp.where(below, 0, nodes) + k] for k in range(2)]
    for p, value in enumerate(from_rows(yd_ref[...], use, mz, cx_rows, ext)):
        inner = sum(cx[a * ext + p : a * ext + p + 1, :] * along_z[a] for a in range(ext))
        total = sum(cy[0, b + 1] * inner[b : b + 1] for b in range(rows))
        out_ref[p] = total + sum(outer[k] * value[k : k + 1] for k in range(2))


def back_by_x(spectral, coefficients):
    return sum(c * spectral[p] for p, c in enumerate(coefficients))


def back_by_y(value, cy, ext):
    return sum(cy[1, q] * value[q : q + 1] for q in range(ext))


def solve_kernel(yp_ref, part_ref, cx, cx_rows, cy, rate, mz, spectral, sent_ref):
    below = trades_below()
    width = yp_ref.shape[2] // 2
    ext, padded, lanes = rate.shape
    nodes = ext - 2
    has_low, has_high = edges("gy")
    passed = jnp.concatenate([yp_ref[:, :, width:], yp_ref[:, :, 0:width]], axis=2)
    use = jnp.where(below, has_high, has_low)
    outer = [cy[0, jnp.where(below, nodes, 0) + k] for k in range(2)]
    for p, value in enumerate(from_rows(passed, use, mz, cx_rows, ext)):
        total = part_ref[p] + sum(outer[k] * value[k : k + 1] for k in range(2))
        spectral[p] = total * rate[p]
    layers = []
    for layer in range(2):
        rows = [layer * ext + p for p in range(ext)]
        last = [r + nodes * ext for r in rows]
        coefficients = [
            jnp.where(trades_below(), cx[r : r + 1, :], cx[k : k + 1, :])
            for r, k in zip(rows, last)
        ]
        layers.append(back_by_y(back_by_x(spectral, coefficients), cy, ext))
    result = back_by_z(jnp.concatenate(layers, axis=0), mz)
    for layer in range(2):
        for half in range(2):
            lanes_at = slice(half * width, (half + 1) * width)
            place = half * 2 + layer
            value = result[layer * padded : layer * padded + nodes + 2, lanes_at]
            sent_ref[place] = value[0:nodes]
            sent_ref[4, 2 * place : 2 * place + 2, :] = value[nodes : nodes + 2]


def interior_kernel(spectral, cx, cy, mz, after_ref, out_ref):
    ext, padded, lanes = spectral.shape
    nodes, _, both = out_ref.shape
    layers = []
    for a in range(1, ext - 1):
        coefficients = [cx[a * ext + p : a * ext + p + 1, :] for p in range(ext)]
        layers.append(back_by_y(back_by_x(spectral, coefficients), cy, ext))
    result = back_by_z(jnp.concatenate(layers, axis=0), mz)
    out_ref[...] = result.reshape(nodes, padded, both)


def return_rows_kernel(initial_ref, inner_ref, direct_ref, passed_ref, out_ref, base_ref):
    has_low, has_high = edges("gx")
    below_x, below_y = trades_below(), trades_below()
    nodes, rows, width = initial_ref.shape
    for layer in range(nodes):
        lanes = [slice(0, width), slice(width, 2 * width)]
        outer = [inner_ref[layer, rows : rows + 2, lanes[h]] for h in range(2)]
        values = [inner_ref[layer, 0:rows, lanes[h]] for h in range(2)]
        if layer < 2 or layer >= nodes - 2:
            slot = layer if layer < 2 else layer - (nodes - 2)

            def parts(ref, h, slot=slot):
                place = 2 * h + slot
                return ref[place], ref[4, 2 * place : 2 * place + 2, :]

            direct = [parts(direct_ref, h) for h in range(2)]
            passed = [parts(passed_ref, h) for h in range(2)]
            side = 0 if layer < 2 else 1
            valid = (has_low, has_high)[side]
            for k, target in enumerate((values, outer)):
                both = sides(below_x, [d[k] for d in direct], [d[k] for d in passed])[side]
                for h in range(2):
                    target[h] = target[h] + jnp.where(valid, both[h], jnp.zeros_like(both[h]))
        base_ref[layer] = initial_ref[layer] + values[0]
        for place, h in enumerate((1, 0)):
            first = jnp.where(below_y, outer[h][0:1], values[h][rows - 1 : rows])
            second = jnp.where(below_y, values[h][0:1], outer[h][1:2])
            out_ref[layer, :, lanes[place]] = jnp.concatenate([first, second], axis=0)


def result_kernel(base_ref, direct_ref, passed_ref, out_ref):
    below = trades_below()
    has_low, has_high = edges("gy")
    nodes, rows, width = base_ref.shape
    for layer in range(nodes):
        direct = direct_ref[layer, :, 0:width]
        passed = passed_ref[layer, :, width:]
        low = jnp.where(below, direct, passed)
        high = jnp.where(below, passed, direct)
        low = jnp.where(has_low, low, jnp.zeros_like(low))
        high = jnp.where(has_high, high, jnp.zeros_like(high))
        between = jnp.zeros((rows - 4, low.shape[1]), f32)
        out_ref[layer] = base_ref[layer] + jnp.concatenate([low, between, high], axis=0)


def swap_pairs(axis):
    sizes = [lax.axis_size(name) for name in AXES]
    along, across = (0, 1) if axis == "gx" else (1, 0)

    def number(place, other, core):
        spot = (place, other) if along == 0 else (other, place)
        return (spot[0] * sizes[1] + spot[1]) * 2 + core

    pairs, idle = [], []
    last = sizes[along] - 1
    for other in range(sizes[across]):
        spare = {(place, core) for place in (0, last) for core in range(2)}
        for place in range(last):
            here, there = trade_cores(axis, place, other)
            spare -= {(place, here), (place + 1, there)}
            here, there = number(place, other, here), number(place + 1, other, there)
            pairs += [(here, there), (there, here)]
        idle.append([number(place, other, core) for place, core in sorted(spare)])
    for one, two in zip(idle[0::2], idle[1::2]):
        for here, there in zip(one, two):
            pairs += [(here, there), (there, here)]
    return pairs


def swap(value, axis):
    if axis == "gz":
        return lax.ppermute(value, "gz", [(0, 1), (1, 0)])
    return lax.ppermute(value, AXES, swap_pairs(axis))


def paired_body(initial, source, metric, eigenvectors, eigenvalues):
    nodes, rows, width = initial.shape
    ext = eigenvectors.shape[1]
    blocks = width // nodes
    lanes = 2 * blocks * ext
    padded = 2 * rows
    vectors = eigenvectors.reshape(3 * ext * ext, 1, blocks)
    values = eigenvalues.reshape(3 * ext, 1, blocks)
    inputs = [
        pltpu.with_memory_space_constraint(value, pltpu.HBM)
        for value in (initial, source, metric, values)
    ]
    own = call(
        residual_kernel,
        [shaped((nodes + -(-3 * ext // rows), rows, width))],
        inputs,
        scratch=[
            *(pltpu.VMEM(value.shape, value.dtype) for value in inputs),
            pltpu.SemaphoreType.DMA((3 + metric.shape[0],)),
        ],
        where=HBM,
    )[0]
    partner = swap(own, "gz")
    vectors, own = lax.optimization_barrier((vectors, own))
    partner_vectors = swap(vectors, "gz")
    sent = call(layers_kernel, [shaped((2, 2, rows, width))], [own, partner])[0]
    x_direct = swap(sent, "gx")
    tiles = -(-2 * ext // rows)
    cx, cx_rows, rate = call(
        x_coefficients_kernel,
        [
            shaped((ext * ext, lanes)),
            shaped((ext * tiles * rows, lanes)),
            shaped((ext, padded, lanes)),
        ],
        [vectors, partner_vectors, own, partner, sent],
    )
    x_direct, cx, rate = lax.optimization_barrier((x_direct, cx, rate))
    x_passed = swap(x_direct, "gz")
    mz = call(
        z_coefficients_kernel,
        [shaped((2, 2 * width, lanes), bf16)],
        [vectors, partner_vectors, x_direct],
    )[0]
    sent = call(
        rows_kernel,
        [shaped((tiles, rows, 2 * width))],
        [own, partner, x_direct, x_passed, mz],
    )[0]
    y_direct = swap(sent, "gy")
    cy = call(
        y_coefficients_kernel,
        [shaped((2, ext, padded, lanes))],
        [vectors, partner_vectors, sent],
    )[0]
    y_direct, cy = lax.optimization_barrier((y_direct, cy))
    y_passed = swap(y_direct, "gz")
    part = call(
        interior_solve_kernel,
        [shaped((ext, padded, lanes))],
        [own, partner, x_direct, x_passed, y_direct, cx, cx_rows, cy, mz],
        scratch=[pltpu.VMEM((ext, rows, 2 * width), f32)],
    )[0]
    spectral, sent = call(
        solve_kernel,
        [shaped((ext, padded, lanes)), shaped((5, rows, width))],
        [y_passed, part, cx, cx_rows, cy, rate, mz],
    )

    x_direct = swap(sent, "gx")
    inner = call(interior_kernel, [shaped((nodes, padded, 2 * width))], [spectral, cx, cy, mz, sent])[0]
    x_passed = swap(x_direct, "gz")
    sent, base = call(
        return_rows_kernel,
        [shaped((nodes, 2, 2 * width)), shaped(initial.shape)],
        [initial, inner, x_direct, x_passed],
    )
    y_direct = swap(sent, "gy")
    y_passed = swap(y_direct, "gz")
    return call(result_kernel, [shaped(initial.shape)], [base, y_direct, y_passed])[0]


def body(initial, source, metric, eigenvectors, eigenvalues):
    nodes = gll_points.shape[0]
    one_element = initial.shape[0] == nodes and initial.shape[1] == nodes
    if lax.axis_size("gz") == 2 and one_element and initial.shape[2] % 128 == 0:
        return paired_body(initial, source, metric, eigenvectors, eigenvalues)
    return general_body(initial, source, metric, eigenvectors, eigenvalues)


def solution(mesh):
    placed = (
        P("gx", "gy", "gz"),
        P("gx", "gy", "gz"),
        P(None, "gx", "gy", "gz"),
        P(None, None, None, "gx", "gy", "gz"),
        P(None, None, "gx", "gy", "gz"),
    )
    return jax.shard_map(
        body, mesh=mesh, in_specs=placed, out_specs=P("gx", "gy", "gz"), check_vma=False
    )
```

```python
import functools

import jax
import jax.numpy as jnp
import numpy as np
from jax import lax
from jax.experimental import pallas as pl
from jax.experimental.pallas import tpu as pltpu
from jax.sharding import PartitionSpec as P

gll_points = np.array(
    [
        -1.0,
        -0.8717401485096066,
        -0.5917001814331423,
        -0.2092992179024789,
        0.2092992179024789,
        0.5917001814331423,
        0.8717401485096066,
        1.0,
    ]
)


def extended_2(value, sides, width):
    for axis, dim in sides:
        size, length = (lax.axis_size(axis), value.shape[dim])
        up = [(i, (i + 1) % size) for i in range(size - 1)]
        down = [(j, i) for i, j in up]
        last = lax.slice_in_dim(value, length - width, length, axis=dim)
        first = lax.slice_in_dim(value, 0, width, axis=dim)
        before = lax.ppermute(last, axis, up)
        after = lax.ppermute(first, axis, down)
        value = jnp.concatenate([before, value, after], axis=dim)
    return value


def derivative_table():
    number = gll_points.shape[0]
    products = np.array(
        [
            np.prod(
                [
                    gll_points[row_index] - gll_points[other]
                    for other in range(number)
                    if other != row_index
                ]
            )
            for row_index in range(number)
        ]
    )
    matrix_out = np.zeros((number, number))
    for row_index in range(number):
        for col_index in range(number):
            if row_index != col_index:
                matrix_out[row_index, col_index] = (
                    products[row_index]
                    / products[col_index]
                    / (gll_points[row_index] - gll_points[col_index])
                )
        matrix_out[row_index, row_index] = -np.sum(matrix_out[row_index])
    return matrix_out


def apply_along(values, matrix, direction):
    block_size = matrix.shape[1]
    old_shape = values.shape
    pieces_shape = (
        old_shape[:direction]
        + (old_shape[direction] // block_size, block_size)
        + old_shape[direction + 1 :]
    )
    result = jnp.tensordot(
        values.reshape(pieces_shape),
        matrix,
        axes=((direction + 1,), (1,)),
        precision=lax.Precision.HIGHEST,
    )
    result = jnp.moveaxis(result, -1, direction + 1)
    return result.reshape(
        old_shape[:direction]
        + (old_shape[direction] // block_size * matrix.shape[0],)
        + old_shape[direction + 1 :]
    )


def apply_operator(values, metric):
    deriv_table = jnp.asarray(derivative_table(), jnp.float32)
    summed = jnp.zeros_like(values)
    for direction in range(3):
        gradient = apply_along(values, deriv_table, direction)
        summed = summed + apply_along(metric[direction] * gradient, deriv_table.T, direction)
    return summed


def assemble(padded, offset):
    result = padded
    for direction in range(3):
        length = result.shape[direction]
        view_shape = [1, 1, 1]
        view_shape[direction] = length
        node_index = ((jnp.arange(length) - offset) % 8).reshape(view_shape)
        edge_zero = jnp.zeros_like(lax.slice_in_dim(result, 0, 1, axis=direction))
        upward = jnp.concatenate(
            [lax.slice_in_dim(result, 1, length, axis=direction), edge_zero], axis=direction
        )
        downward = jnp.concatenate(
            [edge_zero, lax.slice_in_dim(result, 0, length - 1, axis=direction)], axis=direction
        )
        result = (
            result
            + jnp.where(node_index == 7, upward, 0.0)
            + jnp.where(node_index == 0, downward, 0.0)
        )
    return result


def extend_axis(padded, direction):
    shifted = jnp.moveaxis(padded, direction, 0)
    blocks = (shifted.shape[0] - 4) // 8
    trailing = shifted.shape[1:]
    middle = shifted[2:-2].reshape((blocks, 8) + trailing)
    lowest = shifted[0 : 8 * blocks : 8][:, None]
    beyond = shifted[11::8][:, None]
    joined = jnp.concatenate([lowest, middle, beyond], axis=1).reshape((blocks * 10,) + trailing)
    return jnp.moveaxis(joined, 0, direction)


def widen(padded):
    return extend_axis(extend_axis(extend_axis(padded, 0), 1), 2)


def fast_solve(extended, eigenvectors, eigenvalues):
    count_x, count_y, count_z = eigenvectors.shape[3:]
    precise = lax.Precision.HIGHEST
    spectral = extended.reshape(count_x, 10, count_y, 10, count_z, 10)
    spectral = jnp.einsum("apxyz,xaybzc->xpybzc", eigenvectors[0], spectral, precision=precise)
    spectral = jnp.einsum("bqxyz,xpybzc->xpyqzc", eigenvectors[1], spectral, precision=precise)
    spectral = jnp.einsum("csxyz,xpyqzc->xpyqzs", eigenvectors[2], spectral, precision=precise)
    rate_x = jnp.transpose(eigenvalues[0], (1, 0, 2, 3))[:, :, :, None, :, None]
    rate_y = jnp.transpose(eigenvalues[1], (1, 2, 0, 3))[:, None, :, :, :, None]
    rate_z = jnp.transpose(eigenvalues[2], (1, 2, 3, 0))[:, None, :, None, :, :]
    spectral = spectral / (rate_x + rate_y + rate_z)
    spectral = jnp.einsum("csxyz,xpyqzs->xpyqzc", eigenvectors[2], spectral, precision=precise)
    spectral = jnp.einsum("bqxyz,xpyqzc->xpybzc", eigenvectors[1], spectral, precision=precise)
    spectral = jnp.einsum("apxyz,xpybzc->xaybzc", eigenvectors[0], spectral, precision=precise)
    return spectral.reshape(count_x * 10, count_y * 10, count_z * 10)


def return_axis(padded, direction):
    shifted = jnp.moveaxis(padded, direction, 0)
    blocks = (shifted.shape[0] - 4) // 10
    trailing = shifted.shape[1:]
    owned = shifted[2:-2].reshape((blocks, 10) + trailing)[:, 1:9]
    before = shifted[0 : 10 * blocks].reshape((blocks, 10) + trailing)[:, 0:2]
    following = shifted[4:].reshape((blocks, 10) + trailing)[:, 8:10]
    middle = jnp.zeros((blocks, 4) + trailing, shifted.dtype)
    summed = owned + jnp.concatenate([before, middle, following], axis=1)
    return jnp.moveaxis(summed.reshape((blocks * 8,) + trailing), 0, direction)


def general_body(initial, source, metric, eigenvectors, eigenvalues):
    solution = initial
    local_res = source - apply_operator(solution, metric)
    deeper = extended_2(local_res, (("gx", 0), ("gy", 1), ("gz", 2)), 2)
    widened = assemble(deeper, 2)
    extended = widen(widened)
    corrected = fast_solve(extended, eigenvectors, eigenvalues)
    padded = extended_2(corrected, (("gx", 0), ("gy", 1), ("gz", 2)), 2)
    correction = return_axis(return_axis(return_axis(padded, 0), 1), 2)
    solution = solution + correction
    return solution


AXES = ("gx", "gy", "gz")
VMEM = pl.BlockSpec(memory_space=pltpu.VMEM)
HBM = pl.BlockSpec(memory_space=pltpu.HBM)
VMEM_LIMIT = 16 * 2**20
f32 = jnp.float32
bf16 = jnp.bfloat16


def call(kernel, outs, args, scratch=(), where=VMEM):
    moved = sum(int(np.prod(a.shape)) * a.dtype.itemsize for a in (*args, *outs))
    return pl.pallas_call(
        kernel,
        out_shape=outs,
        in_specs=[where] * len(args),
        out_specs=[VMEM] * len(outs),
        scratch_shapes=scratch,
        compiler_params=pltpu.CompilerParams(vmem_limit_bytes=VMEM_LIMIT),
        cost_estimate=pl.CostEstimate(flops=0, bytes_accessed=moved, transcendentals=0),
    )(*args)


def shaped(shape, dtype=f32):
    return jax.ShapeDtypeStruct(shape, dtype)


def counted(shape, axis):
    return lax.broadcasted_iota(jnp.int32, shape, axis)


def split2(value):
    high = value.astype(bf16)
    return high, (value - high.astype(f32)).astype(bf16)


def split3(value):
    high = value.astype(bf16)
    rest = value - high.astype(f32)
    middle = rest.astype(bf16)
    return high, middle, (rest - middle.astype(f32)).astype(bf16)


def dot(left, right):
    return jnp.dot(left, right, preferred_element_type=f32)


def repeated_table(table, width):
    nodes = table.shape[0]
    row, column = counted((nodes, width), 0), counted((nodes, width), 1) % nodes
    tile = jnp.zeros((nodes, width), f32)
    for j in range(nodes):
        values = jnp.zeros((nodes, width), f32)
        for i in range(nodes):
            values = jnp.where(row == i, float(table[i, j]), values)
        tile = jnp.where(column == j, values, tile)
    return tile


def residual_kernel(
    u_hbm, source_hbm, metric_hbm, val_hbm, out_ref, u_ref, source_ref, metric_ref, val_ref, sems
):
    copies = [pltpu.make_async_copy(u_hbm, u_ref, sems.at[0])]
    copies += [
        pltpu.make_async_copy(metric_hbm.at[d], metric_ref.at[d], sems.at[1 + d])
        for d in range(metric_hbm.shape[0])
    ]
    copies.append(pltpu.make_async_copy(source_hbm, source_ref, sems.at[len(copies)]))
    copies.append(pltpu.make_async_copy(val_hbm, val_ref, sems.at[len(copies)]))
    for copy in copies:
        copy.start()
    nodes, rows, width = u_ref.shape
    flat_rows = nodes * rows
    table = np.asarray(derivative_table(), np.float32)
    along_y, along_z = [], []
    for t in range(2):
        tile = repeated_table(table if t == 0 else table.T, width)
        high = tile.astype(bf16).astype(f32)
        low = tile - high
        group = counted((nodes, width), 1) // nodes
        zero = jnp.zeros_like(tile)
        for part in (high, low):
            bands = [jnp.where(group == k, part, zero) for k in range(width // nodes)]
            along_z.append(jnp.concatenate(bands, axis=0).astype(bf16))
        group = group[:, 0 : 2 * flat_rows]
        high, low, zero = (v[:, 0 : 2 * flat_rows] for v in (high, low, zero))
        bands = [jnp.where(group % rows == k, high, zero) for k in range(nodes)]
        bands += [jnp.where(group == k, low, zero) for k in range(nodes)]
        along_y.append(jnp.concatenate(bands, axis=0).astype(bf16))

    def by_y(value, t):
        both = dot(along_y[t], jnp.concatenate(split2(value), axis=0))
        return both[0:flat_rows] + both[flat_rows:]

    def by_z(value, t):
        high, low = split2(value)
        both = dot(jnp.concatenate([high, low], axis=0), along_z[2 * t])
        return both[0:flat_rows] + (both[flat_rows:] + dot(high, along_z[2 * t + 1]))

    copies[0].wait()
    flat = u_ref[...].reshape(flat_rows, width)
    flux_y, flux_z = by_y(flat, 0), by_z(flat, 1)
    layers = [u_ref[j] for j in range(nodes)]
    flux_x = [sum(float(table[i, j]) * layers[j] for j in range(nodes)) for i in range(nodes)]
    for copy in copies[1:]:
        copy.wait()
    total = by_y(flux_y * metric_ref[1].reshape(flat.shape), 1)
    total = total + by_z(flux_z * metric_ref[2].reshape(flat.shape), 0)
    total = total.reshape(nodes, rows, width)
    flux_x = [metric_ref[0, i] * flux_x[i] for i in range(nodes)]
    for j in range(nodes):
        applied = sum(float(table[i, j]) * flux_x[i] for i in range(nodes))
        out_ref[j] = source_ref[j] - (applied + total[j])
    count, _, blocks = val_ref.shape
    values = val_ref[...].reshape(count, blocks)
    for first in range(0, count, rows):
        last = min(first + rows, count)
        out_ref[nodes + first // rows, 0 : last - first, 0:blocks] = values[first:last]


def layers_kernel(own_ref, partner_ref, out_ref):
    start = lax.axis_index("gz") * (out_ref.shape[2] - 2)
    for half, ref in enumerate((partner_ref, own_ref)):
        for layer in range(2):
            out_ref[half, layer] = ref[start + layer]


def taken(ref, first, count):
    return ref[first : first + count].reshape(count, ref.shape[2])


def spread(own, partner, ext):
    blocks = own.shape[1]
    parts = [*split3(own), *split3(partner)]
    shape = (blocks, 2 * blocks * ext)
    repeat = []
    for half in range(2):
        element = counted(shape, 1) // ext - half * blocks
        repeat += [(element == counted(shape, 0)).astype(f32).astype(bf16)] * 3
    return dot(jnp.concatenate(parts, axis=1), jnp.concatenate(repeat, axis=0))


def gathered(choice, value):
    choice = choice.astype(f32).astype(bf16)
    high, middle, low = split3(value)
    return dot(choice, high) + (dot(choice, middle) + dot(choice, low))


def x_coefficients_kernel(
    own_vec, partner_vec, own_ref, partner_ref, after_ref, cx_ref, cx_rows_ref, rate_ref
):
    ext, padded, lanes = rate_ref.shape
    blocks = own_vec.shape[2]
    nodes = ext - 2
    square = ext * ext
    along_x = spread(taken(own_vec, 0, square), taken(partner_vec, 0, square), ext)
    cx_ref[...] = along_x
    shape = (cx_rows_ref.shape[0], square)
    place = counted(shape, 0) % (shape[0] // ext) // 2
    choice = (place < ext) & (counted(shape, 1) == place * ext + counted(shape, 0) // (shape[0] // ext))
    cx_rows_ref[...] = gathered(choice, along_x)
    rates = []
    for ref in (own_ref, partner_ref):
        tiles = ref[nodes : ref.shape[0]]
        rates.append(tiles.reshape(-1, tiles.shape[2])[0 : 3 * ext, 0:blocks])
    rates = spread(*rates, ext)
    shape = (ext, lanes)
    rate_z = rates[2 * ext : 3 * ext]
    same = counted(shape, 0) == counted(shape, 1) % ext
    rate_z = jnp.sum(jnp.where(same, rate_z, jnp.zeros_like(rate_z)), axis=0, keepdims=True)
    rate_y = jnp.concatenate([rates[ext : 2 * ext], jnp.ones((padded - ext, lanes), f32)], axis=0)
    for p in range(ext):
        rate_ref[p] = 1.0 / (rates[p : p + 1] + rate_y + rate_z)


def y_coefficients_kernel(own_vec, partner_vec, after_ref, cy_ref):
    ext, padded = cy_ref.shape[1:3]
    square = ext * ext
    along_y = spread(taken(own_vec, square, square), taken(partner_vec, square, square), ext)
    shape = (ext * padded, square)
    first, second, entry = counted(shape, 0) // padded, counted(shape, 0) % padded, counted(shape, 1)
    forward = (second < ext) & (entry == first * ext + second)
    position = jnp.where(second < ext - 2, second + 1, jnp.where(second == ext - 2, 0, ext - 1))
    backward = (second < ext) & (entry == position * ext + first)
    for k, choice in enumerate((forward, backward)):
        cy_ref[k] = gathered(choice, along_y).reshape(cy_ref.shape[1:])


def z_coefficients_kernel(own_vec, partner_vec, after_ref, out_ref):
    ext, lanes = out_ref.shape
    square = ext * ext
    shape = (square, lanes)
    same = counted(shape, 0) % ext == counted(shape, 1) % ext
    along_z = spread(
        taken(own_vec, 2 * square, square), taken(partner_vec, 2 * square, square), ext
    )
    along_z = jnp.where(same, along_z, jnp.zeros_like(along_z))
    shape = (ext, square)
    out_ref[...] = gathered(counted(shape, 1) // ext == counted(shape, 0), along_z)


def z_matrix_kernel(along_z, after_ref, mz_ref, back_ref):
    ext, lanes = along_z.shape
    half = lanes // 2
    blocks = half // ext
    nodes = ext - 2
    core = lax.axis_index("gz")
    zeros = jnp.zeros((nodes - 2, lanes), f32)
    own = along_z[1 : nodes + 1, :]
    below = jnp.concatenate([zeros, along_z[0:2, :]], axis=0)
    above = jnp.concatenate([along_z[nodes : nodes + 2, :], zeros], axis=0)
    lane = counted((nodes, lanes), 1)
    first_own = core * blocks
    first_partner = blocks - first_own
    element = jnp.where(lane < half, lane // ext + first_own, (lane - half) // ext + first_partner)
    zero = jnp.zeros_like(own)
    rows = []
    for place in range(2 * blocks):
        block = place + first_own if place < blocks else place - blocks + first_partner
        value = jnp.where(element == block, own, zero)
        value = value + jnp.where(element == block + 1, below, zero)
        rows.append(value + jnp.where(element == block - 1, above, zero))
    matrix = jnp.concatenate(rows, axis=0)
    for ref, value in ((mz_ref, matrix), (back_ref, matrix.T)):
        ref[0], ref[1] = split2(value)


OUT_X, BACK_X, ALONG_Y = "out x", "back x", "along y"


def upper_core(leg, x, y):
    if leg == OUT_X:
        return 1 - x // 2 % 2
    return 0 if leg == BACK_X else x % 2


def trades_below(leg):
    x, y = lax.axis_index("gx"), lax.axis_index("gy")
    return lax.axis_index("gz") != upper_core(leg, x, y)


def meets_same(leg):
    x, y = lax.axis_index("gx"), lax.axis_index("gy")
    x = jnp.where(trades_below(leg), x - 1, x)
    return upper_core(leg, x, y) + upper_core(leg, x + 1, y) == 1


def sides(below, direct, passed):
    low = [jnp.where(below, direct[h], passed[1 - h]) for h in range(2)]
    high = [jnp.where(below, passed[1 - h], direct[h]) for h in range(2)]
    return low, high


def edges(axis):
    place, size = lax.axis_index(axis), lax.axis_size(axis)
    return place > 0, place < size - 1


def layers_kernel(own_ref, partner_ref, out_ref):
    start = jnp.where(trades_below(OUT_X), 0, out_ref.shape[2] - 2)
    same = meets_same(OUT_X)
    for layer in range(2):
        own, partner = own_ref[start + layer], partner_ref[start + layer]
        out_ref[0, layer] = jnp.where(same, own, partner)
        out_ref[1, layer] = jnp.where(same, partner, own)


def x_positions(own_ref, partner_ref, direct_ref, passed_ref):
    has_low, has_high = edges("gx")
    length = own_ref.shape[1]
    below = trades_below(OUT_X)
    outer = []
    for slot in range(2):
        direct = [direct_ref[h, slot] for h in range(2)]
        passed = [passed_ref[h, slot] for h in range(2)]
        low, high = sides(below, direct, passed)
        low = [jnp.where(has_low, v, jnp.zeros_like(v)) for v in low]
        high = [jnp.where(has_high, v, jnp.zeros_like(v)) for v in high]
        outer.append((low, high))
    positions = [outer[0][0]]
    for layer in range(length):
        value = [own_ref[layer], partner_ref[layer]]
        if layer == 0:
            value = [v + w for v, w in zip(outer[1][0], value)]
        if layer == length - 1:
            value = [v + w for v, w in zip(value, outer[0][1])]
        positions.append(value)
    return positions + [outer[1][1]]


def rows_kernel(own_ref, partner_ref, direct_ref, passed_ref, after_ref, out_ref):
    _, rows, width = own_ref.shape
    below = trades_below(ALONG_Y)
    positions = x_positions(own_ref, partner_ref, direct_ref, passed_ref)
    out_ref[out_ref.shape[0] - 1] = jnp.zeros(out_ref.shape[1:], f32)
    for a, (own, partner) in enumerate(positions):
        row = 2 * a % rows
        for half, value in enumerate((partner, own)):
            out_ref[2 * a // rows, row : row + 2, half * width : (half + 1) * width] = jnp.where(
                below, value[0:2], value[rows - 2 : rows]
            )


def by_z(value, matrix):
    rows = value.shape[0]
    spare = -rows % 16
    if spare:
        value = jnp.concatenate([value, jnp.zeros((spare, value.shape[1]), f32)], axis=0)
    high, low = split2(value)
    both = dot(jnp.concatenate([high, low], axis=0), matrix[0])
    total = both[0 : rows + spare] + (both[rows + spare :] + dot(high, matrix[1]))
    return total[0:rows]


def from_rows(value, use, mz, cx_rows, ext):
    count, rows, both = value.shape
    value = jnp.where(use, value, jnp.zeros_like(value))
    along_z = by_z(value.reshape(count * rows, both), mz)
    for p in range(ext):
        total = sum(
            cx_rows[(p * count + t) * rows : (p * count + t + 1) * rows, :]
            * along_z[t * rows : (t + 1) * rows]
            for t in range(count)
        )
        shift = 2
        while shift < rows:
            total = total + pltpu.roll(total, shift, 0)
            shift *= 2
        yield total


def interior_solve_kernel(
    own_ref, partner_ref, xd_ref, xp_ref, yd_ref, cx, cx_rows, cy, mz, out_ref, grid
):
    _, rows, width = own_ref.shape
    ext, padded, lanes = out_ref.shape
    nodes = ext - 2
    has_low, has_high = edges("gy")
    positions = x_positions(own_ref, partner_ref, xd_ref, xp_ref)
    for a, halves in enumerate(positions):
        for half, value in enumerate(halves):
            grid[a, :, half * width : (half + 1) * width] = value
    along_z = by_z(grid[...].reshape(ext * rows, 2 * width), mz)
    along_z = along_z.reshape(ext, rows, lanes)
    below = trades_below(ALONG_Y)
    use = jnp.where(below, has_low, has_high)
    outer = [cy[0, jnp.where(below, 0, nodes) + k] for k in range(2)]
    for p, value in enumerate(from_rows(yd_ref[...], use, mz, cx_rows, ext)):
        inner = sum(cx[a * ext + p : a * ext + p + 1, :] * along_z[a] for a in range(ext))
        total = sum(cy[0, b + 1] * inner[b : b + 1] for b in range(rows))
        out_ref[p] = total + sum(outer[k] * value[k : k + 1] for k in range(2))


def back_by_x(spectral, coefficients):
    return sum(c * spectral[p] for p, c in enumerate(coefficients))


def back_by_y(value, cy, ext):
    return sum(cy[1, q] * value[q : q + 1] for q in range(ext))


def solve_kernel(yp_ref, part_ref, cx, cx_rows, cy, rate, mz, mz_back, spectral, sent_ref):
    below = trades_below(ALONG_Y)
    width = yp_ref.shape[2] // 2
    ext, padded, lanes = rate.shape
    nodes = ext - 2
    has_low, has_high = edges("gy")
    passed = jnp.concatenate([yp_ref[:, :, width:], yp_ref[:, :, 0:width]], axis=2)
    use = jnp.where(below, has_high, has_low)
    outer = [cy[0, jnp.where(below, nodes, 0) + k] for k in range(2)]
    for p, value in enumerate(from_rows(passed, use, mz, cx_rows, ext)):
        total = part_ref[p] + sum(outer[k] * value[k : k + 1] for k in range(2))
        spectral[p] = total * rate[p]
    same = meets_same(BACK_X)
    layers = []
    for layer in range(2):
        rows = [layer * ext + p for p in range(ext)]
        last = [r + nodes * ext for r in rows]
        coefficients = [
            jnp.where(trades_below(BACK_X), cx[r : r + 1, :], cx[k : k + 1, :])
            for r, k in zip(rows, last)
        ]
        layers.append(back_by_y(back_by_x(spectral, coefficients), cy, ext))
    result = by_z(jnp.concatenate(layers, axis=0), mz_back)
    for layer in range(2):
        value = result[layer * padded : layer * padded + nodes + 2]
        own, partner = value[:, 0:width], value[:, width:]
        for half in range(2):
            place = half * 2 + layer
            value = jnp.where(same, own, partner) if half == 0 else jnp.where(same, partner, own)
            sent_ref[place] = value[0:nodes]
            sent_ref[4, 2 * place : 2 * place + 2, :] = value[nodes : nodes + 2]


def interior_kernel(spectral, cx, cy, mz_back, after_ref, out_ref):
    ext, padded, lanes = spectral.shape
    nodes, _, both = out_ref.shape
    layers = []
    for a in range(1, ext - 1):
        coefficients = [cx[a * ext + p : a * ext + p + 1, :] for p in range(ext)]
        layers.append(back_by_y(back_by_x(spectral, coefficients), cy, ext))
    result = by_z(jnp.concatenate(layers, axis=0), mz_back)
    out_ref[...] = result.reshape(nodes, padded, both)


def return_rows_kernel(initial_ref, inner_ref, direct_ref, passed_ref, out_ref, base_ref):
    has_low, has_high = edges("gx")
    below_x, below_y = trades_below(BACK_X), trades_below(ALONG_Y)
    nodes, rows, width = initial_ref.shape
    for layer in range(nodes):
        lanes = [slice(0, width), slice(width, 2 * width)]
        outer = [inner_ref[layer, rows : rows + 2, lanes[h]] for h in range(2)]
        values = [inner_ref[layer, 0:rows, lanes[h]] for h in range(2)]
        if layer < 2 or layer >= nodes - 2:
            slot = layer if layer < 2 else layer - (nodes - 2)

            def parts(ref, h, slot=slot):
                place = 2 * h + slot
                return ref[place], ref[4, 2 * place : 2 * place + 2, :]

            direct = [parts(direct_ref, h) for h in range(2)]
            passed = [parts(passed_ref, h) for h in range(2)]
            side = 0 if layer < 2 else 1
            valid = (has_low, has_high)[side]
            for k, target in enumerate((values, outer)):
                both = sides(below_x, [d[k] for d in direct], [d[k] for d in passed])[side]
                for h in range(2):
                    target[h] = target[h] + jnp.where(valid, both[h], jnp.zeros_like(both[h]))
        base_ref[layer] = initial_ref[layer] + values[0]
        for place, h in enumerate((1, 0)):
            first = jnp.where(below_y, outer[h][0:1], values[h][rows - 1 : rows])
            second = jnp.where(below_y, values[h][0:1], outer[h][1:2])
            out_ref[layer, :, lanes[place]] = jnp.concatenate([first, second], axis=0)


def result_kernel(base_ref, direct_ref, passed_ref, out_ref):
    below = trades_below(ALONG_Y)
    has_low, has_high = edges("gy")
    nodes, rows, width = base_ref.shape
    for layer in range(nodes):
        direct = direct_ref[layer, :, 0:width]
        passed = passed_ref[layer, :, width:]
        low = jnp.where(below, direct, passed)
        high = jnp.where(below, passed, direct)
        low = jnp.where(has_low, low, jnp.zeros_like(low))
        high = jnp.where(has_high, high, jnp.zeros_like(high))
        between = jnp.zeros((rows - 4, low.shape[1]), f32)
        out_ref[layer] = base_ref[layer] + jnp.concatenate([low, between, high], axis=0)


def swap_pairs(leg):
    count_x, count_y = (lax.axis_size(name) for name in AXES[:2])
    last, others = (count_y - 1, count_x) if leg == ALONG_Y else (count_x - 1, count_y)

    def cores(place, other):
        x, y = (other, place) if leg == ALONG_Y else (place, other)
        upper, first = upper_core(leg, x, y), (x * count_y + y) * 2
        return first + upper, first + 1 - upper

    pairs, idle = [], []
    for other in range(others):
        line = [cores(place, other) for place in range(last + 1)]
        for place in range(last):
            here, there = line[place][0], line[place + 1][1]
            pairs += [(here, there), (there, here)]
        idle.append((line[0][1], line[last][0]))
    for one, two in zip(idle[0::2], idle[1::2]):
        for here, there in zip(one, two):
            pairs += [(here, there), (there, here)]
    return pairs


def swap_cores(value):
    return lax.ppermute(value, "gz", [(0, 1), (1, 0)])


def swap_chips(value, leg):
    return lax.ppermute(value, AXES, swap_pairs(leg))


def paired_body(initial, source, metric, eigenvectors, eigenvalues):
    nodes, rows, width = initial.shape
    ext = eigenvectors.shape[1]
    blocks = width // nodes
    lanes = 2 * blocks * ext
    padded = 2 * rows
    vectors = eigenvectors.reshape(3 * ext * ext, 1, blocks)
    values = eigenvalues.reshape(3 * ext, 1, blocks)
    inputs = [
        pltpu.with_memory_space_constraint(value, pltpu.HBM)
        for value in (initial, source, metric, values)
    ]
    own = call(
        residual_kernel,
        [shaped((nodes + -(-3 * ext // rows), rows, width))],
        inputs,
        scratch=[
            *(pltpu.VMEM(value.shape, value.dtype) for value in inputs),
            pltpu.SemaphoreType.DMA((3 + metric.shape[0],)),
        ],
        where=HBM,
    )[0]
    partner = swap_cores(own)
    vectors, own = lax.optimization_barrier((vectors, own))
    partner_vectors = swap_cores(vectors)
    sent = call(layers_kernel, [shaped((2, 2, rows, width))], [own, partner])[0]
    x_direct = swap_chips(sent, OUT_X)
    tiles = -(-2 * ext // rows)
    cx, cx_rows, rate = call(
        x_coefficients_kernel,
        [
            shaped((ext * ext, lanes)),
            shaped((ext * tiles * rows, lanes)),
            shaped((ext, padded, lanes)),
        ],
        [vectors, partner_vectors, own, partner, sent],
    )
    x_direct, cx, rate = lax.optimization_barrier((x_direct, cx, rate))
    x_passed = swap_cores(x_direct)
    along_z = call(
        z_coefficients_kernel,
        [shaped((ext, lanes))],
        [vectors, partner_vectors, x_direct],
    )[0]
    sent = call(
        rows_kernel,
        [shaped((tiles, rows, 2 * width))],
        [own, partner, x_direct, x_passed, along_z],
    )[0]
    y_direct = swap_chips(sent, ALONG_Y)
    cy = call(
        y_coefficients_kernel,
        [shaped((2, ext, padded, lanes))],
        [vectors, partner_vectors, sent],
    )[0]
    mz, mz_back = call(
        z_matrix_kernel,
        [shaped((2, 2 * width, lanes), bf16), shaped((2, lanes, 2 * width), bf16)],
        [along_z, cy],
    )
    y_direct, cy, mz = lax.optimization_barrier((y_direct, cy, mz))
    y_passed = swap_cores(y_direct)
    part = call(
        interior_solve_kernel,
        [shaped((ext, padded, lanes))],
        [own, partner, x_direct, x_passed, y_direct, cx, cx_rows, cy, mz],
        scratch=[pltpu.VMEM((ext, rows, 2 * width), f32)],
    )[0]
    spectral, sent = call(
        solve_kernel,
        [shaped((ext, padded, lanes)), shaped((5, rows, width))],
        [y_passed, part, cx, cx_rows, cy, rate, mz, mz_back],
    )

    x_direct = swap_chips(sent, BACK_X)
    inner = call(interior_kernel, [shaped((nodes, padded, 2 * width))], [spectral, cx, cy, mz_back, sent])[0]
    x_passed = swap_cores(x_direct)
    sent, base = call(
        return_rows_kernel,
        [shaped((nodes, 2, 2 * width)), shaped(initial.shape)],
        [initial, inner, x_direct, x_passed],
    )
    y_direct = swap_chips(sent, ALONG_Y)
    y_passed = swap_cores(y_direct)
    return call(result_kernel, [shaped(initial.shape)], [base, y_direct, y_passed])[0]


def body(initial, source, metric, eigenvectors, eigenvalues):
    nodes = gll_points.shape[0]
    one_element = initial.shape[0] == nodes and initial.shape[1] == nodes
    if lax.axis_size("gz") == 2 and one_element and initial.shape[2] % 128 == 0:
        return paired_body(initial, source, metric, eigenvectors, eigenvalues)
    return general_body(initial, source, metric, eigenvectors, eigenvalues)


def solution(mesh):
    placed = (
        P("gx", "gy", "gz"),
        P("gx", "gy", "gz"),
        P(None, "gx", "gy", "gz"),
        P(None, None, None, "gx", "gy", "gz"),
        P(None, None, "gx", "gy", "gz"),
    )
    return jax.shard_map(
        body, mesh=mesh, in_specs=placed, out_specs=P("gx", "gy", "gz"), check_vma=False
    )
```

```python
import functools

import jax
import jax.numpy as jnp
import numpy as np
from jax import lax
from jax.experimental import pallas as pl
from jax.experimental.pallas import tpu as pltpu
from jax.sharding import PartitionSpec as P

gll_points = np.array(
    [
        -1.0,
        -0.8717401485096066,
        -0.5917001814331423,
        -0.2092992179024789,
        0.2092992179024789,
        0.5917001814331423,
        0.8717401485096066,
        1.0,
    ]
)


def extended_2(value, sides, width):
    for axis, dim in sides:
        size, length = (lax.axis_size(axis), value.shape[dim])
        up = [(i, (i + 1) % size) for i in range(size - 1)]
        down = [(j, i) for i, j in up]
        last = lax.slice_in_dim(value, length - width, length, axis=dim)
        first = lax.slice_in_dim(value, 0, width, axis=dim)
        before = lax.ppermute(last, axis, up)
        after = lax.ppermute(first, axis, down)
        value = jnp.concatenate([before, value, after], axis=dim)
    return value


def derivative_table():
    number = gll_points.shape[0]
    products = np.array(
        [
            np.prod(
                [
                    gll_points[row_index] - gll_points[other]
                    for other in range(number)
                    if other != row_index
                ]
            )
            for row_index in range(number)
        ]
    )
    matrix_out = np.zeros((number, number))
    for row_index in range(number):
        for col_index in range(number):
            if row_index != col_index:
                matrix_out[row_index, col_index] = (
                    products[row_index]
                    / products[col_index]
                    / (gll_points[row_index] - gll_points[col_index])
                )
        matrix_out[row_index, row_index] = -np.sum(matrix_out[row_index])
    return matrix_out


def apply_along(values, matrix, direction):
    block_size = matrix.shape[1]
    old_shape = values.shape
    pieces_shape = (
        old_shape[:direction]
        + (old_shape[direction] // block_size, block_size)
        + old_shape[direction + 1 :]
    )
    result = jnp.tensordot(
        values.reshape(pieces_shape),
        matrix,
        axes=((direction + 1,), (1,)),
        precision=lax.Precision.HIGHEST,
    )
    result = jnp.moveaxis(result, -1, direction + 1)
    return result.reshape(
        old_shape[:direction]
        + (old_shape[direction] // block_size * matrix.shape[0],)
        + old_shape[direction + 1 :]
    )


def apply_operator(values, metric):
    deriv_table = jnp.asarray(derivative_table(), jnp.float32)
    summed = jnp.zeros_like(values)
    for direction in range(3):
        gradient = apply_along(values, deriv_table, direction)
        summed = summed + apply_along(metric[direction] * gradient, deriv_table.T, direction)
    return summed


def assemble(padded, offset):
    result = padded
    for direction in range(3):
        length = result.shape[direction]
        view_shape = [1, 1, 1]
        view_shape[direction] = length
        node_index = ((jnp.arange(length) - offset) % 8).reshape(view_shape)
        edge_zero = jnp.zeros_like(lax.slice_in_dim(result, 0, 1, axis=direction))
        upward = jnp.concatenate(
            [lax.slice_in_dim(result, 1, length, axis=direction), edge_zero], axis=direction
        )
        downward = jnp.concatenate(
            [edge_zero, lax.slice_in_dim(result, 0, length - 1, axis=direction)], axis=direction
        )
        result = (
            result
            + jnp.where(node_index == 7, upward, 0.0)
            + jnp.where(node_index == 0, downward, 0.0)
        )
    return result


def extend_axis(padded, direction):
    shifted = jnp.moveaxis(padded, direction, 0)
    blocks = (shifted.shape[0] - 4) // 8
    trailing = shifted.shape[1:]
    middle = shifted[2:-2].reshape((blocks, 8) + trailing)
    lowest = shifted[0 : 8 * blocks : 8][:, None]
    beyond = shifted[11::8][:, None]
    joined = jnp.concatenate([lowest, middle, beyond], axis=1).reshape((blocks * 10,) + trailing)
    return jnp.moveaxis(joined, 0, direction)


def widen(padded):
    return extend_axis(extend_axis(extend_axis(padded, 0), 1), 2)


def fast_solve(extended, eigenvectors, eigenvalues):
    count_x, count_y, count_z = eigenvectors.shape[3:]
    precise = lax.Precision.HIGHEST
    spectral = extended.reshape(count_x, 10, count_y, 10, count_z, 10)
    spectral = jnp.einsum("apxyz,xaybzc->xpybzc", eigenvectors[0], spectral, precision=precise)
    spectral = jnp.einsum("bqxyz,xpybzc->xpyqzc", eigenvectors[1], spectral, precision=precise)
    spectral = jnp.einsum("csxyz,xpyqzc->xpyqzs", eigenvectors[2], spectral, precision=precise)
    rate_x = jnp.transpose(eigenvalues[0], (1, 0, 2, 3))[:, :, :, None, :, None]
    rate_y = jnp.transpose(eigenvalues[1], (1, 2, 0, 3))[:, None, :, :, :, None]
    rate_z = jnp.transpose(eigenvalues[2], (1, 2, 3, 0))[:, None, :, None, :, :]
    spectral = spectral / (rate_x + rate_y + rate_z)
    spectral = jnp.einsum("csxyz,xpyqzs->xpyqzc", eigenvectors[2], spectral, precision=precise)
    spectral = jnp.einsum("bqxyz,xpyqzc->xpybzc", eigenvectors[1], spectral, precision=precise)
    spectral = jnp.einsum("apxyz,xpybzc->xaybzc", eigenvectors[0], spectral, precision=precise)
    return spectral.reshape(count_x * 10, count_y * 10, count_z * 10)


def return_axis(padded, direction):
    shifted = jnp.moveaxis(padded, direction, 0)
    blocks = (shifted.shape[0] - 4) // 10
    trailing = shifted.shape[1:]
    owned = shifted[2:-2].reshape((blocks, 10) + trailing)[:, 1:9]
    before = shifted[0 : 10 * blocks].reshape((blocks, 10) + trailing)[:, 0:2]
    following = shifted[4:].reshape((blocks, 10) + trailing)[:, 8:10]
    middle = jnp.zeros((blocks, 4) + trailing, shifted.dtype)
    summed = owned + jnp.concatenate([before, middle, following], axis=1)
    return jnp.moveaxis(summed.reshape((blocks * 8,) + trailing), 0, direction)


def general_body(initial, source, metric, eigenvectors, eigenvalues):
    solution = initial
    local_res = source - apply_operator(solution, metric)
    deeper = extended_2(local_res, (("gx", 0), ("gy", 1), ("gz", 2)), 2)
    widened = assemble(deeper, 2)
    extended = widen(widened)
    corrected = fast_solve(extended, eigenvectors, eigenvalues)
    padded = extended_2(corrected, (("gx", 0), ("gy", 1), ("gz", 2)), 2)
    correction = return_axis(return_axis(return_axis(padded, 0), 1), 2)
    solution = solution + correction
    return solution


AXES = ("gx", "gy", "gz")
VMEM = pl.BlockSpec(memory_space=pltpu.VMEM)
HBM = pl.BlockSpec(memory_space=pltpu.HBM)
VMEM_LIMIT = 16 * 2**20
f32 = jnp.float32
bf16 = jnp.bfloat16


def call(kernel, outs, args, scratch=(), where=VMEM):
    moved = sum(int(np.prod(a.shape)) * a.dtype.itemsize for a in (*args, *outs))
    return pl.pallas_call(
        kernel,
        out_shape=outs,
        in_specs=[where] * len(args),
        out_specs=[VMEM] * len(outs),
        scratch_shapes=scratch,
        compiler_params=pltpu.CompilerParams(vmem_limit_bytes=VMEM_LIMIT),
        cost_estimate=pl.CostEstimate(flops=0, bytes_accessed=moved, transcendentals=0),
    )(*args)


def shaped(shape, dtype=f32):
    return jax.ShapeDtypeStruct(shape, dtype)


def counted(shape, axis):
    return lax.broadcasted_iota(jnp.int32, shape, axis)


def split2(value):
    high = value.astype(bf16)
    return high, (value - high.astype(f32)).astype(bf16)


def split3(value):
    high = value.astype(bf16)
    rest = value - high.astype(f32)
    middle = rest.astype(bf16)
    return high, middle, (rest - middle.astype(f32)).astype(bf16)


def dot(left, right):
    return jnp.dot(left, right, preferred_element_type=f32)


def repeated_table(table, width):
    nodes = table.shape[0]
    row, column = counted((nodes, width), 0), counted((nodes, width), 1) % nodes
    tile = jnp.zeros((nodes, width), f32)
    for j in range(nodes):
        values = jnp.zeros((nodes, width), f32)
        for i in range(nodes):
            values = jnp.where(row == i, float(table[i, j]), values)
        tile = jnp.where(column == j, values, tile)
    return tile


def residual_kernel(
    u_hbm, source_hbm, metric_hbm, val_hbm, out_ref, u_ref, source_ref, metric_ref, val_ref, sems
):
    copies = [pltpu.make_async_copy(u_hbm, u_ref, sems.at[0])]
    copies += [
        pltpu.make_async_copy(metric_hbm.at[d], metric_ref.at[d], sems.at[1 + d])
        for d in range(metric_hbm.shape[0])
    ]
    copies.append(pltpu.make_async_copy(source_hbm, source_ref, sems.at[len(copies)]))
    copies.append(pltpu.make_async_copy(val_hbm, val_ref, sems.at[len(copies)]))
    for copy in copies:
        copy.start()
    nodes, rows, width = u_ref.shape
    flat_rows = nodes * rows
    table = np.asarray(derivative_table(), np.float32)
    along_y, along_z = [], []
    for t in range(2):
        tile = repeated_table(table if t == 0 else table.T, width)
        high = tile.astype(bf16).astype(f32)
        low = tile - high
        group = counted((nodes, width), 1) // nodes
        zero = jnp.zeros_like(tile)
        for part in (high, low):
            bands = [jnp.where(group == k, part, zero) for k in range(width // nodes)]
            along_z.append(jnp.concatenate(bands, axis=0).astype(bf16))
        group = group[:, 0 : 2 * flat_rows]
        high, low, zero = (v[:, 0 : 2 * flat_rows] for v in (high, low, zero))
        bands = [jnp.where(group % rows == k, high, zero) for k in range(nodes)]
        bands += [jnp.where(group == k, low, zero) for k in range(nodes)]
        along_y.append(jnp.concatenate(bands, axis=0).astype(bf16))

    def by_y(value, t):
        both = dot(along_y[t], jnp.concatenate(split2(value), axis=0))
        return both[0:flat_rows] + both[flat_rows:]

    def by_z(value, t):
        high, low = split2(value)
        both = dot(jnp.concatenate([high, low], axis=0), along_z[2 * t])
        return both[0:flat_rows] + (both[flat_rows:] + dot(high, along_z[2 * t + 1]))

    copies[0].wait()
    flat = u_ref[...].reshape(flat_rows, width)
    flux_y, flux_z = by_y(flat, 0), by_z(flat, 1)
    layers = [u_ref[j] for j in range(nodes)]
    flux_x = [sum(float(table[i, j]) * layers[j] for j in range(nodes)) for i in range(nodes)]
    for copy in copies[1:]:
        copy.wait()
    total = by_y(flux_y * metric_ref[1].reshape(flat.shape), 1)
    total = total + by_z(flux_z * metric_ref[2].reshape(flat.shape), 0)
    total = total.reshape(nodes, rows, width)
    flux_x = [metric_ref[0, i] * flux_x[i] for i in range(nodes)]
    for j in range(nodes):
        applied = sum(float(table[i, j]) * flux_x[i] for i in range(nodes))
        out_ref[j] = source_ref[j] - (applied + total[j])
    count, _, blocks = val_ref.shape
    values = val_ref[...].reshape(count, blocks)
    for first in range(0, count, rows):
        last = min(first + rows, count)
        out_ref[nodes + first // rows, 0 : last - first, 0:blocks] = values[first:last]


def layers_kernel(own_ref, partner_ref, out_ref):
    start = lax.axis_index("gz") * (out_ref.shape[2] - 2)
    for half, ref in enumerate((partner_ref, own_ref)):
        for layer in range(2):
            out_ref[half, layer] = ref[start + layer]


def taken(ref, first, count):
    return ref[first : first + count].reshape(count, ref.shape[2])


def spread(own, partner, ext):
    blocks = own.shape[1]
    parts = [*split3(own), *split3(partner)]
    shape = (blocks, 2 * blocks * ext)
    repeat = []
    for half in range(2):
        element = counted(shape, 1) // ext - half * blocks
        repeat += [(element == counted(shape, 0)).astype(f32).astype(bf16)] * 3
    return dot(jnp.concatenate(parts, axis=1), jnp.concatenate(repeat, axis=0))


def gathered(choice, value):
    choice = choice.astype(f32).astype(bf16)
    high, middle, low = split3(value)
    return dot(choice, high) + (dot(choice, middle) + dot(choice, low))


def x_coefficients_kernel(
    own_vec, partner_vec, own_ref, partner_ref, after_ref, cx_ref, cx_rows_ref, rate_ref
):
    ext, padded, lanes = rate_ref.shape
    blocks = own_vec.shape[2]
    nodes = ext - 2
    square = ext * ext
    along_x = spread(taken(own_vec, 0, square), taken(partner_vec, 0, square), ext)
    cx_ref[...] = along_x
    shape = (cx_rows_ref.shape[0], square)
    place = counted(shape, 0) % (shape[0] // ext) // 2
    choice = (place < ext) & (counted(shape, 1) == place * ext + counted(shape, 0) // (shape[0] // ext))
    cx_rows_ref[...] = gathered(choice, along_x)
    rates = []
    for ref in (own_ref, partner_ref):
        tiles = ref[nodes : ref.shape[0]]
        rates.append(tiles.reshape(-1, tiles.shape[2])[0 : 3 * ext, 0:blocks])
    rates = spread(*rates, ext)
    shape = (ext, lanes)
    rate_z = rates[2 * ext : 3 * ext]
    same = counted(shape, 0) == counted(shape, 1) % ext
    rate_z = jnp.sum(jnp.where(same, rate_z, jnp.zeros_like(rate_z)), axis=0, keepdims=True)
    rate_y = jnp.concatenate([rates[ext : 2 * ext], jnp.ones((padded - ext, lanes), f32)], axis=0)
    for p in range(ext):
        rate_ref[p] = 1.0 / (rates[p : p + 1] + rate_y + rate_z)


def y_coefficients_kernel(own_vec, partner_vec, after_ref, cy_ref):
    ext, padded = cy_ref.shape[1:3]
    square = ext * ext
    along_y = spread(taken(own_vec, square, square), taken(partner_vec, square, square), ext)
    shape = (ext * padded, square)
    first, second, entry = counted(shape, 0) // padded, counted(shape, 0) % padded, counted(shape, 1)
    forward = (second < ext) & (entry == first * ext + second)
    position = jnp.where(second < ext - 2, second + 1, jnp.where(second == ext - 2, 0, ext - 1))
    backward = (second < ext) & (entry == position * ext + first)
    for k, choice in enumerate((forward, backward)):
        cy_ref[k] = gathered(choice, along_y).reshape(cy_ref.shape[1:])


def z_coefficients_kernel(own_vec, partner_vec, after_ref, out_ref):
    ext, lanes = out_ref.shape
    square = ext * ext
    shape = (square, lanes)
    same = counted(shape, 0) % ext == counted(shape, 1) % ext
    along_z = spread(
        taken(own_vec, 2 * square, square), taken(partner_vec, 2 * square, square), ext
    )
    along_z = jnp.where(same, along_z, jnp.zeros_like(along_z))
    shape = (ext, square)
    out_ref[...] = gathered(counted(shape, 1) // ext == counted(shape, 0), along_z)


def z_matrix_kernel(along_z, after_ref, mz_ref, back_ref):
    ext, lanes = along_z.shape
    half = lanes // 2
    blocks = half // ext
    nodes = ext - 2
    core = lax.axis_index("gz")
    zeros = jnp.zeros((nodes - 2, lanes), f32)
    own = along_z[1 : nodes + 1, :]
    below = jnp.concatenate([zeros, along_z[0:2, :]], axis=0)
    above = jnp.concatenate([along_z[nodes : nodes + 2, :], zeros], axis=0)
    lane = counted((nodes, lanes), 1)
    first_own = core * blocks
    first_partner = blocks - first_own
    element = jnp.where(lane < half, lane // ext + first_own, (lane - half) // ext + first_partner)
    zero = jnp.zeros_like(own)
    rows = []
    for place in range(2 * blocks):
        block = place + first_own if place < blocks else place - blocks + first_partner
        value = jnp.where(element == block, own, zero)
        value = value + jnp.where(element == block + 1, below, zero)
        rows.append(value + jnp.where(element == block - 1, above, zero))
    matrix = jnp.concatenate(rows, axis=0)
    for ref, value in ((mz_ref, matrix), (back_ref, matrix.T)):
        ref[0], ref[1] = split2(value)


OUT_X, BACK_X, OUT_Y, BACK_Y = "out x", "back x", "out y", "back y"


def upper_core(leg, x, y):
    if leg == OUT_X:
        return 1 - x // 2 % 2
    if leg == BACK_X:
        return 0
    return x % 2 if leg == OUT_Y else (x + 1) // 2 % 2


def trades_below(leg):
    x, y = lax.axis_index("gx"), lax.axis_index("gy")
    return lax.axis_index("gz") != upper_core(leg, x, y)


def meets_same(leg):
    x, y = lax.axis_index("gx"), lax.axis_index("gy")
    x = jnp.where(trades_below(leg), x - 1, x)
    return upper_core(leg, x, y) + upper_core(leg, x + 1, y) == 1


def sides(below, direct, passed):
    low = [jnp.where(below, direct[h], passed[1 - h]) for h in range(2)]
    high = [jnp.where(below, passed[1 - h], direct[h]) for h in range(2)]
    return low, high


def edges(axis):
    place, size = lax.axis_index(axis), lax.axis_size(axis)
    return place > 0, place < size - 1


def layers_kernel(own_ref, partner_ref, out_ref):
    start = jnp.where(trades_below(OUT_X), 0, out_ref.shape[2] - 2)
    same = meets_same(OUT_X)
    for layer in range(2):
        own, partner = own_ref[start + layer], partner_ref[start + layer]
        out_ref[0, layer] = jnp.where(same, own, partner)
        out_ref[1, layer] = jnp.where(same, partner, own)


def x_positions(own_ref, partner_ref, direct_ref, passed_ref):
    has_low, has_high = edges("gx")
    length = own_ref.shape[1]
    below = trades_below(OUT_X)
    outer = []
    for slot in range(2):
        direct = [direct_ref[h, slot] for h in range(2)]
        passed = [passed_ref[h, slot] for h in range(2)]
        low, high = sides(below, direct, passed)
        low = [jnp.where(has_low, v, jnp.zeros_like(v)) for v in low]
        high = [jnp.where(has_high, v, jnp.zeros_like(v)) for v in high]
        outer.append((low, high))
    positions = [outer[0][0]]
    for layer in range(length):
        value = [own_ref[layer], partner_ref[layer]]
        if layer == 0:
            value = [v + w for v, w in zip(outer[1][0], value)]
        if layer == length - 1:
            value = [v + w for v, w in zip(value, outer[0][1])]
        positions.append(value)
    return positions + [outer[1][1]]


def rows_kernel(own_ref, partner_ref, direct_ref, passed_ref, after_ref, out_ref):
    _, rows, width = own_ref.shape
    below = trades_below(OUT_Y)
    positions = x_positions(own_ref, partner_ref, direct_ref, passed_ref)
    out_ref[out_ref.shape[0] - 1] = jnp.zeros(out_ref.shape[1:], f32)
    for a, (own, partner) in enumerate(positions):
        row = 2 * a % rows
        for half, value in enumerate((partner, own)):
            out_ref[2 * a // rows, row : row + 2, half * width : (half + 1) * width] = jnp.where(
                below, value[0:2], value[rows - 2 : rows]
            )


def by_z(value, matrix):
    rows = value.shape[0]
    spare = -rows % 16
    if spare:
        value = jnp.concatenate([value, jnp.zeros((spare, value.shape[1]), f32)], axis=0)
    high, low = split2(value)
    both = dot(jnp.concatenate([high, low], axis=0), matrix[0])
    total = both[0 : rows + spare] + (both[rows + spare :] + dot(high, matrix[1]))
    return total[0:rows]


def from_rows(value, use, mz, cx_rows, ext):
    count, rows, both = value.shape
    value = jnp.where(use, value, jnp.zeros_like(value))
    along_z = by_z(value.reshape(count * rows, both), mz)
    for p in range(ext):
        total = sum(
            cx_rows[(p * count + t) * rows : (p * count + t + 1) * rows, :]
            * along_z[t * rows : (t + 1) * rows]
            for t in range(count)
        )
        shift = 2
        while shift < rows:
            total = total + pltpu.roll(total, shift, 0)
            shift *= 2
        yield total


def interior_solve_kernel(
    own_ref, partner_ref, xd_ref, xp_ref, yd_ref, cx, cx_rows, cy, mz, out_ref, grid
):
    _, rows, width = own_ref.shape
    ext, padded, lanes = out_ref.shape
    nodes = ext - 2
    has_low, has_high = edges("gy")
    positions = x_positions(own_ref, partner_ref, xd_ref, xp_ref)
    for a, halves in enumerate(positions):
        for half, value in enumerate(halves):
            grid[a, :, half * width : (half + 1) * width] = value
    along_z = by_z(grid[...].reshape(ext * rows, 2 * width), mz)
    along_z = along_z.reshape(ext, rows, lanes)
    below = trades_below(OUT_Y)
    use = jnp.where(below, has_low, has_high)
    outer = [cy[0, jnp.where(below, 0, nodes) + k] for k in range(2)]
    for p, value in enumerate(from_rows(yd_ref[...], use, mz, cx_rows, ext)):
        inner = sum(cx[a * ext + p : a * ext + p + 1, :] * along_z[a] for a in range(ext))
        total = sum(cy[0, b + 1] * inner[b : b + 1] for b in range(rows))
        out_ref[p] = total + sum(outer[k] * value[k : k + 1] for k in range(2))


def back_by_x(spectral, coefficients):
    return sum(c * spectral[p] for p, c in enumerate(coefficients))


def back_by_y(value, cy, ext):
    return sum(cy[1, q] * value[q : q + 1] for q in range(ext))


def solve_kernel(yp_ref, part_ref, cx, cx_rows, cy, rate, mz, mz_back, spectral, sent_ref):
    below = trades_below(OUT_Y)
    width = yp_ref.shape[2] // 2
    ext, padded, lanes = rate.shape
    nodes = ext - 2
    has_low, has_high = edges("gy")
    passed = jnp.concatenate([yp_ref[:, :, width:], yp_ref[:, :, 0:width]], axis=2)
    use = jnp.where(below, has_high, has_low)
    outer = [cy[0, jnp.where(below, nodes, 0) + k] for k in range(2)]
    for p, value in enumerate(from_rows(passed, use, mz, cx_rows, ext)):
        total = part_ref[p] + sum(outer[k] * value[k : k + 1] for k in range(2))
        spectral[p] = total * rate[p]
    same = meets_same(BACK_X)
    layers = []
    for layer in range(2):
        rows = [layer * ext + p for p in range(ext)]
        last = [r + nodes * ext for r in rows]
        coefficients = [
            jnp.where(trades_below(BACK_X), cx[r : r + 1, :], cx[k : k + 1, :])
            for r, k in zip(rows, last)
        ]
        layers.append(back_by_y(back_by_x(spectral, coefficients), cy, ext))
    result = by_z(jnp.concatenate(layers, axis=0), mz_back)
    for layer in range(2):
        value = result[layer * padded : layer * padded + nodes + 2]
        own, partner = value[:, 0:width], value[:, width:]
        for half in range(2):
            place = half * 2 + layer
            value = jnp.where(same, own, partner) if half == 0 else jnp.where(same, partner, own)
            sent_ref[place] = value[0:nodes]
            sent_ref[4, 2 * place : 2 * place + 2, :] = value[nodes : nodes + 2]


def interior_kernel(spectral, cx, cy, mz_back, after_ref, out_ref):
    ext, padded, lanes = spectral.shape
    nodes, _, both = out_ref.shape
    layers = []
    for a in range(1, ext - 1):
        coefficients = [cx[a * ext + p : a * ext + p + 1, :] for p in range(ext)]
        layers.append(back_by_y(back_by_x(spectral, coefficients), cy, ext))
    result = by_z(jnp.concatenate(layers, axis=0), mz_back)
    out_ref[...] = result.reshape(nodes, padded, both)


def return_rows_kernel(initial_ref, inner_ref, direct_ref, passed_ref, out_ref, base_ref):
    has_low, has_high = edges("gx")
    below_x, below_y = trades_below(BACK_X), trades_below(BACK_Y)
    nodes, rows, width = initial_ref.shape
    for layer in range(nodes):
        lanes = [slice(0, width), slice(width, 2 * width)]
        outer = [inner_ref[layer, rows : rows + 2, lanes[h]] for h in range(2)]
        values = [inner_ref[layer, 0:rows, lanes[h]] for h in range(2)]
        if layer < 2 or layer >= nodes - 2:
            slot = layer if layer < 2 else layer - (nodes - 2)

            def parts(ref, h, slot=slot):
                place = 2 * h + slot
                return ref[place], ref[4, 2 * place : 2 * place + 2, :]

            direct = [parts(direct_ref, h) for h in range(2)]
            passed = [parts(passed_ref, h) for h in range(2)]
            side = 0 if layer < 2 else 1
            valid = (has_low, has_high)[side]
            for k, target in enumerate((values, outer)):
                both = sides(below_x, [d[k] for d in direct], [d[k] for d in passed])[side]
                for h in range(2):
                    target[h] = target[h] + jnp.where(valid, both[h], jnp.zeros_like(both[h]))
        base_ref[layer] = initial_ref[layer] + values[0]
        for place, h in enumerate((1, 0)):
            first = jnp.where(below_y, outer[h][0:1], values[h][rows - 1 : rows])
            second = jnp.where(below_y, values[h][0:1], outer[h][1:2])
            out_ref[layer, :, lanes[place]] = jnp.concatenate([first, second], axis=0)


def result_kernel(base_ref, direct_ref, passed_ref, out_ref):
    below = trades_below(BACK_Y)
    has_low, has_high = edges("gy")
    nodes, rows, width = base_ref.shape
    for layer in range(nodes):
        direct = direct_ref[layer, :, 0:width]
        passed = passed_ref[layer, :, width:]
        low = jnp.where(below, direct, passed)
        high = jnp.where(below, passed, direct)
        low = jnp.where(has_low, low, jnp.zeros_like(low))
        high = jnp.where(has_high, high, jnp.zeros_like(high))
        between = jnp.zeros((rows - 4, low.shape[1]), f32)
        out_ref[layer] = base_ref[layer] + jnp.concatenate([low, between, high], axis=0)


def swap_pairs(leg):
    count_x, count_y = (lax.axis_size(name) for name in AXES[:2])
    by_y = leg in (OUT_Y, BACK_Y)
    last, others = (count_y - 1, count_x) if by_y else (count_x - 1, count_y)

    def cores(place, other):
        x, y = (other, place) if by_y else (place, other)
        upper, first = upper_core(leg, x, y), (x * count_y + y) * 2
        return first + upper, first + 1 - upper

    pairs, idle = [], []
    for other in range(others):
        line = [cores(place, other) for place in range(last + 1)]
        for place in range(last):
            here, there = line[place][0], line[place + 1][1]
            pairs += [(here, there), (there, here)]
        idle.append((line[0][1], line[last][0]))
    step = 2 if leg == BACK_Y and others % 4 == 0 else 1
    for other in range(others - step):
        if other // step % 2 == 0:
            for here, there in zip(idle[other], idle[other + step]):
                pairs += [(here, there), (there, here)]
    return pairs


def swap_cores(value):
    return lax.ppermute(value, "gz", [(0, 1), (1, 0)])


def swap_chips(value, leg):
    return lax.ppermute(value, AXES, swap_pairs(leg))


def paired_body(initial, source, metric, eigenvectors, eigenvalues):
    nodes, rows, width = initial.shape
    ext = eigenvectors.shape[1]
    blocks = width // nodes
    lanes = 2 * blocks * ext
    padded = 2 * rows
    vectors = eigenvectors.reshape(3 * ext * ext, 1, blocks)
    values = eigenvalues.reshape(3 * ext, 1, blocks)
    inputs = [
        pltpu.with_memory_space_constraint(value, pltpu.HBM)
        for value in (initial, source, metric, values)
    ]
    own = call(
        residual_kernel,
        [shaped((nodes + -(-3 * ext // rows), rows, width))],
        inputs,
        scratch=[
            *(pltpu.VMEM(value.shape, value.dtype) for value in inputs),
            pltpu.SemaphoreType.DMA((3 + metric.shape[0],)),
        ],
        where=HBM,
    )[0]
    partner = swap_cores(own)
    vectors, own = lax.optimization_barrier((vectors, own))
    partner_vectors = swap_cores(vectors)
    sent = call(layers_kernel, [shaped((2, 2, rows, width))], [own, partner])[0]
    x_direct = swap_chips(sent, OUT_X)
    tiles = -(-2 * ext // rows)
    cx, cx_rows, rate = call(
        x_coefficients_kernel,
        [
            shaped((ext * ext, lanes)),
            shaped((ext * tiles * rows, lanes)),
            shaped((ext, padded, lanes)),
        ],
        [vectors, partner_vectors, own, partner, sent],
    )
    x_direct, cx, rate = lax.optimization_barrier((x_direct, cx, rate))
    x_passed = swap_cores(x_direct)
    along_z = call(
        z_coefficients_kernel,
        [shaped((ext, lanes))],
        [vectors, partner_vectors, x_direct],
    )[0]
    sent = call(
        rows_kernel,
        [shaped((tiles, rows, 2 * width))],
        [own, partner, x_direct, x_passed, along_z],
    )[0]
    y_direct = swap_chips(sent, OUT_Y)
    cy = call(
        y_coefficients_kernel,
        [shaped((2, ext, padded, lanes))],
        [vectors, partner_vectors, sent],
    )[0]
    mz, mz_back = call(
        z_matrix_kernel,
        [shaped((2, 2 * width, lanes), bf16), shaped((2, lanes, 2 * width), bf16)],
        [along_z, cy],
    )
    y_direct, cy, mz = lax.optimization_barrier((y_direct, cy, mz))
    y_passed = swap_cores(y_direct)
    part = call(
        interior_solve_kernel,
        [shaped((ext, padded, lanes))],
        [own, partner, x_direct, x_passed, y_direct, cx, cx_rows, cy, mz],
        scratch=[pltpu.VMEM((ext, rows, 2 * width), f32)],
    )[0]
    spectral, sent = call(
        solve_kernel,
        [shaped((ext, padded, lanes)), shaped((5, rows, width))],
        [y_passed, part, cx, cx_rows, cy, rate, mz, mz_back],
    )

    x_direct = swap_chips(sent, BACK_X)
    inner = call(interior_kernel, [shaped((nodes, padded, 2 * width))], [spectral, cx, cy, mz_back, sent])[0]
    x_passed = swap_cores(x_direct)
    sent, base = call(
        return_rows_kernel,
        [shaped((nodes, 2, 2 * width)), shaped(initial.shape)],
        [initial, inner, x_direct, x_passed],
    )
    y_direct = swap_chips(sent, BACK_Y)
    y_passed = swap_cores(y_direct)
    return call(result_kernel, [shaped(initial.shape)], [base, y_direct, y_passed])[0]


def body(initial, source, metric, eigenvectors, eigenvalues):
    nodes = gll_points.shape[0]
    one_element = initial.shape[0] == nodes and initial.shape[1] == nodes
    if lax.axis_size("gz") == 2 and one_element and initial.shape[2] % 128 == 0:
        return paired_body(initial, source, metric, eigenvectors, eigenvalues)
    return general_body(initial, source, metric, eigenvectors, eigenvalues)


def solution(mesh):
    placed = (
        P("gx", "gy", "gz"),
        P("gx", "gy", "gz"),
        P(None, "gx", "gy", "gz"),
        P(None, None, None, "gx", "gy", "gz"),
        P(None, None, "gx", "gy", "gz"),
    )
    return jax.shard_map(
        body, mesh=mesh, in_specs=placed, out_specs=P("gx", "gy", "gz"), check_vma=False
    )
```

```python
import functools

import jax
import jax.numpy as jnp
import numpy as np
from jax import lax
from jax.experimental import pallas as pl
from jax.experimental.pallas import tpu as pltpu
from jax.sharding import PartitionSpec as P

gll_points = np.array(
    [
        -1.0,
        -0.8717401485096066,
        -0.5917001814331423,
        -0.2092992179024789,
        0.2092992179024789,
        0.5917001814331423,
        0.8717401485096066,
        1.0,
    ]
)


def extended_2(value, sides, width):
    for axis, dim in sides:
        size, length = (lax.axis_size(axis), value.shape[dim])
        up = [(i, (i + 1) % size) for i in range(size - 1)]
        down = [(j, i) for i, j in up]
        last = lax.slice_in_dim(value, length - width, length, axis=dim)
        first = lax.slice_in_dim(value, 0, width, axis=dim)
        before = lax.ppermute(last, axis, up)
        after = lax.ppermute(first, axis, down)
        value = jnp.concatenate([before, value, after], axis=dim)
    return value


def derivative_table():
    number = gll_points.shape[0]
    products = np.array(
        [
            np.prod(
                [
                    gll_points[row_index] - gll_points[other]
                    for other in range(number)
                    if other != row_index
                ]
            )
            for row_index in range(number)
        ]
    )
    matrix_out = np.zeros((number, number))
    for row_index in range(number):
        for col_index in range(number):
            if row_index != col_index:
                matrix_out[row_index, col_index] = (
                    products[row_index]
                    / products[col_index]
                    / (gll_points[row_index] - gll_points[col_index])
                )
        matrix_out[row_index, row_index] = -np.sum(matrix_out[row_index])
    return matrix_out


def apply_along(values, matrix, direction):
    block_size = matrix.shape[1]
    old_shape = values.shape
    pieces_shape = (
        old_shape[:direction]
        + (old_shape[direction] // block_size, block_size)
        + old_shape[direction + 1 :]
    )
    result = jnp.tensordot(
        values.reshape(pieces_shape),
        matrix,
        axes=((direction + 1,), (1,)),
        precision=lax.Precision.HIGHEST,
    )
    result = jnp.moveaxis(result, -1, direction + 1)
    return result.reshape(
        old_shape[:direction]
        + (old_shape[direction] // block_size * matrix.shape[0],)
        + old_shape[direction + 1 :]
    )


def apply_operator(values, metric):
    deriv_table = jnp.asarray(derivative_table(), jnp.float32)
    summed = jnp.zeros_like(values)
    for direction in range(3):
        gradient = apply_along(values, deriv_table, direction)
        summed = summed + apply_along(metric[direction] * gradient, deriv_table.T, direction)
    return summed


def assemble(padded, offset):
    result = padded
    for direction in range(3):
        length = result.shape[direction]
        view_shape = [1, 1, 1]
        view_shape[direction] = length
        node_index = ((jnp.arange(length) - offset) % 8).reshape(view_shape)
        edge_zero = jnp.zeros_like(lax.slice_in_dim(result, 0, 1, axis=direction))
        upward = jnp.concatenate(
            [lax.slice_in_dim(result, 1, length, axis=direction), edge_zero], axis=direction
        )
        downward = jnp.concatenate(
            [edge_zero, lax.slice_in_dim(result, 0, length - 1, axis=direction)], axis=direction
        )
        result = (
            result
            + jnp.where(node_index == 7, upward, 0.0)
            + jnp.where(node_index == 0, downward, 0.0)
        )
    return result


def extend_axis(padded, direction):
    shifted = jnp.moveaxis(padded, direction, 0)
    blocks = (shifted.shape[0] - 4) // 8
    trailing = shifted.shape[1:]
    middle = shifted[2:-2].reshape((blocks, 8) + trailing)
    lowest = shifted[0 : 8 * blocks : 8][:, None]
    beyond = shifted[11::8][:, None]
    joined = jnp.concatenate([lowest, middle, beyond], axis=1).reshape((blocks * 10,) + trailing)
    return jnp.moveaxis(joined, 0, direction)


def widen(padded):
    return extend_axis(extend_axis(extend_axis(padded, 0), 1), 2)


def fast_solve(extended, eigenvectors, eigenvalues):
    count_x, count_y, count_z = eigenvectors.shape[3:]
    precise = lax.Precision.HIGHEST
    spectral = extended.reshape(count_x, 10, count_y, 10, count_z, 10)
    spectral = jnp.einsum("apxyz,xaybzc->xpybzc", eigenvectors[0], spectral, precision=precise)
    spectral = jnp.einsum("bqxyz,xpybzc->xpyqzc", eigenvectors[1], spectral, precision=precise)
    spectral = jnp.einsum("csxyz,xpyqzc->xpyqzs", eigenvectors[2], spectral, precision=precise)
    rate_x = jnp.transpose(eigenvalues[0], (1, 0, 2, 3))[:, :, :, None, :, None]
    rate_y = jnp.transpose(eigenvalues[1], (1, 2, 0, 3))[:, None, :, :, :, None]
    rate_z = jnp.transpose(eigenvalues[2], (1, 2, 3, 0))[:, None, :, None, :, :]
    spectral = spectral / (rate_x + rate_y + rate_z)
    spectral = jnp.einsum("csxyz,xpyqzs->xpyqzc", eigenvectors[2], spectral, precision=precise)
    spectral = jnp.einsum("bqxyz,xpyqzc->xpybzc", eigenvectors[1], spectral, precision=precise)
    spectral = jnp.einsum("apxyz,xpybzc->xaybzc", eigenvectors[0], spectral, precision=precise)
    return spectral.reshape(count_x * 10, count_y * 10, count_z * 10)


def return_axis(padded, direction):
    shifted = jnp.moveaxis(padded, direction, 0)
    blocks = (shifted.shape[0] - 4) // 10
    trailing = shifted.shape[1:]
    owned = shifted[2:-2].reshape((blocks, 10) + trailing)[:, 1:9]
    before = shifted[0 : 10 * blocks].reshape((blocks, 10) + trailing)[:, 0:2]
    following = shifted[4:].reshape((blocks, 10) + trailing)[:, 8:10]
    middle = jnp.zeros((blocks, 4) + trailing, shifted.dtype)
    summed = owned + jnp.concatenate([before, middle, following], axis=1)
    return jnp.moveaxis(summed.reshape((blocks * 8,) + trailing), 0, direction)


def general_body(initial, source, metric, eigenvectors, eigenvalues):
    solution = initial
    local_res = source - apply_operator(solution, metric)
    deeper = extended_2(local_res, (("gx", 0), ("gy", 1), ("gz", 2)), 2)
    widened = assemble(deeper, 2)
    extended = widen(widened)
    corrected = fast_solve(extended, eigenvectors, eigenvalues)
    padded = extended_2(corrected, (("gx", 0), ("gy", 1), ("gz", 2)), 2)
    correction = return_axis(return_axis(return_axis(padded, 0), 1), 2)
    solution = solution + correction
    return solution


AXES = ("gx", "gy", "gz")
VMEM = pl.BlockSpec(memory_space=pltpu.VMEM)
HBM = pl.BlockSpec(memory_space=pltpu.HBM)
VMEM_LIMIT = 16 * 2**20
f32 = jnp.float32
bf16 = jnp.bfloat16


def call(kernel, outs, args, scratch=(), where=VMEM):
    moved = sum(int(np.prod(a.shape)) * a.dtype.itemsize for a in (*args, *outs))
    return pl.pallas_call(
        kernel,
        out_shape=outs,
        in_specs=[where] * len(args),
        out_specs=[VMEM] * len(outs),
        scratch_shapes=scratch,
        compiler_params=pltpu.CompilerParams(vmem_limit_bytes=VMEM_LIMIT),
        cost_estimate=pl.CostEstimate(flops=0, bytes_accessed=moved, transcendentals=0),
    )(*args)


def shaped(shape, dtype=f32):
    return jax.ShapeDtypeStruct(shape, dtype)


def counted(shape, axis):
    return lax.broadcasted_iota(jnp.int32, shape, axis)


def split2(value):
    high = value.astype(bf16)
    return high, (value - high.astype(f32)).astype(bf16)


def split3(value):
    high = value.astype(bf16)
    rest = value - high.astype(f32)
    middle = rest.astype(bf16)
    return high, middle, (rest - middle.astype(f32)).astype(bf16)


def dot(left, right):
    return jnp.dot(left, right, preferred_element_type=f32)


def repeated_table(table, width):
    nodes = table.shape[0]
    row, column = counted((nodes, width), 0), counted((nodes, width), 1) % nodes
    tile = jnp.zeros((nodes, width), f32)
    for j in range(nodes):
        values = jnp.zeros((nodes, width), f32)
        for i in range(nodes):
            values = jnp.where(row == i, float(table[i, j]), values)
        tile = jnp.where(column == j, values, tile)
    return tile


def residual_kernel(
    u_hbm, source_hbm, metric_hbm, val_hbm, out_ref, u_ref, source_ref, metric_ref, val_ref, sems
):
    copies = [pltpu.make_async_copy(u_hbm, u_ref, sems.at[0])]
    copies += [
        pltpu.make_async_copy(metric_hbm.at[d], metric_ref.at[d], sems.at[1 + d])
        for d in range(metric_hbm.shape[0])
    ]
    copies.append(pltpu.make_async_copy(source_hbm, source_ref, sems.at[len(copies)]))
    copies.append(pltpu.make_async_copy(val_hbm, val_ref, sems.at[len(copies)]))
    for copy in copies:
        copy.start()
    nodes, rows, width = u_ref.shape
    flat_rows = nodes * rows
    table = np.asarray(derivative_table(), np.float32)
    along_y, along_z = [], []
    for t in range(2):
        tile = repeated_table(table if t == 0 else table.T, width)
        high = tile.astype(bf16).astype(f32)
        low = tile - high
        group = counted((nodes, width), 1) // nodes
        zero = jnp.zeros_like(tile)
        for part in (high, low):
            bands = [jnp.where(group == k, part, zero) for k in range(width // nodes)]
            along_z.append(jnp.concatenate(bands, axis=0).astype(bf16))
        group = group[:, 0 : 2 * flat_rows]
        high, low, zero = (v[:, 0 : 2 * flat_rows] for v in (high, low, zero))
        bands = [jnp.where(group % rows == k, high, zero) for k in range(nodes)]
        bands += [jnp.where(group == k, low, zero) for k in range(nodes)]
        along_y.append(jnp.concatenate(bands, axis=0).astype(bf16))

    def by_y(value, t):
        both = dot(along_y[t], jnp.concatenate(split2(value), axis=0))
        return both[0:flat_rows] + both[flat_rows:]

    def by_z(value, t):
        high, low = split2(value)
        both = dot(jnp.concatenate([high, low], axis=0), along_z[2 * t])
        return both[0:flat_rows] + (both[flat_rows:] + dot(high, along_z[2 * t + 1]))

    copies[0].wait()
    flat = u_ref[...].reshape(flat_rows, width)
    flux_y, flux_z = by_y(flat, 0), by_z(flat, 1)
    layers = [u_ref[j] for j in range(nodes)]
    flux_x = [sum(float(table[i, j]) * layers[j] for j in range(nodes)) for i in range(nodes)]
    for copy in copies[1:]:
        copy.wait()
    total = by_y(flux_y * metric_ref[1].reshape(flat.shape), 1)
    total = total + by_z(flux_z * metric_ref[2].reshape(flat.shape), 0)
    total = total.reshape(nodes, rows, width)
    flux_x = [metric_ref[0, i] * flux_x[i] for i in range(nodes)]
    for j in range(nodes):
        applied = sum(float(table[i, j]) * flux_x[i] for i in range(nodes))
        out_ref[j] = source_ref[j] - (applied + total[j])
    count, _, blocks = val_ref.shape
    values = val_ref[...].reshape(count, blocks)
    for first in range(0, count, rows):
        last = min(first + rows, count)
        out_ref[nodes + first // rows, 0 : last - first, 0:blocks] = values[first:last]


def layers_kernel(own_ref, partner_ref, out_ref):
    start = lax.axis_index("gz") * (out_ref.shape[2] - 2)
    for half, ref in enumerate((partner_ref, own_ref)):
        for layer in range(2):
            out_ref[half, layer] = ref[start + layer]


def taken(ref, first, count):
    return ref[first : first + count].reshape(count, ref.shape[2])


def spread(own, partner, ext):
    blocks = own.shape[1]
    parts = [*split3(own), *split3(partner)]
    shape = (blocks, 2 * blocks * ext)
    repeat = []
    for half in range(2):
        element = counted(shape, 1) // ext - half * blocks
        repeat += [(element == counted(shape, 0)).astype(f32).astype(bf16)] * 3
    return dot(jnp.concatenate(parts, axis=1), jnp.concatenate(repeat, axis=0))


def gathered(choice, value):
    choice = choice.astype(f32).astype(bf16)
    high, middle, low = split3(value)
    return dot(choice, high) + (dot(choice, middle) + dot(choice, low))


def x_coefficients_kernel(
    own_vec, partner_vec, own_ref, partner_ref, after_ref, cx_ref, cx_rows_ref, rate_ref
):
    ext, padded, lanes = rate_ref.shape
    blocks = own_vec.shape[2]
    nodes = ext - 2
    square = ext * ext
    along_x = spread(taken(own_vec, 0, square), taken(partner_vec, 0, square), ext)
    cx_ref[...] = along_x
    shape = (cx_rows_ref.shape[0], square)
    place = counted(shape, 0) % (shape[0] // ext) // 2
    choice = (place < ext) & (counted(shape, 1) == place * ext + counted(shape, 0) // (shape[0] // ext))
    cx_rows_ref[...] = gathered(choice, along_x)
    rates = []
    for ref in (own_ref, partner_ref):
        tiles = ref[nodes : ref.shape[0]]
        rates.append(tiles.reshape(-1, tiles.shape[2])[0 : 3 * ext, 0:blocks])
    rates = spread(*rates, ext)
    shape = (ext, lanes)
    rate_z = rates[2 * ext : 3 * ext]
    same = counted(shape, 0) == counted(shape, 1) % ext
    rate_z = jnp.sum(jnp.where(same, rate_z, jnp.zeros_like(rate_z)), axis=0, keepdims=True)
    rate_y = jnp.concatenate([rates[ext : 2 * ext], jnp.ones((padded - ext, lanes), f32)], axis=0)
    for p in range(ext):
        rate_ref[p] = 1.0 / (rates[p : p + 1] + rate_y + rate_z)


def y_coefficients_kernel(own_vec, partner_vec, after_ref, cy_ref):
    ext, padded = cy_ref.shape[1:3]
    square = ext * ext
    along_y = spread(taken(own_vec, square, square), taken(partner_vec, square, square), ext)
    shape = (ext * padded, square)
    first, second, entry = counted(shape, 0) // padded, counted(shape, 0) % padded, counted(shape, 1)
    forward = (second < ext) & (entry == first * ext + second)
    position = jnp.where(second < ext - 2, second + 1, jnp.where(second == ext - 2, 0, ext - 1))
    backward = (second < ext) & (entry == position * ext + first)
    for k, choice in enumerate((forward, backward)):
        cy_ref[k] = gathered(choice, along_y).reshape(cy_ref.shape[1:])


def z_coefficients_kernel(own_vec, partner_vec, after_ref, out_ref):
    ext, lanes = out_ref.shape
    square = ext * ext
    shape = (square, lanes)
    same = counted(shape, 0) % ext == counted(shape, 1) % ext
    along_z = spread(
        taken(own_vec, 2 * square, square), taken(partner_vec, 2 * square, square), ext
    )
    along_z = jnp.where(same, along_z, jnp.zeros_like(along_z))
    shape = (ext, square)
    out_ref[...] = gathered(counted(shape, 1) // ext == counted(shape, 0), along_z)


def z_matrix_kernel(along_z, after_ref, mz_ref, back_ref):
    ext, lanes = along_z.shape
    half = lanes // 2
    blocks = half // ext
    nodes = ext - 2
    core = lax.axis_index("gz")
    zeros = jnp.zeros((nodes - 2, lanes), f32)
    own = along_z[1 : nodes + 1, :]
    below = jnp.concatenate([zeros, along_z[0:2, :]], axis=0)
    above = jnp.concatenate([along_z[nodes : nodes + 2, :], zeros], axis=0)
    lane = counted((nodes, lanes), 1)
    first_own = core * blocks
    first_partner = blocks - first_own
    element = jnp.where(lane < half, lane // ext + first_own, (lane - half) // ext + first_partner)
    zero = jnp.zeros_like(own)
    rows = []
    for place in range(2 * blocks):
        block = place + first_own if place < blocks else place - blocks + first_partner
        value = jnp.where(element == block, own, zero)
        value = value + jnp.where(element == block + 1, below, zero)
        rows.append(value + jnp.where(element == block - 1, above, zero))
    matrix = jnp.concatenate(rows, axis=0)
    for ref, value in ((mz_ref, matrix), (back_ref, matrix.T)):
        ref[0], ref[1] = split2(value)


OUT_X, BACK_X, ALONG_Y = "out x", "back x", "along y"


def upper_core(leg, x, y):
    if leg == OUT_X:
        return 1 - x // 2 % 2
    return 0 if leg == BACK_X else x % 2


def trades_below(leg):
    x, y = lax.axis_index("gx"), lax.axis_index("gy")
    return lax.axis_index("gz") != upper_core(leg, x, y)


def meets_same(leg):
    x, y = lax.axis_index("gx"), lax.axis_index("gy")
    x = jnp.where(trades_below(leg), x - 1, x)
    return upper_core(leg, x, y) + upper_core(leg, x + 1, y) == 1


def sides(below, direct, passed):
    low = [jnp.where(below, direct[h], passed[1 - h]) for h in range(2)]
    high = [jnp.where(below, passed[1 - h], direct[h]) for h in range(2)]
    return low, high


def edges(axis):
    place, size = lax.axis_index(axis), lax.axis_size(axis)
    return place > 0, place < size - 1


def layers_kernel(own_ref, partner_ref, out_ref):
    start = jnp.where(trades_below(OUT_X), 0, out_ref.shape[2] - 2)
    same = meets_same(OUT_X)
    for layer in range(2):
        own, partner = own_ref[start + layer], partner_ref[start + layer]
        out_ref[0, layer] = jnp.where(same, own, partner)
        out_ref[1, layer] = jnp.where(same, partner, own)


def x_positions(own_ref, partner_ref, direct_ref, passed_ref):
    has_low, has_high = edges("gx")
    length = own_ref.shape[1]
    below = trades_below(OUT_X)
    outer = []
    for slot in range(2):
        direct = [direct_ref[h, slot] for h in range(2)]
        passed = [passed_ref[h, slot] for h in range(2)]
        low, high = sides(below, direct, passed)
        low = [jnp.where(has_low, v, jnp.zeros_like(v)) for v in low]
        high = [jnp.where(has_high, v, jnp.zeros_like(v)) for v in high]
        outer.append((low, high))
    positions = [outer[0][0]]
    for layer in range(length):
        value = [own_ref[layer], partner_ref[layer]]
        if layer == 0:
            value = [v + w for v, w in zip(outer[1][0], value)]
        if layer == length - 1:
            value = [v + w for v, w in zip(value, outer[0][1])]
        positions.append(value)
    return positions + [outer[1][1]]


def rows_kernel(own_ref, partner_ref, direct_ref, passed_ref, after_ref, out_ref):
    _, rows, width = own_ref.shape
    below = trades_below(ALONG_Y)
    positions = x_positions(own_ref, partner_ref, direct_ref, passed_ref)
    out_ref[out_ref.shape[0] - 1] = jnp.zeros(out_ref.shape[1:], f32)
    for a, (own, partner) in enumerate(positions):
        row = 2 * a % rows
        for half, value in enumerate((partner, own)):
            out_ref[2 * a // rows, row : row + 2, half * width : (half + 1) * width] = jnp.where(
                below, value[0:2], value[rows - 2 : rows]
            )


def by_z(value, matrix):
    rows = value.shape[0]
    spare = -rows % 16
    if spare:
        value = jnp.concatenate([value, jnp.zeros((spare, value.shape[1]), f32)], axis=0)
    high, low = split2(value)
    both = dot(jnp.concatenate([high, low], axis=0), matrix[0])
    total = both[0 : rows + spare] + (both[rows + spare :] + dot(high, matrix[1]))
    return total[0:rows]


def from_rows(value, use, mz, cx_rows, ext):
    count, rows, both = value.shape
    value = jnp.where(use, value, jnp.zeros_like(value))
    along_z = by_z(value.reshape(count * rows, both), mz)
    for p in range(ext):
        total = sum(
            cx_rows[(p * count + t) * rows : (p * count + t + 1) * rows, :]
            * along_z[t * rows : (t + 1) * rows]
            for t in range(count)
        )
        shift = 2
        while shift < rows:
            total = total + pltpu.roll(total, shift, 0)
            shift *= 2
        yield total


def interior_solve_kernel(
    own_ref, partner_ref, xd_ref, xp_ref, yd_ref, cx, cx_rows, cy, mz, out_ref, grid
):
    _, rows, width = own_ref.shape
    ext, padded, lanes = out_ref.shape
    nodes = ext - 2
    has_low, has_high = edges("gy")
    positions = x_positions(own_ref, partner_ref, xd_ref, xp_ref)
    for a, halves in enumerate(positions):
        for half, value in enumerate(halves):
            grid[a, :, half * width : (half + 1) * width] = value
    along_z = by_z(grid[...].reshape(ext * rows, 2 * width), mz)
    along_z = along_z.reshape(ext, rows, lanes)
    below = trades_below(ALONG_Y)
    use = jnp.where(below, has_low, has_high)
    outer = [cy[0, jnp.where(below, 0, nodes) + k] for k in range(2)]
    for p, value in enumerate(from_rows(yd_ref[...], use, mz, cx_rows, ext)):
        inner = sum(cx[a * ext + p : a * ext + p + 1, :] * along_z[a] for a in range(ext))
        total = sum(cy[0, b + 1] * inner[b : b + 1] for b in range(rows))
        out_ref[p] = total + sum(outer[k] * value[k : k + 1] for k in range(2))


def back_by_x(spectral, coefficients):
    return sum(c * spectral[p] for p, c in enumerate(coefficients))


def back_by_y(value, cy, ext):
    return sum(cy[1, q] * value[q : q + 1] for q in range(ext))


def solve_kernel(yp_ref, part_ref, cx, cx_rows, cy, rate, mz, mz_back, spectral, sent_ref):
    below = trades_below(ALONG_Y)
    width = yp_ref.shape[2] // 2
    ext, padded, lanes = rate.shape
    nodes = ext - 2
    has_low, has_high = edges("gy")
    passed = jnp.concatenate([yp_ref[:, :, width:], yp_ref[:, :, 0:width]], axis=2)
    use = jnp.where(below, has_high, has_low)
    outer = [cy[0, jnp.where(below, nodes, 0) + k] for k in range(2)]
    for p, value in enumerate(from_rows(passed, use, mz, cx_rows, ext)):
        total = part_ref[p] + sum(outer[k] * value[k : k + 1] for k in range(2))
        spectral[p] = total * rate[p]
    same = meets_same(BACK_X)
    layers = []
    for layer in range(2):
        rows = [layer * ext + p for p in range(ext)]
        last = [r + nodes * ext for r in rows]
        coefficients = [
            jnp.where(trades_below(BACK_X), cx[r : r + 1, :], cx[k : k + 1, :])
            for r, k in zip(rows, last)
        ]
        layers.append(back_by_y(back_by_x(spectral, coefficients), cy, ext))
    result = by_z(jnp.concatenate(layers, axis=0), mz_back)
    for layer in range(2):
        value = result[layer * padded : layer * padded + nodes + 2]
        own, partner = value[:, 0:width], value[:, width:]
        for half in range(2):
            place = half * 2 + layer
            value = jnp.where(same, own, partner) if half == 0 else jnp.where(same, partner, own)
            sent_ref[place] = value[0:nodes]
            sent_ref[4, 2 * place : 2 * place + 2, :] = value[nodes : nodes + 2]


def interior_kernel(spectral, cx, cy, mz_back, after_ref, out_ref):
    ext, padded, lanes = spectral.shape
    nodes, _, both = out_ref.shape
    layers = []
    for a in range(1, ext - 1):
        coefficients = [cx[a * ext + p : a * ext + p + 1, :] for p in range(ext)]
        layers.append(back_by_y(back_by_x(spectral, coefficients), cy, ext))
    result = by_z(jnp.concatenate(layers, axis=0), mz_back)
    out_ref[...] = result.reshape(nodes, padded, both)


def return_rows_kernel(initial_ref, inner_ref, direct_ref, passed_ref, out_ref, base_ref):
    has_low, has_high = edges("gx")
    below_x, below_y = trades_below(BACK_X), trades_below(ALONG_Y)
    nodes, rows, width = initial_ref.shape
    for layer in range(nodes):
        lanes = [slice(0, width), slice(width, 2 * width)]
        outer = [inner_ref[layer, rows : rows + 2, lanes[h]] for h in range(2)]
        values = [inner_ref[layer, 0:rows, lanes[h]] for h in range(2)]
        if layer < 2 or layer >= nodes - 2:
            slot = layer if layer < 2 else layer - (nodes - 2)

            def parts(ref, h, slot=slot):
                place = 2 * h + slot
                return ref[place], ref[4, 2 * place : 2 * place + 2, :]

            direct = [parts(direct_ref, h) for h in range(2)]
            passed = [parts(passed_ref, h) for h in range(2)]
            side = 0 if layer < 2 else 1
            valid = (has_low, has_high)[side]
            for k, target in enumerate((values, outer)):
                both = sides(below_x, [d[k] for d in direct], [d[k] for d in passed])[side]
                for h in range(2):
                    target[h] = target[h] + jnp.where(valid, both[h], jnp.zeros_like(both[h]))
        base_ref[layer] = initial_ref[layer] + values[0]
        for place, h in enumerate((1, 0)):
            first = jnp.where(below_y, outer[h][0:1], values[h][rows - 1 : rows])
            second = jnp.where(below_y, values[h][0:1], outer[h][1:2])
            out_ref[layer, :, lanes[place]] = jnp.concatenate([first, second], axis=0)


def result_kernel(base_ref, direct_ref, passed_ref, out_ref):
    below = trades_below(ALONG_Y)
    has_low, has_high = edges("gy")
    nodes, rows, width = base_ref.shape
    for layer in range(nodes):
        direct = direct_ref[layer, :, 0:width]
        passed = passed_ref[layer]
        low = jnp.where(below, direct, passed)
        high = jnp.where(below, passed, direct)
        low = jnp.where(has_low, low, jnp.zeros_like(low))
        high = jnp.where(has_high, high, jnp.zeros_like(high))
        between = jnp.zeros((rows - 4, low.shape[1]), f32)
        out_ref[layer] = base_ref[layer] + jnp.concatenate([low, between, high], axis=0)


def swap_pairs(leg):
    count_x, count_y = (lax.axis_size(name) for name in AXES[:2])
    last, others = (count_y - 1, count_x) if leg == ALONG_Y else (count_x - 1, count_y)

    def cores(place, other):
        x, y = (other, place) if leg == ALONG_Y else (place, other)
        upper, first = upper_core(leg, x, y), (x * count_y + y) * 2
        return first + upper, first + 1 - upper

    pairs, idle = [], []
    for other in range(others):
        line = [cores(place, other) for place in range(last + 1)]
        for place in range(last):
            here, there = line[place][0], line[place + 1][1]
            pairs += [(here, there), (there, here)]
        idle.append((line[0][1], line[last][0]))
    for one, two in zip(idle[0::2], idle[1::2]):
        for here, there in zip(one, two):
            pairs += [(here, there), (there, here)]
    return pairs


def swap_cores(value):
    return lax.ppermute(value, "gz", [(0, 1), (1, 0)])


def swap_chips(value, leg):
    return lax.ppermute(value, AXES, swap_pairs(leg))


def paired_body(initial, source, metric, eigenvectors, eigenvalues):
    nodes, rows, width = initial.shape
    ext = eigenvectors.shape[1]
    blocks = width // nodes
    lanes = 2 * blocks * ext
    padded = 2 * rows
    vectors = eigenvectors.reshape(3 * ext * ext, 1, blocks)
    values = eigenvalues.reshape(3 * ext, 1, blocks)
    inputs = [
        pltpu.with_memory_space_constraint(value, pltpu.HBM)
        for value in (initial, source, metric, values)
    ]
    own = call(
        residual_kernel,
        [shaped((nodes + -(-3 * ext // rows), rows, width))],
        inputs,
        scratch=[
            *(pltpu.VMEM(value.shape, value.dtype) for value in inputs),
            pltpu.SemaphoreType.DMA((3 + metric.shape[0],)),
        ],
        where=HBM,
    )[0]
    partner = swap_cores(own)
    vectors, own = lax.optimization_barrier((vectors, own))
    partner_vectors = swap_cores(vectors)
    sent = call(layers_kernel, [shaped((2, 2, rows, width))], [own, partner])[0]
    x_direct = swap_chips(sent, OUT_X)
    tiles = -(-2 * ext // rows)
    cx, cx_rows, rate = call(
        x_coefficients_kernel,
        [
            shaped((ext * ext, lanes)),
            shaped((ext * tiles * rows, lanes)),
            shaped((ext, padded, lanes)),
        ],
        [vectors, partner_vectors, own, partner, sent],
    )
    x_direct, cx, rate = lax.optimization_barrier((x_direct, cx, rate))
    x_passed = swap_cores(x_direct)
    along_z = call(
        z_coefficients_kernel,
        [shaped((ext, lanes))],
        [vectors, partner_vectors, x_direct],
    )[0]
    sent = call(
        rows_kernel,
        [shaped((tiles, rows, 2 * width))],
        [own, partner, x_direct, x_passed, along_z],
    )[0]
    y_direct = swap_chips(sent, ALONG_Y)
    cy = call(
        y_coefficients_kernel,
        [shaped((2, ext, padded, lanes))],
        [vectors, partner_vectors, sent],
    )[0]
    mz, mz_back = call(
        z_matrix_kernel,
        [shaped((2, 2 * width, lanes), bf16), shaped((2, lanes, 2 * width), bf16)],
        [along_z, cy],
    )
    y_direct, cy, mz = lax.optimization_barrier((y_direct, cy, mz))
    y_passed = swap_cores(y_direct)
    part = call(
        interior_solve_kernel,
        [shaped((ext, padded, lanes))],
        [own, partner, x_direct, x_passed, y_direct, cx, cx_rows, cy, mz],
        scratch=[pltpu.VMEM((ext, rows, 2 * width), f32)],
    )[0]
    spectral, sent = call(
        solve_kernel,
        [shaped((ext, padded, lanes)), shaped((5, rows, width))],
        [y_passed, part, cx, cx_rows, cy, rate, mz, mz_back],
    )

    x_direct = swap_chips(sent, BACK_X)
    inner = call(interior_kernel, [shaped((nodes, padded, 2 * width))], [spectral, cx, cy, mz_back, sent])[0]
    x_passed = swap_cores(x_direct)
    sent, base = call(
        return_rows_kernel,
        [shaped((nodes, 2, 2 * width)), shaped(initial.shape)],
        [initial, inner, x_direct, x_passed],
    )
    y_direct = swap_chips(sent, ALONG_Y)
    y_passed = swap_cores(y_direct[:, :, width:])
    return call(result_kernel, [shaped(initial.shape)], [base, y_direct, y_passed])[0]


def body(initial, source, metric, eigenvectors, eigenvalues):
    nodes = gll_points.shape[0]
    one_element = initial.shape[0] == nodes and initial.shape[1] == nodes
    if lax.axis_size("gz") == 2 and one_element and initial.shape[2] % 128 == 0:
        return paired_body(initial, source, metric, eigenvectors, eigenvalues)
    return general_body(initial, source, metric, eigenvectors, eigenvalues)


def solution(mesh):
    placed = (
        P("gx", "gy", "gz"),
        P("gx", "gy", "gz"),
        P(None, "gx", "gy", "gz"),
        P(None, None, None, "gx", "gy", "gz"),
        P(None, None, "gx", "gy", "gz"),
    )
    return jax.shard_map(
        body, mesh=mesh, in_specs=placed, out_specs=P("gx", "gy", "gz"), check_vma=False
    )
```

```python
import functools

import jax
import jax.numpy as jnp
import numpy as np
from jax import lax
from jax.experimental import pallas as pl
from jax.experimental.pallas import tpu as pltpu
from jax.sharding import PartitionSpec as P

gll_points = np.array(
    [
        -1.0,
        -0.8717401485096066,
        -0.5917001814331423,
        -0.2092992179024789,
        0.2092992179024789,
        0.5917001814331423,
        0.8717401485096066,
        1.0,
    ]
)


def extended_2(value, sides, width):
    for axis, dim in sides:
        size, length = (lax.axis_size(axis), value.shape[dim])
        up = [(i, (i + 1) % size) for i in range(size - 1)]
        down = [(j, i) for i, j in up]
        last = lax.slice_in_dim(value, length - width, length, axis=dim)
        first = lax.slice_in_dim(value, 0, width, axis=dim)
        before = lax.ppermute(last, axis, up)
        after = lax.ppermute(first, axis, down)
        value = jnp.concatenate([before, value, after], axis=dim)
    return value


def derivative_table():
    number = gll_points.shape[0]
    products = np.array(
        [
            np.prod(
                [
                    gll_points[row_index] - gll_points[other]
                    for other in range(number)
                    if other != row_index
                ]
            )
            for row_index in range(number)
        ]
    )
    matrix_out = np.zeros((number, number))
    for row_index in range(number):
        for col_index in range(number):
            if row_index != col_index:
                matrix_out[row_index, col_index] = (
                    products[row_index]
                    / products[col_index]
                    / (gll_points[row_index] - gll_points[col_index])
                )
        matrix_out[row_index, row_index] = -np.sum(matrix_out[row_index])
    return matrix_out


def apply_along(values, matrix, direction):
    block_size = matrix.shape[1]
    old_shape = values.shape
    pieces_shape = (
        old_shape[:direction]
        + (old_shape[direction] // block_size, block_size)
        + old_shape[direction + 1 :]
    )
    result = jnp.tensordot(
        values.reshape(pieces_shape),
        matrix,
        axes=((direction + 1,), (1,)),
        precision=lax.Precision.HIGHEST,
    )
    result = jnp.moveaxis(result, -1, direction + 1)
    return result.reshape(
        old_shape[:direction]
        + (old_shape[direction] // block_size * matrix.shape[0],)
        + old_shape[direction + 1 :]
    )


def apply_operator(values, metric):
    deriv_table = jnp.asarray(derivative_table(), jnp.float32)
    summed = jnp.zeros_like(values)
    for direction in range(3):
        gradient = apply_along(values, deriv_table, direction)
        summed = summed + apply_along(metric[direction] * gradient, deriv_table.T, direction)
    return summed


def assemble(padded, offset):
    result = padded
    for direction in range(3):
        length = result.shape[direction]
        view_shape = [1, 1, 1]
        view_shape[direction] = length
        node_index = ((jnp.arange(length) - offset) % 8).reshape(view_shape)
        edge_zero = jnp.zeros_like(lax.slice_in_dim(result, 0, 1, axis=direction))
        upward = jnp.concatenate(
            [lax.slice_in_dim(result, 1, length, axis=direction), edge_zero], axis=direction
        )
        downward = jnp.concatenate(
            [edge_zero, lax.slice_in_dim(result, 0, length - 1, axis=direction)], axis=direction
        )
        result = (
            result
            + jnp.where(node_index == 7, upward, 0.0)
            + jnp.where(node_index == 0, downward, 0.0)
        )
    return result


def extend_axis(padded, direction):
    shifted = jnp.moveaxis(padded, direction, 0)
    blocks = (shifted.shape[0] - 4) // 8
    trailing = shifted.shape[1:]
    middle = shifted[2:-2].reshape((blocks, 8) + trailing)
    lowest = shifted[0 : 8 * blocks : 8][:, None]
    beyond = shifted[11::8][:, None]
    joined = jnp.concatenate([lowest, middle, beyond], axis=1).reshape((blocks * 10,) + trailing)
    return jnp.moveaxis(joined, 0, direction)


def widen(padded):
    return extend_axis(extend_axis(extend_axis(padded, 0), 1), 2)


def fast_solve(extended, eigenvectors, eigenvalues):
    count_x, count_y, count_z = eigenvectors.shape[3:]
    precise = lax.Precision.HIGHEST
    spectral = extended.reshape(count_x, 10, count_y, 10, count_z, 10)
    spectral = jnp.einsum("apxyz,xaybzc->xpybzc", eigenvectors[0], spectral, precision=precise)
    spectral = jnp.einsum("bqxyz,xpybzc->xpyqzc", eigenvectors[1], spectral, precision=precise)
    spectral = jnp.einsum("csxyz,xpyqzc->xpyqzs", eigenvectors[2], spectral, precision=precise)
    rate_x = jnp.transpose(eigenvalues[0], (1, 0, 2, 3))[:, :, :, None, :, None]
    rate_y = jnp.transpose(eigenvalues[1], (1, 2, 0, 3))[:, None, :, :, :, None]
    rate_z = jnp.transpose(eigenvalues[2], (1, 2, 3, 0))[:, None, :, None, :, :]
    spectral = spectral / (rate_x + rate_y + rate_z)
    spectral = jnp.einsum("csxyz,xpyqzs->xpyqzc", eigenvectors[2], spectral, precision=precise)
    spectral = jnp.einsum("bqxyz,xpyqzc->xpybzc", eigenvectors[1], spectral, precision=precise)
    spectral = jnp.einsum("apxyz,xpybzc->xaybzc", eigenvectors[0], spectral, precision=precise)
    return spectral.reshape(count_x * 10, count_y * 10, count_z * 10)


def return_axis(padded, direction):
    shifted = jnp.moveaxis(padded, direction, 0)
    blocks = (shifted.shape[0] - 4) // 10
    trailing = shifted.shape[1:]
    owned = shifted[2:-2].reshape((blocks, 10) + trailing)[:, 1:9]
    before = shifted[0 : 10 * blocks].reshape((blocks, 10) + trailing)[:, 0:2]
    following = shifted[4:].reshape((blocks, 10) + trailing)[:, 8:10]
    middle = jnp.zeros((blocks, 4) + trailing, shifted.dtype)
    summed = owned + jnp.concatenate([before, middle, following], axis=1)
    return jnp.moveaxis(summed.reshape((blocks * 8,) + trailing), 0, direction)


def general_body(initial, source, metric, eigenvectors, eigenvalues):
    solution = initial
    local_res = source - apply_operator(solution, metric)
    deeper = extended_2(local_res, (("gx", 0), ("gy", 1), ("gz", 2)), 2)
    widened = assemble(deeper, 2)
    extended = widen(widened)
    corrected = fast_solve(extended, eigenvectors, eigenvalues)
    padded = extended_2(corrected, (("gx", 0), ("gy", 1), ("gz", 2)), 2)
    correction = return_axis(return_axis(return_axis(padded, 0), 1), 2)
    solution = solution + correction
    return solution


AXES = ("gx", "gy", "gz")
VMEM = pl.BlockSpec(memory_space=pltpu.VMEM)
HBM = pl.BlockSpec(memory_space=pltpu.HBM)
VMEM_LIMIT = 16 * 2**20
f32 = jnp.float32
bf16 = jnp.bfloat16


def call(kernel, outs, args, scratch=(), where=VMEM):
    moved = sum(int(np.prod(a.shape)) * a.dtype.itemsize for a in (*args, *outs))
    return pl.pallas_call(
        kernel,
        out_shape=outs,
        in_specs=[where] * len(args),
        out_specs=[VMEM] * len(outs),
        scratch_shapes=scratch,
        compiler_params=pltpu.CompilerParams(vmem_limit_bytes=VMEM_LIMIT),
        cost_estimate=pl.CostEstimate(flops=0, bytes_accessed=moved, transcendentals=0),
    )(*args)


def shaped(shape, dtype=f32):
    return jax.ShapeDtypeStruct(shape, dtype)


def counted(shape, axis):
    return lax.broadcasted_iota(jnp.int32, shape, axis)


def split2(value):
    high = value.astype(bf16)
    return high, (value - high.astype(f32)).astype(bf16)


def split3(value):
    high = value.astype(bf16)
    rest = value - high.astype(f32)
    middle = rest.astype(bf16)
    return high, middle, (rest - middle.astype(f32)).astype(bf16)


def dot(left, right):
    return jnp.dot(left, right, preferred_element_type=f32)


def repeated_table(table, width):
    nodes = table.shape[0]
    row, column = counted((nodes, width), 0), counted((nodes, width), 1) % nodes
    tile = jnp.zeros((nodes, width), f32)
    for j in range(nodes):
        values = jnp.zeros((nodes, width), f32)
        for i in range(nodes):
            values = jnp.where(row == i, float(table[i, j]), values)
        tile = jnp.where(column == j, values, tile)
    return tile


def residual_kernel(
    u_hbm, source_hbm, metric_hbm, val_hbm, out_ref, u_ref, source_ref, metric_ref, val_ref, sems
):
    copies = [pltpu.make_async_copy(u_hbm, u_ref, sems.at[0])]
    copies += [
        pltpu.make_async_copy(metric_hbm.at[d], metric_ref.at[d], sems.at[1 + d])
        for d in range(metric_hbm.shape[0])
    ]
    copies.append(pltpu.make_async_copy(source_hbm, source_ref, sems.at[len(copies)]))
    copies.append(pltpu.make_async_copy(val_hbm, val_ref, sems.at[len(copies)]))
    for copy in copies:
        copy.start()
    nodes, rows, width = u_ref.shape
    flat_rows = nodes * rows
    table = np.asarray(derivative_table(), np.float32)
    along_y, along_z = [], []
    for t in range(2):
        tile = repeated_table(table if t == 0 else table.T, width)
        high = tile.astype(bf16).astype(f32)
        low = tile - high
        group = counted((nodes, width), 1) // nodes
        zero = jnp.zeros_like(tile)
        for part in (high, low):
            bands = [jnp.where(group == k, part, zero) for k in range(width // nodes)]
            along_z.append(jnp.concatenate(bands, axis=0).astype(bf16))
        group = group[:, 0 : 2 * flat_rows]
        high, low, zero = (v[:, 0 : 2 * flat_rows] for v in (high, low, zero))
        bands = [jnp.where(group % rows == k, high, zero) for k in range(nodes)]
        bands += [jnp.where(group == k, low, zero) for k in range(nodes)]
        along_y.append(jnp.concatenate(bands, axis=0).astype(bf16))

    def by_y(value, t):
        both = dot(along_y[t], jnp.concatenate(split2(value), axis=0))
        return both[0:flat_rows] + both[flat_rows:]

    def by_z(value, t):
        high, low = split2(value)
        both = dot(jnp.concatenate([high, low], axis=0), along_z[2 * t])
        return both[0:flat_rows] + (both[flat_rows:] + dot(high, along_z[2 * t + 1]))

    copies[0].wait()
    flat = u_ref[...].reshape(flat_rows, width)
    flux_y, flux_z = by_y(flat, 0), by_z(flat, 1)
    layers = [u_ref[j] for j in range(nodes)]
    flux_x = [sum(float(table[i, j]) * layers[j] for j in range(nodes)) for i in range(nodes)]
    for copy in copies[1:]:
        copy.wait()
    total = by_y(flux_y * metric_ref[1].reshape(flat.shape), 1)
    total = total + by_z(flux_z * metric_ref[2].reshape(flat.shape), 0)
    total = total.reshape(nodes, rows, width)
    flux_x = [metric_ref[0, i] * flux_x[i] for i in range(nodes)]
    for j in range(nodes):
        applied = sum(float(table[i, j]) * flux_x[i] for i in range(nodes))
        out_ref[j] = source_ref[j] - (applied + total[j])
    count, _, blocks = val_ref.shape
    values = val_ref[...].reshape(count, blocks)
    for first in range(0, count, rows):
        last = min(first + rows, count)
        out_ref[nodes + first // rows, 0 : last - first, 0:blocks] = values[first:last]


def layers_kernel(own_ref, partner_ref, out_ref):
    start = lax.axis_index("gz") * (out_ref.shape[2] - 2)
    for half, ref in enumerate((partner_ref, own_ref)):
        for layer in range(2):
            out_ref[half, layer] = ref[start + layer]


def taken(ref, first, count):
    return ref[first : first + count].reshape(count, ref.shape[2])


def spread(own, partner, ext):
    blocks = own.shape[1]
    parts = [*split3(own), *split3(partner)]
    shape = (blocks, 2 * blocks * ext)
    repeat = []
    for half in range(2):
        element = counted(shape, 1) // ext - half * blocks
        repeat += [(element == counted(shape, 0)).astype(f32).astype(bf16)] * 3
    return dot(jnp.concatenate(parts, axis=1), jnp.concatenate(repeat, axis=0))


def gathered(choice, value):
    choice = choice.astype(f32).astype(bf16)
    high, middle, low = split3(value)
    return dot(choice, high) + (dot(choice, middle) + dot(choice, low))


def x_coefficients_kernel(
    own_vec, partner_vec, own_ref, partner_ref, after_ref, cx_ref, cx_rows_ref, rate_ref
):
    ext, padded, lanes = rate_ref.shape
    blocks = own_vec.shape[2]
    nodes = ext - 2
    square = ext * ext
    along_x = spread(taken(own_vec, 0, square), taken(partner_vec, 0, square), ext)
    cx_ref[...] = along_x
    shape = (cx_rows_ref.shape[0], square)
    place = counted(shape, 0) % (shape[0] // ext) // 2
    choice = (place < ext) & (counted(shape, 1) == place * ext + counted(shape, 0) // (shape[0] // ext))
    cx_rows_ref[...] = gathered(choice, along_x)
    rates = []
    for ref in (own_ref, partner_ref):
        tiles = ref[nodes : ref.shape[0]]
        rates.append(tiles.reshape(-1, tiles.shape[2])[0 : 3 * ext, 0:blocks])
    rates = spread(*rates, ext)
    shape = (ext, lanes)
    rate_z = rates[2 * ext : 3 * ext]
    same = counted(shape, 0) == counted(shape, 1) % ext
    rate_z = jnp.sum(jnp.where(same, rate_z, jnp.zeros_like(rate_z)), axis=0, keepdims=True)
    rate_y = jnp.concatenate([rates[ext : 2 * ext], jnp.ones((padded - ext, lanes), f32)], axis=0)
    for p in range(ext):
        rate_ref[p] = 1.0 / (rates[p : p + 1] + rate_y + rate_z)


def y_coefficients_kernel(own_vec, partner_vec, after_ref, cy_ref):
    ext, padded = cy_ref.shape[1:3]
    square = ext * ext
    along_y = spread(taken(own_vec, square, square), taken(partner_vec, square, square), ext)
    shape = (ext * padded, square)
    first, second, entry = counted(shape, 0) // padded, counted(shape, 0) % padded, counted(shape, 1)
    forward = (second < ext) & (entry == first * ext + second)
    position = jnp.where(second < ext - 2, second + 1, jnp.where(second == ext - 2, 0, ext - 1))
    backward = (second < ext) & (entry == position * ext + first)
    for k, choice in enumerate((forward, backward)):
        cy_ref[k] = gathered(choice, along_y).reshape(cy_ref.shape[1:])


def z_coefficients_kernel(own_vec, partner_vec, after_ref, out_ref):
    ext, lanes = out_ref.shape
    square = ext * ext
    shape = (square, lanes)
    same = counted(shape, 0) % ext == counted(shape, 1) % ext
    along_z = spread(
        taken(own_vec, 2 * square, square), taken(partner_vec, 2 * square, square), ext
    )
    along_z = jnp.where(same, along_z, jnp.zeros_like(along_z))
    shape = (ext, square)
    out_ref[...] = gathered(counted(shape, 1) // ext == counted(shape, 0), along_z)


def z_matrix_kernel(along_z, after_ref, mz_ref, back_ref):
    ext, lanes = along_z.shape
    half = lanes // 2
    blocks = half // ext
    nodes = ext - 2
    core = lax.axis_index("gz")
    zeros = jnp.zeros((nodes - 2, lanes), f32)
    own = along_z[1 : nodes + 1, :]
    below = jnp.concatenate([zeros, along_z[0:2, :]], axis=0)
    above = jnp.concatenate([along_z[nodes : nodes + 2, :], zeros], axis=0)
    lane = counted((nodes, lanes), 1)
    first_own = core * blocks
    first_partner = blocks - first_own
    element = jnp.where(lane < half, lane // ext + first_own, (lane - half) // ext + first_partner)
    zero = jnp.zeros_like(own)
    rows = []
    for place in range(2 * blocks):
        block = place + first_own if place < blocks else place - blocks + first_partner
        value = jnp.where(element == block, own, zero)
        value = value + jnp.where(element == block + 1, below, zero)
        rows.append(value + jnp.where(element == block - 1, above, zero))
    matrix = jnp.concatenate(rows, axis=0)
    for ref, value in ((mz_ref, matrix), (back_ref, matrix.T)):
        ref[0], ref[1] = split2(value)


OUT_X, BACK_X, OUT_Y, BACK_Y = "out x", "back x", "out y", "back y"


def upper_core(leg, x, y):
    if leg == OUT_X:
        return 1 - x // 2 % 2
    if leg == BACK_X:
        return 0
    return x % 2 if leg == OUT_Y else (x + 1) // 2 % 2


def trades_below(leg):
    x, y = lax.axis_index("gx"), lax.axis_index("gy")
    return lax.axis_index("gz") != upper_core(leg, x, y)


def meets_same(leg):
    x, y = lax.axis_index("gx"), lax.axis_index("gy")
    x = jnp.where(trades_below(leg), x - 1, x)
    return upper_core(leg, x, y) + upper_core(leg, x + 1, y) == 1


def sides(below, direct, passed):
    low = [jnp.where(below, direct[h], passed[1 - h]) for h in range(2)]
    high = [jnp.where(below, passed[1 - h], direct[h]) for h in range(2)]
    return low, high


def edges(axis):
    place, size = lax.axis_index(axis), lax.axis_size(axis)
    return place > 0, place < size - 1


def layers_kernel(own_ref, partner_ref, out_ref):
    start = jnp.where(trades_below(OUT_X), 0, out_ref.shape[2] - 2)
    same = meets_same(OUT_X)
    for layer in range(2):
        own, partner = own_ref[start + layer], partner_ref[start + layer]
        out_ref[0, layer] = jnp.where(same, own, partner)
        out_ref[1, layer] = jnp.where(same, partner, own)


def x_positions(own_ref, partner_ref, direct_ref, passed_ref):
    has_low, has_high = edges("gx")
    length = own_ref.shape[1]
    below = trades_below(OUT_X)
    outer = []
    for slot in range(2):
        direct = [direct_ref[h, slot] for h in range(2)]
        passed = [passed_ref[h, slot] for h in range(2)]
        low, high = sides(below, direct, passed)
        low = [jnp.where(has_low, v, jnp.zeros_like(v)) for v in low]
        high = [jnp.where(has_high, v, jnp.zeros_like(v)) for v in high]
        outer.append((low, high))
    positions = [outer[0][0]]
    for layer in range(length):
        value = [own_ref[layer], partner_ref[layer]]
        if layer == 0:
            value = [v + w for v, w in zip(outer[1][0], value)]
        if layer == length - 1:
            value = [v + w for v, w in zip(value, outer[0][1])]
        positions.append(value)
    return positions + [outer[1][1]]


def rows_kernel(own_ref, partner_ref, direct_ref, passed_ref, after_ref, out_ref):
    _, rows, width = own_ref.shape
    below = trades_below(OUT_Y)
    positions = x_positions(own_ref, partner_ref, direct_ref, passed_ref)
    out_ref[out_ref.shape[0] - 1] = jnp.zeros(out_ref.shape[1:], f32)
    for a, (own, partner) in enumerate(positions):
        row = 2 * a % rows
        for half, value in enumerate((partner, own)):
            out_ref[2 * a // rows, row : row + 2, half * width : (half + 1) * width] = jnp.where(
                below, value[0:2], value[rows - 2 : rows]
            )


def by_z(value, matrix):
    rows = value.shape[0]
    spare = -rows % 16
    if spare:
        value = jnp.concatenate([value, jnp.zeros((spare, value.shape[1]), f32)], axis=0)
    high, low = split2(value)
    both = dot(jnp.concatenate([high, low], axis=0), matrix[0])
    total = both[0 : rows + spare] + (both[rows + spare :] + dot(high, matrix[1]))
    return total[0:rows]


def from_rows(value, use, mz, cx_rows, ext):
    count, rows, both = value.shape
    value = jnp.where(use, value, jnp.zeros_like(value))
    along_z = by_z(value.reshape(count * rows, both), mz)
    for p in range(ext):
        total = sum(
            cx_rows[(p * count + t) * rows : (p * count + t + 1) * rows, :]
            * along_z[t * rows : (t + 1) * rows]
            for t in range(count)
        )
        shift = 2
        while shift < rows:
            total = total + pltpu.roll(total, shift, 0)
            shift *= 2
        yield total


def interior_solve_kernel(
    own_ref, partner_ref, xd_ref, xp_ref, yd_ref, cx, cx_rows, cy, mz, out_ref, grid
):
    _, rows, width = own_ref.shape
    ext, padded, lanes = out_ref.shape
    nodes = ext - 2
    has_low, has_high = edges("gy")
    positions = x_positions(own_ref, partner_ref, xd_ref, xp_ref)
    for a, halves in enumerate(positions):
        for half, value in enumerate(halves):
            grid[a, :, half * width : (half + 1) * width] = value
    along_z = by_z(grid[...].reshape(ext * rows, 2 * width), mz)
    along_z = along_z.reshape(ext, rows, lanes)
    below = trades_below(OUT_Y)
    use = jnp.where(below, has_low, has_high)
    outer = [cy[0, jnp.where(below, 0, nodes) + k] for k in range(2)]
    for p, value in enumerate(from_rows(yd_ref[...], use, mz, cx_rows, ext)):
        inner = sum(cx[a * ext + p : a * ext + p + 1, :] * along_z[a] for a in range(ext))
        total = sum(cy[0, b + 1] * inner[b : b + 1] for b in range(rows))
        out_ref[p] = total + sum(outer[k] * value[k : k + 1] for k in range(2))


def back_by_x(spectral, coefficients):
    return sum(c * spectral[p] for p, c in enumerate(coefficients))


def back_by_y(value, cy, ext):
    return sum(cy[1, q] * value[q : q + 1] for q in range(ext))


def solve_kernel(yp_ref, part_ref, cx, cx_rows, cy, rate, mz, mz_back, spectral, sent_ref):
    below = trades_below(OUT_Y)
    width = yp_ref.shape[2] // 2
    ext, padded, lanes = rate.shape
    nodes = ext - 2
    has_low, has_high = edges("gy")
    passed = jnp.concatenate([yp_ref[:, :, width:], yp_ref[:, :, 0:width]], axis=2)
    use = jnp.where(below, has_high, has_low)
    outer = [cy[0, jnp.where(below, nodes, 0) + k] for k in range(2)]
    for p, value in enumerate(from_rows(passed, use, mz, cx_rows, ext)):
        total = part_ref[p] + sum(outer[k] * value[k : k + 1] for k in range(2))
        spectral[p] = total * rate[p]
    same = meets_same(BACK_X)
    layers = []
    for layer in range(2):
        rows = [layer * ext + p for p in range(ext)]
        last = [r + nodes * ext for r in rows]
        coefficients = [
            jnp.where(trades_below(BACK_X), cx[r : r + 1, :], cx[k : k + 1, :])
            for r, k in zip(rows, last)
        ]
        layers.append(back_by_y(back_by_x(spectral, coefficients), cy, ext))
    result = by_z(jnp.concatenate(layers, axis=0), mz_back)
    for layer in range(2):
        value = result[layer * padded : layer * padded + nodes + 2]
        own, partner = value[:, 0:width], value[:, width:]
        for half in range(2):
            place = half * 2 + layer
            value = jnp.where(same, own, partner) if half == 0 else jnp.where(same, partner, own)
            sent_ref[place] = value[0:nodes]
            sent_ref[4, 2 * place : 2 * place + 2, :] = value[nodes : nodes + 2]


def interior_kernel(spectral, cx, cy, mz_back, after_ref, out_ref):
    ext, padded, lanes = spectral.shape
    nodes, _, both = out_ref.shape
    layers = []
    for a in range(1, ext - 1):
        coefficients = [cx[a * ext + p : a * ext + p + 1, :] for p in range(ext)]
        layers.append(back_by_y(back_by_x(spectral, coefficients), cy, ext))
    result = by_z(jnp.concatenate(layers, axis=0), mz_back)
    out_ref[...] = result.reshape(nodes, padded, both)


def return_rows_kernel(initial_ref, inner_ref, direct_ref, passed_ref, out_ref, base_ref):
    has_low, has_high = edges("gx")
    below_x, below_y = trades_below(BACK_X), trades_below(BACK_Y)
    nodes, rows, width = initial_ref.shape
    for layer in range(nodes):
        lanes = [slice(0, width), slice(width, 2 * width)]
        outer = [inner_ref[layer, rows : rows + 2, lanes[h]] for h in range(2)]
        values = [inner_ref[layer, 0:rows, lanes[h]] for h in range(2)]
        if layer < 2 or layer >= nodes - 2:
            slot = layer if layer < 2 else layer - (nodes - 2)

            def parts(ref, h, slot=slot):
                place = 2 * h + slot
                return ref[place], ref[4, 2 * place : 2 * place + 2, :]

            direct = [parts(direct_ref, h) for h in range(2)]
            passed = [parts(passed_ref, h) for h in range(2)]
            side = 0 if layer < 2 else 1
            valid = (has_low, has_high)[side]
            for k, target in enumerate((values, outer)):
                both = sides(below_x, [d[k] for d in direct], [d[k] for d in passed])[side]
                for h in range(2):
                    target[h] = target[h] + jnp.where(valid, both[h], jnp.zeros_like(both[h]))
        base_ref[layer] = initial_ref[layer] + values[0]
        for place, h in enumerate((1, 0)):
            first = jnp.where(below_y, outer[h][0:1], values[h][rows - 1 : rows])
            second = jnp.where(below_y, values[h][0:1], outer[h][1:2])
            out_ref[layer, :, lanes[place]] = jnp.concatenate([first, second], axis=0)


def result_kernel(base_ref, direct_ref, passed_ref, out_ref):
    below = trades_below(BACK_Y)
    has_low, has_high = edges("gy")
    nodes, rows, width = base_ref.shape
    for layer in range(nodes):
        direct = direct_ref[layer, :, 0:width]
        passed = passed_ref[layer]
        low = jnp.where(below, direct, passed)
        high = jnp.where(below, passed, direct)
        low = jnp.where(has_low, low, jnp.zeros_like(low))
        high = jnp.where(has_high, high, jnp.zeros_like(high))
        between = jnp.zeros((rows - 4, low.shape[1]), f32)
        out_ref[layer] = base_ref[layer] + jnp.concatenate([low, between, high], axis=0)


def swap_pairs(leg):
    count_x, count_y = (lax.axis_size(name) for name in AXES[:2])
    by_y = leg in (OUT_Y, BACK_Y)
    last, others = (count_y - 1, count_x) if by_y else (count_x - 1, count_y)

    def cores(place, other):
        x, y = (other, place) if by_y else (place, other)
        upper, first = upper_core(leg, x, y), (x * count_y + y) * 2
        return first + upper, first + 1 - upper

    pairs, idle = [], []
    for other in range(others):
        line = [cores(place, other) for place in range(last + 1)]
        for place in range(last):
            here, there = line[place][0], line[place + 1][1]
            pairs += [(here, there), (there, here)]
        idle.append((line[0][1], line[last][0]))
    step = 2 if leg == BACK_Y and others % 4 == 0 else 1
    for other in range(others - step):
        if other // step % 2 == 0:
            for here, there in zip(idle[other], idle[other + step]):
                pairs += [(here, there), (there, here)]
    return pairs


def swap_cores(value):
    return lax.ppermute(value, "gz", [(0, 1), (1, 0)])


def swap_chips(value, leg):
    return lax.ppermute(value, AXES, swap_pairs(leg))


def paired_body(initial, source, metric, eigenvectors, eigenvalues):
    nodes, rows, width = initial.shape
    ext = eigenvectors.shape[1]
    blocks = width // nodes
    lanes = 2 * blocks * ext
    padded = 2 * rows
    vectors = eigenvectors.reshape(3 * ext * ext, 1, blocks)
    values = eigenvalues.reshape(3 * ext, 1, blocks)
    inputs = [
        pltpu.with_memory_space_constraint(value, pltpu.HBM)
        for value in (initial, source, metric, values)
    ]
    own = call(
        residual_kernel,
        [shaped((nodes + -(-3 * ext // rows), rows, width))],
        inputs,
        scratch=[
            *(pltpu.VMEM(value.shape, value.dtype) for value in inputs),
            pltpu.SemaphoreType.DMA((3 + metric.shape[0],)),
        ],
        where=HBM,
    )[0]
    partner = swap_cores(own)
    vectors, own = lax.optimization_barrier((vectors, own))
    partner_vectors = swap_cores(vectors)
    sent = call(layers_kernel, [shaped((2, 2, rows, width))], [own, partner])[0]
    x_direct = swap_chips(sent, OUT_X)
    tiles = -(-2 * ext // rows)
    cx, cx_rows, rate = call(
        x_coefficients_kernel,
        [
            shaped((ext * ext, lanes)),
            shaped((ext * tiles * rows, lanes)),
            shaped((ext, padded, lanes)),
        ],
        [vectors, partner_vectors, own, partner, sent],
    )
    x_direct, cx, rate = lax.optimization_barrier((x_direct, cx, rate))
    x_passed = swap_cores(x_direct)
    along_z = call(
        z_coefficients_kernel,
        [shaped((ext, lanes))],
        [vectors, partner_vectors, x_direct],
    )[0]
    sent = call(
        rows_kernel,
        [shaped((tiles, rows, 2 * width))],
        [own, partner, x_direct, x_passed, along_z],
    )[0]
    y_direct = swap_chips(sent, OUT_Y)
    cy = call(
        y_coefficients_kernel,
        [shaped((2, ext, padded, lanes))],
        [vectors, partner_vectors, sent],
    )[0]
    mz, mz_back = call(
        z_matrix_kernel,
        [shaped((2, 2 * width, lanes), bf16), shaped((2, lanes, 2 * width), bf16)],
        [along_z, cy],
    )
    y_direct, cy, mz = lax.optimization_barrier((y_direct, cy, mz))
    y_passed = swap_cores(y_direct)
    part = call(
        interior_solve_kernel,
        [shaped((ext, padded, lanes))],
        [own, partner, x_direct, x_passed, y_direct, cx, cx_rows, cy, mz],
        scratch=[pltpu.VMEM((ext, rows, 2 * width), f32)],
    )[0]
    spectral, sent = call(
        solve_kernel,
        [shaped((ext, padded, lanes)), shaped((5, rows, width))],
        [y_passed, part, cx, cx_rows, cy, rate, mz, mz_back],
    )

    x_direct = swap_chips(sent, BACK_X)
    inner = call(interior_kernel, [shaped((nodes, padded, 2 * width))], [spectral, cx, cy, mz_back, sent])[0]
    x_passed = swap_cores(x_direct)
    sent, base = call(
        return_rows_kernel,
        [shaped((nodes, 2, 2 * width)), shaped(initial.shape)],
        [initial, inner, x_direct, x_passed],
    )
    y_direct = swap_chips(sent, BACK_Y)
    y_passed = swap_cores(y_direct[:, :, width:])
    return call(result_kernel, [shaped(initial.shape)], [base, y_direct, y_passed])[0]


def body(initial, source, metric, eigenvectors, eigenvalues):
    nodes = gll_points.shape[0]
    one_element = initial.shape[0] == nodes and initial.shape[1] == nodes
    if lax.axis_size("gz") == 2 and one_element and initial.shape[2] % 128 == 0:
        return paired_body(initial, source, metric, eigenvectors, eigenvalues)
    return general_body(initial, source, metric, eigenvectors, eigenvalues)


def solution(mesh):
    placed = (
        P("gx", "gy", "gz"),
        P("gx", "gy", "gz"),
        P(None, "gx", "gy", "gz"),
        P(None, None, None, "gx", "gy", "gz"),
        P(None, None, "gx", "gy", "gz"),
    )
    return jax.shard_map(
        body, mesh=mesh, in_specs=placed, out_specs=P("gx", "gy", "gz"), check_vma=False
    )
```
